256 devices in a mesh: seq: 32 (over z, x), head: 8 (over y, core).
Axes of the slice: x: 4, y: 4, z: 8, core: 2. Of those that a mesh axis runs over, the one named last changes fastest.
Arguments:
- mixer_input: bfloat16 [32768, 8192], P('seq', 'head'), may hold values from -6 to 6
- state_input: bfloat16 [32768, 256], P('seq'), may hold values from -6 to 6
- gate_input: bfloat16 [32768, 8192], P('seq', 'head'), may hold values from -6 to 6
- step_raw: float32 [32768, 64], P('seq', 'head'), may hold values from -2 to 1
- decay_rate: float32 [64], P('head'), may hold values from 2e-05 to 0.05
- conv_inner: bfloat16 [4, 8192], P(None, 'head'), may hold values from -3 to 3
- conv_state: bfloat16 [4, 256], replicated, may hold values from -3 to 3
- level_table: float32 [8, 13, 64], P(None, None, 'head'), may hold values from 0.25 to 2
- stretch_kind: int32 [512], P('seq'), may hold values from 0 to 7
- norm_gain: float32 [8192], P('head'), may hold values from 0.1 to 1.9
Outputs:
- mixed_out: bfloat16 [32768, 8192], P('seq', 'head')
The draws below stay inside these ranges and needn't reach their ends.
Inputs may be any that keep to these rules, and one draw needn't show every extreme that they name: `stretch_kind`: each stretch of 64 tokens names one row of level_table.
All inputs are finite; a program needn't handle non-finite values.
Results may differ from the reference program's by a relative error of at most 0.0036.
Values may be sent and summed in bfloat16 or wider, within the bound.
No kernel may reach another device: no remote copies, remote signals or barrier semaphores. Data moves between devices by JAX's collectives and lax.ppermute only.
A program may use at most 128 MiB of HBM per device.

```python
import math
import jax
import jax.numpy as jnp
from jax import lax

HEADS = 64
STATE = 128
CONV = 4
CH = 64
LEVELS = 13
KINDS = 8
L_DEV = 1024
D_INNER = 8192
SEQ = 32768
NCHUNK = 512


def plant(array, rng, least, high):
    spot = [jax.random.randint(jax.random.fold_in(rng, axis), (), 0, length) for axis, length in enumerate(array.shape)]
    longest = array.shape.index(max(array.shape))
    neighbour = spot[:longest] + [(spot[longest] + 1) % array.shape[longest]] + spot[longest + 1:]
    return array.at[tuple(spot)].set(least).at[tuple(neighbour)].set(high)


def levels(rng, shape, cuts, smallest, largest):
    gain, own = 1.0, jax.random.fold_in(rng, 6)
    for dim, shards_of in cuts:
        steps = jnp.exp(jax.random.uniform(jax.random.fold_in(own, dim), (shards_of,), jnp.float32, smallest / len(cuts), largest / len(cuts)))
        gain = gain * jnp.repeat(steps, shape[dim] // shards_of).reshape([-1 if axis == dim else 1 for axis in range(len(shape))])
    return gain


def bell_draw(own_key, dims, scale, most, pieces=(), held_as=jnp.bfloat16):
    entries = jax.random.normal(own_key, dims, jnp.float32) * scale
    if len(pieces) > 0:
        entries = levels(own_key, dims, pieces, -0.22, 0.18) * entries
    return jnp.clip(entries, min=-most, max=most).astype(held_as)


def setup_inputs(seed: int = 0) -> dict:
    streams_of = jax.random.split(jax.random.key(seed), 11)
    mixer_input = bell_draw(streams_of[0], (SEQ, D_INNER), 1.0, 6.0, ((0, 32), (1, 8)))
    state_input = bell_draw(streams_of[1], (SEQ, 2 * STATE), 1.0, 6.0, ((0, 32),))
    gate_input = bell_draw(streams_of[2], (SEQ, D_INNER), 1.0, 6.0, ((0, 32), (1, 8)))
    step_raw = jnp.clip(-2.0 + 3.0 * jax.random.uniform(streams_of[3], (SEQ, HEADS), jnp.float32) ** levels(streams_of[3], (SEQ, HEADS), ((0, 32), (1, 8)), -0.2, 0.2), -2.0, 1.0)
    decay_rate = jnp.clip(jnp.exp(math.log(0.05) - 7.824046 * jax.random.uniform(streams_of[4], (HEADS,), jnp.float32) ** levels(streams_of[4], (HEADS,), ((0, 8),), -0.2, 0.2)), 1.9999999494757503e-05, 0.05)
    conv_inner = bell_draw(streams_of[5], (CONV, D_INNER), CONV ** -0.5, 3.0, ((1, 8),))
    conv_state = bell_draw(streams_of[6], (CONV, 2 * STATE), CONV ** -0.5, 3.0)
    level_table = jnp.clip(jnp.exp(math.log(2.0) - 2.0794415 * jax.random.uniform(streams_of[7], (KINDS, LEVELS, HEADS), jnp.float32) ** levels(streams_of[7], (KINDS, LEVELS, HEADS), ((2, 8),), -0.2, 0.2)), 0.25, 2.0)
    stretch_kind = plant(jax.random.randint(streams_of[8], (NCHUNK,), 0, KINDS), jax.random.fold_in(streams_of[8], 1), 0, KINDS - 1).astype(jnp.int32)
    norm_gain = jnp.clip(1.0 + 0.18 * jax.random.normal(streams_of[9], (D_INNER,), jnp.float32), 0.1, 1.9)
    return {"mixer_input": mixer_input, "state_input": state_input, "gate_input": gate_input, "step_raw": step_raw, "decay_rate": decay_rate, "conv_inner": conv_inner, "conv_state": conv_state, "level_table": level_table, "stretch_kind": stretch_kind, "norm_gain": norm_gain}


HIGHEST = lax.Precision.HIGHEST

def bit_length(values, limit):
    result = jnp.zeros_like(values)
    for power in range(limit):
        result = result + (values >= 2 ** power).astype(jnp.int32)
    return result

def causal_conv(padded, kernel, length):
    width = kernel.shape[0]
    summed = jnp.zeros((length, padded.shape[1]), jnp.float32)
    for offset in range(width):
        summed = summed + padded[offset:offset + length].astype(jnp.float32) * kernel[offset].astype(jnp.float32)
    return jax.nn.silu(summed).astype(jnp.bfloat16)

def token_table(kinds, level_table, stretch_len):
    kind_count, level_count, heads = level_table.shape
    stretches = kinds.shape[0]
    onehot = (kinds[:, None] == jnp.arange(kind_count, dtype=jnp.int32)[None, :]).astype(jnp.float32)
    rows = jnp.dot(onehot, level_table.reshape(kind_count, level_count * heads), precision=HIGHEST)
    rows = rows.reshape(stretches, 1, level_count, heads)
    return jnp.broadcast_to(rows, (stretches, stretch_len, level_count, heads)).reshape(stretches * stretch_len, level_count, heads)

def local_states(inner, keys_b, step_size, running):
    length = inner.shape[0]
    heads = running.shape[1]
    head_dim = inner.shape[1] // heads
    keys_f = keys_b.astype(jnp.float32)
    final = running[length - 1]

    def one_head(head):
        values = lax.dynamic_slice_in_dim(inner, head * head_dim, head_dim, 1)
        run_here = lax.dynamic_index_in_dim(running, head, 1, keepdims=False)
        step_here = lax.dynamic_index_in_dim(step_size, head, 1, keepdims=False)
        scale = jnp.exp(lax.dynamic_index_in_dim(final, head, 0, keepdims=False) - run_here) * step_here
        scaled_keys = (keys_f * scale[:, None]).astype(jnp.bfloat16)
        return jnp.dot(scaled_keys.T, values, preferred_element_type=jnp.float32)
    return lax.map(one_head, jnp.arange(heads, dtype=jnp.int32))

def fold_levels(sources, target, decays, states, seq_bits):
    device_ids = jnp.arange(decays.shape[0], dtype=jnp.int32)
    between = ((device_ids[None, :] > sources[:, None]) & (device_ids[None, :] < target)).astype(jnp.float32)
    span = jnp.dot(between, decays, precision=HIGHEST)
    level = bit_length(jnp.bitwise_xor(sources, target), seq_bits) - 1
    chosen = ((level[:, None] == jnp.arange(seq_bits, dtype=jnp.int32)[None, :]) & (sources < target)[:, None]).astype(jnp.float32)
    factor = chosen[:, :, None] * jnp.exp(span)[:, None, :]
    return jnp.einsum('jbh,jhnp->bhnp', factor, states, precision=HIGHEST)

def block_output(inner, keys_b, queries_c, step_size, running, token_weights, level_states, local_bits, seq_bits):
    length = inner.shape[0]
    heads = running.shape[1]
    head_dim = inner.shape[1] // heads
    state_dim = keys_b.shape[1]
    stretch_len = length // 2 ** local_bits
    position = jnp.arange(length, dtype=jnp.int32)
    stretch_local = position // stretch_len
    pair_level = bit_length(jnp.bitwise_xor(stretch_local[:, None], stretch_local[None, :]), local_bits + 1)
    causal = position[:, None] >= position[None, :]
    scores = jnp.dot(queries_c, keys_b.T, preferred_element_type=jnp.float32)
    far_weights = token_weights[:, local_bits + 1:local_bits + 1 + seq_bits, :] * jnp.exp(running)[:, None, :]
    queries_f = queries_c.astype(jnp.float32)
    far_rounded = level_states.astype(jnp.bfloat16)

    def one_head(head):
        values = lax.dynamic_slice_in_dim(inner, head * head_dim, head_dim, 1)
        weights_here = lax.dynamic_index_in_dim(token_weights, head, 2, keepdims=False)
        pair_weight = jnp.zeros((length, length), jnp.float32)
        for level in range(local_bits + 1):
            pair_weight = jnp.where(pair_level == level, weights_here[:, level][:, None], pair_weight)
        run_here = lax.dynamic_index_in_dim(running, head, 1, keepdims=False)
        step_here = lax.dynamic_index_in_dim(step_size, head, 1, keepdims=False)
        decay = jnp.exp(jnp.where(causal, run_here[:, None] - run_here[None, :], -jnp.inf))
        mixing = (scores * decay * step_here[None, :] * pair_weight).astype(jnp.bfloat16)
        local_out = jnp.dot(mixing, values, preferred_element_type=jnp.float32)
        far_here = lax.dynamic_index_in_dim(far_weights, head, 2, keepdims=False)
        lifted = (far_here[:, :, None] * queries_f[:, None, :]).reshape(length, seq_bits * state_dim).astype(jnp.bfloat16)
        states_here = lax.dynamic_index_in_dim(far_rounded, head, 1, keepdims=False).reshape(seq_bits * state_dim, head_dim)
        return local_out + jnp.dot(lifted, states_here, preferred_element_type=jnp.float32)
    outputs = lax.map(one_head, jnp.arange(heads, dtype=jnp.int32))
    return jnp.transpose(outputs, (1, 0, 2)).reshape(length, heads * head_dim)

def reference(mixer_input, state_input, gate_input, step_raw, decay_rate, conv_inner, conv_state, level_table, stretch_kind, norm_gain):
    width = conv_inner.shape[0]
    blocks = SEQ // L_DEV
    seq_bits = blocks.bit_length() - 1
    stretches_here = L_DEV // CH
    local_bits = stretches_here.bit_length() - 1
    pad_inner = jnp.concatenate([jnp.zeros((width - 1, D_INNER), jnp.bfloat16), mixer_input], axis=0)
    pad_state = jnp.concatenate([jnp.zeros((width - 1, 2 * STATE), jnp.bfloat16), state_input], axis=0)
    step_size = jax.nn.softplus(step_raw)
    log_decay = -decay_rate[None, :] * step_size
    running_all = jnp.cumsum(log_decay.reshape(blocks, L_DEV, HEADS), axis=1)
    block_decay = running_all[:, L_DEV - 1, :]
    step_blocks = step_size.reshape(blocks, L_DEV, HEADS)

    def prepare(block):
        start = block * L_DEV
        inner = causal_conv(lax.dynamic_slice_in_dim(pad_inner, start, L_DEV + width - 1, 0), conv_inner, L_DEV)
        state_rows = causal_conv(lax.dynamic_slice_in_dim(pad_state, start, L_DEV + width - 1, 0), conv_state, L_DEV)
        step_here = lax.dynamic_index_in_dim(step_blocks, block, 0, keepdims=False)
        running = lax.dynamic_index_in_dim(running_all, block, 0, keepdims=False)
        return (inner, state_rows, step_here, running)

    def block_state(block):
        inner, state_rows, step_here, running = prepare(block)
        return local_states(inner, state_rows[:, :STATE], step_here, running)
    block_ids = jnp.arange(blocks, dtype=jnp.int32)
    all_states = lax.map(block_state, block_ids)

    def block_result(block):
        inner, state_rows, step_here, running = prepare(block)
        kinds = lax.dynamic_slice_in_dim(stretch_kind, block * stretches_here, stretches_here, 0)
        weights = token_table(kinds, level_table, CH)
        level_states = fold_levels(block_ids, block, block_decay, all_states, seq_bits)
        mixed = block_output(inner, state_rows[:, :STATE], state_rows[:, STATE:], step_here, running, weights, level_states, local_bits, seq_bits)
        gate_here = lax.dynamic_slice_in_dim(gate_input, block * L_DEV, L_DEV, 0).astype(jnp.float32)
        gated = mixed * jax.nn.silu(gate_here)
        squares = lax.optimization_barrier(jnp.sum(gated * gated, axis=1))
        scale = lax.rsqrt(squares / D_INNER + 1e-05)
        return (gated * scale[:, None] * norm_gain[None, :]).astype(jnp.bfloat16)
    return lax.map(block_result, block_ids).reshape(SEQ, D_INNER)
```

```python
import functools
import jax
import jax.numpy as jnp
from jax import lax
from jax.experimental import pallas as pl
from jax.experimental.pallas import tpu as pltpu
from jax.sharding import PartitionSpec as P

F32 = jnp.float32
BF16 = jnp.bfloat16
HIGHEST = lax.Precision.HIGHEST

XS = 4
ZS = 8
YS = 4
CORES = 2
PAIR = 2
DIM = 128
HALO = 16
TILE = 128
MESSAGE = PAIR * DIM + 8


def seq_perm(move):
    pairs = []
    for z in range(ZS):
        for x in range(XS):
            target = move(z, x)
            if target is not None:
                pairs.append((z * XS + x, target[0] * XS + target[1]))
    return pairs


def head_perm(move):
    pairs = []
    for y in range(YS):
        for core in range(CORES):
            target = move(y, core)
            pairs.append((y * CORES + core, target[0] * CORES + target[1]))
    return pairs


def along_x(value, step):
    return lax.ppermute(value, "seq", seq_perm(lambda z, x: (z, (x + step) % XS)))


def silu(value):
    return value / (1.0 + jnp.exp(-value))


def whole(*dims):
    return pl.BlockSpec(dims, lambda *_: (0,) * len(dims))


def conv(block, halo, taps):
    length = block.shape[0]
    width = taps.shape[0]
    joined = jnp.concatenate([halo[HALO - 8 :].astype(F32), block.astype(F32)], axis=0)
    taps = taps.astype(F32)
    total = jnp.zeros((length, block.shape[1]), F32)
    for offset in range(width):
        shift = width - 1 - offset
        moved = joined if shift == 0 else pltpu.roll(joined, shift, axis=0)
        total = total + moved[8:] * taps[offset : offset + 1]
    return silu(total).astype(BF16)


def prepare_kernel(
    place,
    mixer,
    mixer_halo,
    state,
    state_halo,
    taps,
    state_taps,
    step_raw,
    rate,
    inner,
    rows,
    running_out,
    step_out,
    part0,
    part1,
    part2,
    part3,
    keys_t,
    scale,
    last,
):
    turn = pl.program_id(0)
    parts = (part0, part1, part2, part3)
    heads, length = step_raw.shape

    @pl.when(turn == 0)
    def _():
        raw = step_raw[...]
        step = jnp.maximum(raw, 0.0) + jnp.log1p(jnp.exp(-jnp.abs(raw)))
        running = -rate[...] * step
        lane = lax.broadcasted_iota(jnp.int32, (heads, length), 1)
        shift = 1
        while shift < length:
            moved = pltpu.roll(running, shift, axis=1)
            running = running + jnp.where(lane >= shift, moved, 0.0)
            shift *= 2
        final = running[:, length - 1 :]
        running_out[...] = running
        step_out[...] = step
        scale[...] = jnp.exp(final - running) * step
        last[...] = jnp.broadcast_to(final, last.shape)
        state_rows = conv(state[...], state_halo[...], state_taps[...])
        rows[...] = state_rows
        keys_t[...] = state_rows[:, :DIM].astype(F32).T

    values = conv(mixer[...], mixer_halo[...], taps[...])
    inner[...] = values
    pair = lax.rem(place[0] + turn, XS)
    states = []
    for head in range(PAIR):
        row = scale[pl.ds(pair * PAIR + head, 1), :]
        scaled_t = (keys_t[...] * row).astype(BF16)
        states.append(
            jnp.dot(
                scaled_t, values[:, head * DIM : (head + 1) * DIM], preferred_element_type=F32
            )
        )
    first = last[pl.ds(pair * PAIR, 1), :]
    second = last[pl.ds(pair * PAIR + 1, 1), :]
    spot = lax.broadcasted_iota(jnp.int32, (8, DIM), 0)
    decay_rows = jnp.where(spot == 0, first, jnp.where(spot == 1, second, 0.0))
    for index, part in enumerate(parts):

        @pl.when(turn == index)
        def _(part=part):
            part[:DIM] = states[0]
            part[DIM : 2 * DIM] = states[1]
            part[2 * DIM :] = decay_rows


def prepare(place, mixer, halo, state, taps, state_taps, step_raw_t, rate):
    length, width = mixer.shape
    heads = step_raw_t.shape[0]
    wide = PAIR * DIM

    def column(turn, place):
        return (0, lax.rem(place[0] + turn, XS))

    part = jax.ShapeDtypeStruct((MESSAGE, DIM), F32)
    return pl.pallas_call(
        prepare_kernel,
        grid_spec=pltpu.PrefetchScalarGridSpec(
            num_scalar_prefetch=1,
            grid=(XS,),
            in_specs=[
                pl.BlockSpec((length, wide), column),
                pl.BlockSpec((HALO, wide), column),
                whole(length, 2 * DIM),
                pl.BlockSpec((HALO, 2 * DIM), lambda *_: (0, width // (2 * DIM))),
                pl.BlockSpec((taps.shape[0], wide), column),
                whole(*state_taps.shape),
                whole(heads, length),
                whole(heads, 1),
            ],
            out_specs=[
                pl.BlockSpec((length, wide), column),
                whole(length, 2 * DIM),
                whole(heads, length),
                whole(heads, length),
            ]
            + [whole(MESSAGE, DIM)] * XS,
            scratch_shapes=[
                pltpu.VMEM((DIM, length), F32),
                pltpu.VMEM((heads, length), F32),
                pltpu.VMEM((heads, DIM), F32),
            ],
        ),
        out_shape=[
            jax.ShapeDtypeStruct((length, width), BF16),
            jax.ShapeDtypeStruct((length, 2 * DIM), BF16),
            jax.ShapeDtypeStruct((heads, length), F32),
            jax.ShapeDtypeStruct((heads, length), F32),
        ]
        + [part] * XS,
        compiler_params=pltpu.CompilerParams(vmem_limit_bytes=24 * 2**20),
        cost_estimate=pl.CostEstimate(
            flops=2 * length * width * DIM, bytes_accessed=8 * 2**20, transcendentals=2 * length * width
        ),
        name="prepare",
    )(place, mixer, halo, state, halo, taps, state_taps, step_raw_t, rate)


def local_kernel(inner, rows, running_in, step_in, table, kinds, out, far_rows, scores, weights):
    head = pl.program_id(0)
    length = inner.shape[0]
    tiles = length // TILE
    local_bits = 4

    @pl.when(head == 0)
    def _():
        for i in range(tiles):
            wide = (i + 1) * TILE
            scores[i * TILE : wide, :wide] = lax.dot_general(
                rows[i * TILE : wide, DIM:],
                rows[:wide, :DIM],
                (((1,), (1,)), ((), ())),
                preferred_element_type=F32,
            )
        spot = lax.broadcasted_iota(jnp.int32, (8, length), 0)
        onehot = (spot == kinds[...]).astype(F32)
        weights[...] = jnp.dot(table[...], onehot, precision=HIGHEST, preferred_element_type=F32)

    running = running_in[pl.ds(head, 1), :]
    step = step_in[pl.ds(head, 1), :]
    starts = [running[:, i * TILE : i * TILE + 1] for i in range(tiles)]
    ahead = jnp.concatenate(
        [jnp.exp(running[:, i * TILE : (i + 1) * TILE] - starts[i]) for i in range(tiles)], axis=1
    )
    near = weights[pl.ds(pl.multiple_of(head * 16, 16), 8), :] * ahead
    far = weights[pl.ds(pl.multiple_of(head * 16 + 8, 8), 8), :] * jnp.exp(running)
    far_rows[0] = far
    near_columns = near.T
    row = lax.broadcasted_iota(jnp.int32, (TILE, TILE), 0)
    lane = lax.broadcasted_iota(jnp.int32, (TILE, TILE), 1)
    causal = row >= lane
    crossed = (row >= TILE // 2) & (lane < TILE // 2)
    for i in range(tiles):
        wide = (i + 1) * TILE
        behind = jnp.exp(starts[i] - running[:, :wide]) * step[:, :wide]
        here = near_columns[i * TILE : wide]
        level_columns = [
            jnp.broadcast_to(here[:, level : level + 1], (TILE, TILE))
            for level in range(local_bits + 1)
        ]
        pieces = []
        for j in range(i + 1):
            piece = scores[i * TILE : wide, j * TILE : (j + 1) * TILE]
            piece = piece * behind[:, j * TILE : (j + 1) * TILE]
            if j < i:
                piece = piece * level_columns[(i ^ j).bit_length() + 1]
            else:
                piece = piece * jnp.where(crossed, level_columns[1], level_columns[0])
                piece = jnp.where(causal, piece, 0.0)
            pieces.append(piece.astype(BF16))
        mixing = jnp.concatenate(pieces, axis=1)
        out[i * TILE : wide] = jnp.dot(mixing, inner[:wide], preferred_element_type=F32)


def local_part(inner, rows, running, step, table, kinds):
    length, width = inner.shape
    heads = width // DIM
    return pl.pallas_call(
        local_kernel,
        grid=(heads,),
        in_specs=[
            pl.BlockSpec((length, DIM), lambda head: (0, head)),
            whole(length, 2 * DIM),
            whole(heads, length),
            whole(heads, length),
            whole(*table.shape),
            whole(1, length),
        ],
        out_specs=[
            pl.BlockSpec((length, DIM), lambda head: (0, head)),
            pl.BlockSpec((1, 8, length), lambda head: (head, 0, 0)),
        ],
        out_shape=[
            jax.ShapeDtypeStruct((length, width), F32),
            jax.ShapeDtypeStruct((heads, 8, length), F32),
        ],
        scratch_shapes=[pltpu.VMEM((length, length), F32), pltpu.VMEM((heads * 16, length), F32)],
        compiler_params=pltpu.CompilerParams(vmem_limit_bytes=24 * 2**20),
        cost_estimate=pl.CostEstimate(
            flops=8 * length * length * DIM, bytes_accessed=8 * 2**20, transcendentals=2**18
        ),
        name="local_part",
    )(inner, rows, running, step, table, kinds)


def flag(condition):
    return jnp.where(condition, 1.0, 0.0).astype(F32)


def fold_row_kernel(place, p0, p1, p2, p3, row_out, m0, m1, m2, m3):
    x = place[0]
    parts = (p0, p1, p2, p3)
    owner = [lax.rem(x + XS - k, XS) for k in range(XS)]
    decays = [part[2 * DIM :] for part in parts]

    def from_block(block):
        return [flag(owner[k] == block) for k in range(XS)]

    def pick(values, chosen):
        return sum(value * mark for value, mark in zip(values, chosen))

    block_marks = [from_block(block) for block in range(XS)]
    later = [
        jnp.exp(sum(decays[m] * flag(owner[m] > owner[k]) for m in range(XS))) for k in range(XS)
    ]
    decay_one = jnp.exp(pick(decays, block_marks[1]))
    decay_two = jnp.exp(pick(decays, block_marks[2]))
    for head in range(PAIR):
        span = slice(head * DIM, (head + 1) * DIM)
        blocks = [part[span] for part in parts]
        row_out[span] = sum(blocks[k] * later[k][head : head + 1] for k in range(XS))
        first = pick(blocks, block_marks[0])
        third = pick(blocks, block_marks[2])
        joined = first * decay_one[head : head + 1] + pick(blocks, block_marks[1])
        for k, message in enumerate((m0, m1, m2, m3)):
            target = lax.rem(x + k, XS)
            message[span] = (
                first * flag(target == 1) + third * flag(target == 3)
            ).astype(BF16)
            message[PAIR * DIM + head * DIM : PAIR * DIM + (head + 1) * DIM] = (
                joined
                * (flag(target == 2) + flag(target == 3) * decay_two[head : head + 1])
            ).astype(BF16)
    row_out[2 * DIM :] = sum(decays)


SMEM = pl.BlockSpec(memory_space=pltpu.SMEM)


def fold_row(place, parts):
    return pl.pallas_call(
        fold_row_kernel,
        in_specs=[SMEM] + [whole(MESSAGE, DIM)] * XS,
        out_specs=[whole(MESSAGE, DIM)] + [whole(4 * DIM, DIM)] * XS,
        out_shape=[jax.ShapeDtypeStruct((MESSAGE, DIM), F32)]
        + [jax.ShapeDtypeStruct((4 * DIM, DIM), BF16)] * XS,
        grid=(1,),
        cost_estimate=pl.CostEstimate(flops=2**20, bytes_accessed=2**20, transcendentals=2**10),
        name="fold_row",
    )(place, *parts)


def fold_pair_kernel(place, own, other, pair_out):
    upper = flag(lax.rem(place[1], 2) == 1)
    own_decay = own[2 * DIM :]
    other_decay = other[2 * DIM :]
    own_scale = jnp.exp(other_decay * (1.0 - upper))
    other_scale = jnp.exp(own_decay * upper)
    for head in range(PAIR):
        span = slice(head * DIM, (head + 1) * DIM)
        pair_out[span] = (
            own[span] * own_scale[head : head + 1] + other[span] * other_scale[head : head + 1]
        )
    pair_out[2 * DIM :] = own_decay + other_decay


def fold_pair(place, own, other):
    return pl.pallas_call(
        fold_pair_kernel,
        in_specs=[SMEM] + [whole(MESSAGE, DIM)] * 2,
        out_specs=whole(MESSAGE, DIM),
        out_shape=jax.ShapeDtypeStruct((MESSAGE, DIM), F32),
        grid=(1,),
        cost_estimate=pl.CostEstimate(flops=2**18, bytes_accessed=2**19, transcendentals=2**10),
        name="fold_pair",
    )(place, own, other)


def fold_far_kernel(place, d0, d1, d2, d3, other, g1, g2, g3, m0, m1, m2, m3):
    x = place[0]
    z = place[1]
    upper = flag(lax.rem(z, 2) == 1)
    pair = lax.div(z, 2)
    odd_pair = flag(lax.rem(pair, 2) == 1)
    third_pair = flag(pair == 2)
    last_pair = flag(pair == 3)
    decays = [d0[...], d1[...], d2[...], d3[...]]
    owner = [lax.rem(x + XS - k, XS) for k in range(XS)]
    in_pair = other[2 * DIM :] * upper
    after = in_pair + g1[2 * DIM :] * last_pair
    inside_first = jnp.exp(g1[2 * DIM :])
    inside_last = jnp.exp(g2[2 * DIM :])
    for head in range(PAIR):
        span = slice(head * DIM, (head + 1) * DIM)
        row = slice(head, head + 1)
        two = other[span]
        three = g1[span]
        four = (g2[span] * inside_first[row] + three) * third_pair + (
            g3[span] * inside_last[row] + g2[span]
        ) * last_pair
        for k, message in enumerate((m0, m1, m2, m3)):
            target = lax.rem(x + k, XS)
            before = sum(decays[m][row] * flag(owner[m] < target) for m in range(XS))
            factors = (
                jnp.exp(before) * upper,
                jnp.exp(before + in_pair[row]) * odd_pair,
                jnp.exp(before + after[row]),
            )
            for level, (state, factor) in enumerate(zip((two, three, four), factors)):
                base = level * PAIR * DIM + head * DIM
                message[base : base + DIM] = (state * factor).astype(BF16)


def fold_far(place, parts, other, gathered):
    decay_rows = pl.BlockSpec((8, DIM), lambda *_: (2 * DIM // 8, 0))
    return pl.pallas_call(
        fold_far_kernel,
        in_specs=[SMEM] + [decay_rows] * XS + [whole(MESSAGE, DIM)] * 4,
        out_specs=[whole(6 * DIM, DIM)] * XS,
        out_shape=[jax.ShapeDtypeStruct((6 * DIM, DIM), BF16)] * XS,
        grid=(1,),
        cost_estimate=pl.CostEstimate(flops=2**20, bytes_accessed=2**20, transcendentals=2**12),
        name="fold_far",
    )(place, *parts, other, *gathered)


def far_kernel(
    place, local, gate, rows, far_rows, n0, n1, n2, n3, f0, f1, f2, f3, gated, squares, held, total
):
    turn = pl.program_id(0)
    length = local.shape[0]
    for k, (near, far) in enumerate(((n0, f0), (n1, f1), (n2, f2), (n3, f3))):

        @pl.when(turn == k)
        def _(near=near, far=far):
            for head in range(PAIR):
                for level in range(2):
                    base = (level * PAIR + head) * DIM
                    held[head, level * DIM : (level + 1) * DIM] = near[base : base + DIM]
                for level in range(3):
                    base = (level * PAIR + head) * DIM
                    held[head, (level + 2) * DIM : (level + 3) * DIM] = far[base : base + DIM]

    @pl.when(turn == 0)
    def _():
        total[...] = jnp.zeros_like(total)

    step = 256
    columns = [far_rows[head].T for head in range(PAIR)]
    for start in range(0, length, step):
        span = slice(start, start + step)
        queries = rows[span, DIM:].astype(F32)
        gates = silu(gate[span].astype(F32))
        for head in range(PAIR):
            lane = slice(head * DIM, (head + 1) * DIM)
            lifted = jnp.concatenate(
                [
                    (queries * columns[head][span, level : level + 1]).astype(BF16)
                    for level in range(5)
                ],
                axis=1,
            )
            mixed = local[span, lane] + jnp.dot(lifted, held[head], preferred_element_type=F32)
            value = mixed * gates[:, lane]
            gated[span, lane] = value
            total[span] += value * value

    @pl.when(turn == XS - 1)
    def _():
        for tile in range(length // TILE):
            part = total[tile * TILE : (tile + 1) * TILE].T
            squares[tile : tile + 1] = jnp.sum(part, axis=0, keepdims=True)


def far_part(place, local, gate, rows, far_rows, near_states, far_states):
    length, width = local.shape
    wide = PAIR * DIM

    def pair(turn, place):
        return lax.rem(place[0] + XS - turn, XS)

    def column(turn, place):
        return (0, pair(turn, place))

    return pl.pallas_call(
        far_kernel,
        grid_spec=pltpu.PrefetchScalarGridSpec(
            num_scalar_prefetch=1,
            grid=(XS,),
            in_specs=[
                pl.BlockSpec((length, wide), column),
                pl.BlockSpec((length, wide), column),
                whole(length, 2 * DIM),
                pl.BlockSpec((PAIR, 8, length), lambda turn, place: (pair(turn, place), 0, 0)),
            ]
            + [whole(4 * DIM, DIM)] * XS
            + [whole(6 * DIM, DIM)] * XS,
            out_specs=[
                pl.BlockSpec((length, wide), column),
                whole(length // TILE, TILE),
            ],
            scratch_shapes=[pltpu.VMEM((PAIR, 5 * DIM, DIM), BF16), pltpu.VMEM((length, DIM), F32)],
        ),
        out_shape=[
            jax.ShapeDtypeStruct((length, width), F32),
            jax.ShapeDtypeStruct((length // TILE, TILE), F32),
        ],
        compiler_params=pltpu.CompilerParams(vmem_limit_bytes=24 * 2**20),
        cost_estimate=pl.CostEstimate(
            flops=10 * length * width * DIM, bytes_accessed=12 * 2**20, transcendentals=2**20
        ),
        name="far_part",
    )(place, local, gate, rows, far_rows, *near_states, *far_states)


def norm_kernel(total_width, gated, s0, s1, s2, s3, gain, out):
    scale = lax.rsqrt((s0[...] + s1[...] + s2[...] + s3[...]) / total_width + 1e-05)
    tiles = scale.shape[0]
    which = lax.broadcasted_iota(jnp.int32, scale.shape, 0)
    here = pl.program_id(0)
    row = jnp.sum(jnp.where(which == here, scale, 0.0), axis=0, keepdims=True)
    column = jnp.broadcast_to(row, (TILE, TILE)).T
    for piece in range(gated.shape[1] // TILE):
        lane = slice(piece * TILE, (piece + 1) * TILE)
        out[:, lane] = (gated[:, lane] * column * gain[:, lane]).astype(BF16)


def norm(gated, squares, gain, total_width):
    length, width = gated.shape
    tiles = length // TILE
    return pl.pallas_call(
        functools.partial(norm_kernel, total_width),
        grid=(tiles,),
        in_specs=[pl.BlockSpec((TILE, width), lambda i: (i, 0))]
        + [whole(tiles, TILE)] * YS
        + [whole(1, width)],
        out_specs=pl.BlockSpec((TILE, width), lambda i: (i, 0)),
        out_shape=jax.ShapeDtypeStruct((length, width), BF16),
        cost_estimate=pl.CostEstimate(
            flops=2 * length * width, bytes_accessed=6 * 2**20, transcendentals=2**10
        ),
        name="norm",
    )(gated, *squares, gain)


def local(
    mixer_input,
    state_input,
    gate_input,
    step_raw,
    decay_rate,
    conv_inner,
    conv_state,
    level_table,
    stretch_kind,
    norm_gain,
):
    length, width = mixer_input.shape
    heads = step_raw.shape[1]
    index = lax.axis_index("seq")
    place = jnp.stack([lax.rem(index, XS), lax.div(index, XS)]).astype(jnp.int32)
    tails = jnp.concatenate([mixer_input[length - HALO :], state_input[length - HALO :]], axis=1)
    halo = lax.ppermute(tails, "seq", [(i, i + 1) for i in range(XS * ZS - 1)])
    inner, rows, running, step, *parts = prepare(
        place,
        mixer_input,
        halo,
        state_input,
        conv_inner,
        conv_state,
        step_raw.T,
        decay_rate[:, None],
    )
    kinds = jnp.repeat(stretch_kind, length // stretch_kind.shape[0])[None, :]
    by_head = jnp.transpose(level_table, (2, 1, 0))
    gap = jnp.zeros((heads, 3, by_head.shape[2]), F32)
    table = jnp.concatenate([by_head[:, :5], gap, by_head[:, 5:10], gap], axis=1)
    table = table.reshape(heads * 16, by_head.shape[2])
    arrived = [parts[0]] + [along_x(parts[k], k) for k in range(1, XS)]
    local_out, far_rows = local_part(inner, rows, running, step, table, kinds)
    row_state, *near = fold_row(place, arrived)
    near = [near[0]] + [along_x(near[k], k) for k in range(1, XS)]
    other = lax.ppermute(row_state, "seq", seq_perm(lambda z, x: (z ^ 1, x)))
    pair_state = fold_pair(place, row_state, other)
    gathered = [
        lax.ppermute(
            pair_state,
            "seq",
            seq_perm(lambda z, x, far=far: (z + far, x) if z + far < ZS else None),
        )
        for far in (2, 4, 6)
    ]
    far = fold_far(place, arrived, other, gathered)
    far = [far[0]] + [along_x(far[k], k) for k in range(1, XS)]
    gated, squares = far_part(place, local_out, gate_input, rows, far_rows, near, far)
    squares = squares + lax.ppermute(squares, "head", head_perm(lambda y, core: (y, 1 - core)))
    sums = [squares] + [
        lax.ppermute(squares, "head", head_perm(lambda y, core, k=k: ((y + k) % YS, core)))
        for k in range(1, YS)
    ]
    total_width = width * lax.axis_size("head")
    return norm(gated, sums, norm_gain[None, :], total_width)


def solution(mesh):
    return jax.shard_map(
        local,
        mesh=mesh,
        in_specs=(
            P("seq", "head"),
            P("seq", None),
            P("seq", "head"),
            P("seq", "head"),
            P("head"),
            P(None, "head"),
            P(),
            P(None, None, "head"),
            P("seq"),
            P("head"),
        ),
        out_specs=P("seq", "head"),
        check_vma=False,
    )
```

```python
import functools
import jax
import jax.numpy as jnp
from jax import lax
from jax.experimental import pallas as pl
from jax.experimental.pallas import tpu as pltpu
from jax.sharding import PartitionSpec as P

F32 = jnp.float32
BF16 = jnp.bfloat16

XS = 4
ZS = 8
YS = 4
CORES = 2
PAIR = 2
DIM = 128
HALO = 16
TILE = 128
WIDE = 256
TOP = 16384.0
MESSAGE = PAIR * DIM + 8


def seq_perm(move):
    pairs = []
    for z in range(ZS):
        for x in range(XS):
            target = move(z, x)
            if target is not None:
                pairs.append((z * XS + x, target[0] * XS + target[1]))
    return pairs


def head_perm(move):
    pairs = []
    for y in range(YS):
        for core in range(CORES):
            target = move(y, core)
            pairs.append((y * CORES + core, target[0] * CORES + target[1]))
    return pairs


def along_x(value, step):
    return lax.ppermute(value, "seq", seq_perm(lambda z, x: (z, (x + step) % XS)))


def silu(value):
    return value / (1.0 + jnp.exp(-value))


VMEM = pl.BlockSpec(memory_space=pltpu.VMEM)
SMEM = pl.BlockSpec(memory_space=pltpu.SMEM)
HBM = pl.BlockSpec(memory_space=pltpu.HBM)
DMA = pltpu.SemaphoreType.DMA


def params(mebibytes):
    return pltpu.CompilerParams(vmem_limit_bytes=mebibytes * 2**20)


def in_hbm(value):
    return pltpu.with_memory_space_constraint(value, pltpu.HBM)


def block_place():
    index = lax.axis_index("seq")
    return lax.rem(index, XS), lax.div(index, XS)


def conv(block, halo, taps):
    length = block.shape[0]
    width = taps.shape[0]
    joined = jnp.concatenate([halo[HALO - 8 :].astype(F32), block.astype(F32)], axis=0)
    taps = taps.astype(F32)
    total = jnp.zeros((length, block.shape[1]), F32)
    for offset in range(width):
        shift = width - 1 - offset
        moved = joined if shift == 0 else pltpu.roll(joined, shift, axis=0)
        total = total + moved[8:] * taps[offset : offset + 1]
    return silu(total).astype(BF16)


def prepare_kernel(
    mixer,
    halo,
    state,
    taps,
    state_taps,
    step_raw,
    rate,
    inner,
    rows,
    running_out,
    step_out,
    part0,
    part1,
    part2,
    part3,
    mixer_here,
    state_here,
    taps_here,
    state_taps_here,
    raw_here,
    rate_here,
    keys_t,
    scale,
    last,
    mixer_sem,
    small_sem,
):
    x, _ = block_place()
    heads, length = step_raw.shape
    width = mixer.shape[1]
    wide = PAIR * DIM
    small = [
        pltpu.make_async_copy(source, target, small_sem.at[n])
        for n, (source, target) in enumerate(
            (
                (step_raw, raw_here),
                (rate, rate_here),
                (state, state_here),
                (state_taps, state_taps_here),
                (taps, taps_here),
            )
        )
    ]
    for copy in small:
        copy.start()
    pairs = [lax.rem(x + turn, XS) for turn in range(XS)]
    columns = [pl.ds(pl.multiple_of(pair * wide, wide), wide) for pair in pairs]
    large = [
        pltpu.make_async_copy(
            mixer.at[:, columns[turn]], mixer_here.at[turn], mixer_sem.at[turn]
        )
        for turn in range(XS)
    ]
    for copy in large:
        copy.start()

    small[0].wait()
    small[1].wait()
    raw = raw_here[...]
    step = jnp.maximum(raw, 0.0) + jnp.log1p(jnp.exp(-jnp.abs(raw)))
    spot = lax.broadcasted_iota(jnp.int32, (heads, length), 0)
    rates = jnp.zeros((heads, length), F32)
    for head in range(heads):
        rates = jnp.where(spot == head, rate_here[head], rates)
    running = -rates * step
    lane = lax.broadcasted_iota(jnp.int32, (heads, length), 1)
    shift = 1
    while shift < length:
        moved = pltpu.roll(running, shift, axis=1)
        running = running + jnp.where(lane >= shift, moved, 0.0)
        shift *= 2
    final = running[:, length - 1 :]
    running_out[...] = running
    step_out[...] = step
    scale[...] = jnp.exp(final - running) * step
    last[...] = jnp.broadcast_to(final, last.shape)
    for copy in small[2:]:
        copy.wait()
    state_rows = conv(state_here[...], halo[:, width:], state_taps_here[...])
    rows[...] = state_rows
    keys_t[...] = state_rows[:, :DIM].astype(F32).T

    spot = lax.broadcasted_iota(jnp.int32, (8, DIM), 0)
    for turn, part in enumerate((part0, part1, part2, part3)):
        large[turn].wait()
        values = conv(
            mixer_here[turn], halo[:, columns[turn]], taps_here[:, columns[turn]]
        )
        inner[:, columns[turn]] = values
        pair = pairs[turn]
        for head in range(PAIR):
            row = scale[pl.ds(pair * PAIR + head, 1), :]
            scaled_t = (keys_t[...] * row).astype(BF16)
            part[head * DIM : (head + 1) * DIM] = jnp.dot(
                scaled_t, values[:, head * DIM : (head + 1) * DIM], preferred_element_type=F32
            )
        first = last[pl.ds(pair * PAIR, 1), :]
        second = last[pl.ds(pair * PAIR + 1, 1), :]
        part[2 * DIM :] = jnp.where(spot == 0, first, jnp.where(spot == 1, second, 0.0))


def prepare(mixer, halo, state, taps, state_taps, step_raw_t, rate):
    length, width = mixer.shape
    heads = step_raw_t.shape[0]
    return pl.pallas_call(
        prepare_kernel,
        in_specs=[HBM, VMEM, HBM, HBM, HBM, HBM, HBM],
        out_specs=[VMEM] * (4 + XS),
        out_shape=[
            pltpu.VMEM((length, width), BF16),
            pltpu.VMEM((length, 2 * DIM), BF16),
            pltpu.VMEM((heads, length), F32),
            pltpu.VMEM((heads, length), F32),
        ]
        + [pltpu.VMEM((MESSAGE, DIM), F32)] * XS,
        scratch_shapes=[
            pltpu.VMEM((XS, length, PAIR * DIM), BF16),
            pltpu.VMEM((length, 2 * DIM), BF16),
            pltpu.VMEM(taps.shape, BF16),
            pltpu.VMEM(state_taps.shape, BF16),
            pltpu.VMEM((heads, length), F32),
            pltpu.SMEM((heads,), F32),
            pltpu.VMEM((DIM, length), F32),
            pltpu.VMEM((heads, length), F32),
            pltpu.VMEM((heads, DIM), F32),
            DMA((XS,)),
            DMA((5,)),
        ],
        compiler_params=params(16),
        cost_estimate=pl.CostEstimate(
            flops=2 * length * width * DIM, bytes_accessed=8 * 2**20, transcendentals=2 * length * width
        ),
        name="prepare",
    )(
        in_hbm(mixer),
        halo,
        in_hbm(state),
        in_hbm(taps),
        in_hbm(state_taps),
        in_hbm(step_raw_t),
        in_hbm(rate),
    )


def shared_kernel(rows, running_in, gate, scores, gates, lifted_base, gate_here, gate_sem):
    length, width = gate.shape
    heads = width // DIM
    tiles = length // TILE
    gate_copy = pltpu.make_async_copy(gate, gate_here, gate_sem)
    gate_copy.start()
    for i in range(tiles):
        wide = (i + 1) * TILE
        scores[i * TILE : wide, :wide] = lax.dot_general(
            rows[i * TILE : wide, DIM:],
            rows[:wide, :DIM],
            (((1,), (1,)), ((), ())),
            preferred_element_type=F32,
        )
    columns = jnp.exp(running_in[...]).T
    for i in range(tiles):
        span = slice(i * TILE, (i + 1) * TILE)
        queries = rows[span, DIM:].astype(F32)
        for head in range(heads):
            lifted_base[span, head * DIM : (head + 1) * DIM] = queries * jnp.broadcast_to(
                columns[span, head : head + 1], (TILE, DIM)
            )
    gate_copy.wait()

    def one_tile(tile, carry):
        span = pl.ds(pl.multiple_of(tile * TILE, TILE), TILE)
        gates[span, :] = silu(gate_here[span, :].astype(F32))
        return carry

    lax.fori_loop(0, tiles, one_tile, 0)


def shared_part(rows, running, gate):
    length, width = gate.shape
    return pl.pallas_call(
        shared_kernel,
        in_specs=[VMEM, VMEM, HBM],
        out_specs=[VMEM] * 3,
        out_shape=[
            pltpu.VMEM((length, length), F32),
            pltpu.VMEM((length, width), F32),
            pltpu.VMEM((length, width), F32),
        ],
        scratch_shapes=[pltpu.VMEM((length, width), BF16), DMA],
        compiler_params=params(8),
        cost_estimate=pl.CostEstimate(
            flops=length * length * DIM, bytes_accessed=4 * 2**20, transcendentals=2**21
        ),
        name="shared_part",
    )(rows, running, in_hbm(gate))


def local_kernel(
    table, kinds, inner, running_in, step_in, scores, lifted_base, n0, n1, n2, n3, out, held
):
    x, _ = block_place()
    length, width = inner.shape
    heads = width // DIM
    stretch = length // kinds.shape[0]
    each = WIDE // stretch
    for k, near in enumerate((n0, n1, n2, n3)):
        pair = lax.rem(x + XS - k, XS)
        for head in range(PAIR):
            for level in range(2):
                base = (level * PAIR + head) * DIM
                held[pair * PAIR + head, level * DIM : (level + 1) * DIM] = near[
                    base : base + DIM
                ]
    row = lax.broadcasted_iota(jnp.int32, (stretch, TILE), 0)
    column = lax.broadcasted_iota(jnp.int32, (stretch, TILE), 1)
    causal = [row + part * stretch >= column for part in range(TILE // stretch)]
    lane = lax.broadcasted_iota(jnp.int32, (1, TILE), 1)
    empty = jnp.zeros((stretch, TILE), BF16)

    def one_head(head, carry):
        lanes = pl.ds(pl.multiple_of(head * DIM, DIM), DIM)
        running = running_in[pl.ds(head, 1), :]
        step = step_in[pl.ds(head, 1), :]
        starts = [running[:, i * WIDE : i * WIDE + 1] for i in range(length // WIDE)]
        ahead = jnp.concatenate(
            [
                jnp.exp(running[:, i * WIDE : (i + 1) * WIDE] - starts[i])
                for i in range(length // WIDE)
            ],
            axis=1,
        )
        columns = jnp.broadcast_to(ahead, (8, length)).T
        for i in range(length // WIDE):
            wide = (i + 1) * WIDE
            span = slice(i * WIDE, wide)
            behind = jnp.exp(starts[i] - running[:, :wide]) * step[:, :wide]
            bands = []
            lifted = []
            for part in range(each):
                here = i * each + part
                kind = kinds[here]
                weight = [table[kind, head, level] for level in range(7)]
                band = slice(here * stretch, (here + 1) * stretch)
                ahead_column = jnp.broadcast_to(columns[band, 0:1], (stretch, TILE))
                pieces = []
                for j in range(wide // TILE):
                    first, second = 2 * j, 2 * j + 1
                    if first > here:
                        pieces.append(empty)
                        continue
                    left = weight[(here ^ first).bit_length()]
                    right = weight[(here ^ second).bit_length()]
                    if second > here or (here ^ first).bit_length() == (here ^ second).bit_length():
                        factor = left
                    else:
                        factor = jnp.where(lane < stretch, left, right)
                    tile = slice(j * TILE, (j + 1) * TILE)
                    piece = scores[band, tile] * (behind[:, tile] * factor) * ahead_column
                    if second >= here:
                        piece = jnp.where(causal[here - first], piece, 0.0)
                    pieces.append(piece.astype(BF16))
                bands.append(jnp.concatenate(pieces, axis=1))
                base = lifted_base[band, lanes]
                lifted.append(
                    jnp.concatenate(
                        [(base * weight[5 + level]).astype(BF16) for level in range(2)], axis=1
                    )
                )
            out[span, lanes] = jnp.dot(
                jnp.concatenate(bands, axis=0), inner[:wide, lanes], preferred_element_type=F32
            ) + jnp.dot(
                jnp.concatenate(lifted, axis=0), held[head], preferred_element_type=F32
            )
        return carry

    lax.fori_loop(0, heads, one_head, 0)


def local_part(table, kinds, inner, running, step, scores, lifted_base, near):
    length, width = inner.shape
    heads = width // DIM
    return pl.pallas_call(
        local_kernel,
        in_specs=[SMEM, SMEM] + [VMEM] * (5 + XS),
        out_specs=VMEM,
        out_shape=pltpu.VMEM((length, width), F32),
        scratch_shapes=[pltpu.VMEM((heads, 2 * DIM, DIM), BF16)],
        compiler_params=params(8),
        cost_estimate=pl.CostEstimate(
            flops=8 * length * length * DIM, bytes_accessed=8 * 2**20, transcendentals=2**18
        ),
        name="local_part",
    )(table, kinds, inner, running, step, scores, lifted_base, *near)


def flag(condition):
    return jnp.where(condition, 1.0, 0.0).astype(F32)


def fold_row_kernel(p0, p1, p2, p3, row_out, m0, m1, m2, m3):
    x, _ = block_place()
    parts = (p0, p1, p2, p3)
    owner = [lax.rem(x + XS - k, XS) for k in range(XS)]
    decays = [part[2 * DIM :] for part in parts]

    def from_block(block):
        return [flag(owner[k] == block) for k in range(XS)]

    def pick(values, chosen):
        return sum(value * mark for value, mark in zip(values, chosen))

    block_marks = [from_block(block) for block in range(XS)]
    later = [
        jnp.exp(sum(decays[m] * flag(owner[m] > owner[k]) for m in range(XS))) for k in range(XS)
    ]
    decay_one = jnp.exp(pick(decays, block_marks[1]))
    decay_two = jnp.exp(pick(decays, block_marks[2]))
    for head in range(PAIR):
        span = slice(head * DIM, (head + 1) * DIM)
        blocks = [part[span] for part in parts]
        row_out[span] = sum(blocks[k] * later[k][head : head + 1] for k in range(XS))
        first = pick(blocks, block_marks[0])
        third = pick(blocks, block_marks[2])
        joined = first * decay_one[head : head + 1] + pick(blocks, block_marks[1])
        for k, message in enumerate((m0, m1, m2, m3)):
            target = lax.rem(x + k, XS)
            message[span] = (
                first * flag(target == 1) + third * flag(target == 3)
            ).astype(BF16)
            message[PAIR * DIM + head * DIM : PAIR * DIM + (head + 1) * DIM] = (
                joined
                * (flag(target == 2) + flag(target == 3) * decay_two[head : head + 1])
            ).astype(BF16)
    row_out[2 * DIM :] = sum(decays)


def fold_row(parts):
    return pl.pallas_call(
        fold_row_kernel,
        in_specs=[VMEM] * XS,
        out_specs=[VMEM] * (1 + XS),
        out_shape=[pltpu.VMEM((MESSAGE, DIM), F32)] + [pltpu.VMEM((4 * DIM, DIM), BF16)] * XS,
        compiler_params=params(4),
        cost_estimate=pl.CostEstimate(flops=2**20, bytes_accessed=2**20, transcendentals=2**10),
        name="fold_row",
    )(*parts)


def fold_pair_kernel(own, other, pair_out):
    _, z = block_place()
    upper = flag(lax.rem(z, 2) == 1)
    own_decay = own[2 * DIM :]
    other_decay = other[2 * DIM :]
    own_scale = jnp.exp(other_decay * (1.0 - upper))
    other_scale = jnp.exp(own_decay * upper)
    decay = own_decay + other_decay
    coarse = jnp.floor(decay)
    middle = jnp.floor((decay - coarse) * 1024.0) / 1024.0
    rest = decay - coarse - middle
    spot = lax.broadcasted_iota(jnp.int32, (8, DIM), 0)
    tail = jnp.zeros((8, DIM), F32)
    for head in range(PAIR):
        span = slice(head * DIM, (head + 1) * DIM)
        row = slice(head, head + 1)
        state = own[span] * own_scale[row] + other[span] * other_scale[row]
        most = jnp.max(jnp.max(jnp.abs(state), axis=0, keepdims=True), axis=1, keepdims=True)
        power = jnp.ceil(jnp.log(jnp.maximum(most, 1e-30)))
        pair_out[span] = state * (jnp.exp(-power) * TOP)
        for index, value in enumerate((coarse[row], middle[row], rest[row], power)):
            tail = jnp.where(spot == 2 * index + head, value, tail)
    pair_out[2 * DIM :] = tail


def fold_pair(own, other):
    return pl.pallas_call(
        fold_pair_kernel,
        in_specs=[VMEM] * 2,
        out_specs=VMEM,
        out_shape=pltpu.VMEM((MESSAGE, DIM), F32),
        compiler_params=params(4),
        cost_estimate=pl.CostEstimate(flops=2**18, bytes_accessed=2**19, transcendentals=2**10),
        name="fold_pair",
    )(own, other)


def fold_far_kernel(d0, d1, d2, d3, other, g1, g2, g3, m0, m1, m2, m3):
    x, z = block_place()
    upper = flag(lax.rem(z, 2) == 1)
    pair = lax.div(z, 2)
    odd_pair = flag(lax.rem(pair, 2) == 1)
    third_pair = flag(pair == 2)
    last_pair = flag(pair == 3)
    decays = [part[2 * DIM :] for part in (d0, d1, d2, d3)]
    owner = [lax.rem(x + XS - k, XS) for k in range(XS)]
    tails = [part[2 * DIM :] for part in (g1, g2, g3)]
    inside = [tail[0:2] + tail[2:4] + tail[4:6] for tail in tails]
    sizes = [jnp.exp(tail[6:8]) / TOP for tail in tails]
    in_pair = other[2 * DIM : 2 * DIM + PAIR] * upper
    after = in_pair + inside[0] * last_pair
    inside_first = jnp.exp(inside[0])
    inside_last = jnp.exp(inside[1])
    for head in range(PAIR):
        span = slice(head * DIM, (head + 1) * DIM)
        row = slice(head, head + 1)
        two = other[span]
        three, second, third = (
            part[span] * size[row] for part, size in zip((g1, g2, g3), sizes)
        )
        four = (second * inside_first[row] + three) * third_pair + (
            third * inside_last[row] + second
        ) * last_pair
        for k, message in enumerate((m0, m1, m2, m3)):
            target = lax.rem(x + k, XS)
            before = sum(decays[m][row] * flag(owner[m] < target) for m in range(XS))
            factors = (
                jnp.exp(before) * upper,
                jnp.exp(before + in_pair[row]) * odd_pair,
                jnp.exp(before + after[row]),
            )
            for level, (state, factor) in enumerate(zip((two, three, four), factors)):
                base = level * PAIR * DIM + head * DIM
                message[base : base + DIM] = (state * factor).astype(BF16)


def fold_far(parts, other, gathered):
    return pl.pallas_call(
        fold_far_kernel,
        in_specs=[VMEM] * (XS + 4),
        out_specs=[VMEM] * XS,
        out_shape=[pltpu.VMEM((6 * DIM, DIM), BF16)] * XS,
        compiler_params=params(4),
        cost_estimate=pl.CostEstimate(flops=2**20, bytes_accessed=2**20, transcendentals=2**12),
        name="fold_far",
    )(*parts, other, *gathered)


def far_kernel(
    table, kinds, local, gates, lifted_base, f0, f1, f2, f3, gated, squares, held, total
):
    x, _ = block_place()
    length, width = local.shape
    heads = width // DIM
    for k, far in enumerate((f0, f1, f2, f3)):
        pair = lax.rem(x + XS - k, XS)
        for head in range(PAIR):
            for level in range(3):
                base = (level * PAIR + head) * DIM
                held[pair * PAIR + head, level * DIM : (level + 1) * DIM] = far[base : base + DIM]
    total[...] = jnp.zeros_like(total)

    stretch = length // kinds.shape[0]

    def one_head(head, carry):
        lanes = pl.ds(pl.multiple_of(head * DIM, DIM), DIM)
        for tile in range(length // WIDE):
            span = slice(tile * WIDE, (tile + 1) * WIDE)
            lifted = []
            for here in range(tile * WIDE // stretch, (tile + 1) * WIDE // stretch):
                kind = kinds[here]
                base = lifted_base[here * stretch : (here + 1) * stretch, lanes]
                lifted.append(
                    jnp.concatenate(
                        [
                            (base * table[kind, head, 7 + level]).astype(BF16)
                            for level in range(3)
                        ],
                        axis=1,
                    )
                )
            mixed = local[span, lanes] + jnp.dot(
                jnp.concatenate(lifted, axis=0), held[head], preferred_element_type=F32
            )
            value = mixed * gates[span, lanes]
            gated[span, lanes] = value
            total[span] += value * value
        return carry

    lax.fori_loop(0, heads, one_head, 0)
    for tile in range(length // TILE):
        part = total[tile * TILE : (tile + 1) * TILE].T
        squares[tile : tile + 1] = jnp.sum(part, axis=0, keepdims=True)


def far_part(table, kinds, local, gates, lifted_base, far_states):
    length, width = local.shape
    heads = width // DIM
    return pl.pallas_call(
        far_kernel,
        in_specs=[SMEM, SMEM] + [VMEM] * (3 + XS),
        out_specs=[VMEM] * 2,
        out_shape=[pltpu.VMEM((length, width), F32), pltpu.VMEM((length // TILE, TILE), F32)],
        scratch_shapes=[pltpu.VMEM((heads, 3 * DIM, DIM), BF16), pltpu.VMEM((length, DIM), F32)],
        compiler_params=params(8),
        cost_estimate=pl.CostEstimate(
            flops=6 * length * width * DIM, bytes_accessed=12 * 2**20, transcendentals=0
        ),
        name="far_part",
    )(table, kinds, local, gates, lifted_base, *far_states)


def norm_kernel(total_width, gated, s0, s1, s2, s3, gain, out, made, sems):
    scale = lax.rsqrt((s0[...] + s1[...] + s2[...] + s3[...]) / total_width + 1e-05)
    length, width = gated.shape
    copies = []
    for tile in range(length // TILE):
        span = slice(tile * TILE, (tile + 1) * TILE)
        column = jnp.broadcast_to(scale[tile : tile + 1], (TILE, TILE)).T
        for piece in range(width // TILE):
            lane = slice(piece * TILE, (piece + 1) * TILE)
            made[span, lane] = (gated[span, lane] * column * gain[:, lane]).astype(BF16)
        copies.append(pltpu.make_async_copy(made.at[span], out.at[span], sems.at[tile]))
        copies[-1].start()
    for copy in copies:
        copy.wait()


def norm(gated, squares, gain, total_width):
    length, width = gated.shape
    return pl.pallas_call(
        functools.partial(norm_kernel, total_width),
        in_specs=[VMEM] * (2 + YS),
        out_specs=HBM,
        out_shape=jax.ShapeDtypeStruct((length, width), BF16),
        scratch_shapes=[pltpu.VMEM((length, width), BF16), DMA((length // TILE,))],
        compiler_params=params(8),
        cost_estimate=pl.CostEstimate(
            flops=2 * length * width, bytes_accessed=6 * 2**20, transcendentals=2**10
        ),
        name="norm",
    )(gated, *squares, gain)


def local(
    mixer_input,
    state_input,
    gate_input,
    step_raw,
    decay_rate,
    conv_inner,
    conv_state,
    level_table,
    stretch_kind,
    norm_gain,
):
    length, width = mixer_input.shape
    tails = jnp.concatenate([mixer_input[length - HALO :], state_input[length - HALO :]], axis=1)
    halo = lax.ppermute(tails, "seq", [(i, i + 1) for i in range(XS * ZS - 1)])
    inner, rows, running, step, *parts = prepare(
        mixer_input, halo, state_input, conv_inner, conv_state, step_raw.T, decay_rate
    )
    table = jnp.transpose(level_table, (0, 2, 1))
    arrived = [parts[0]] + [along_x(parts[k], k) for k in range(1, XS)]
    shared = shared_part(rows, running, gate_input)
    arrived, shared = lax.optimization_barrier((arrived, shared))
    scores, gates, lifted_base = shared
    row_state, *near = fold_row(arrived)
    near = [near[0]] + [along_x(near[k], k) for k in range(1, XS)]
    other = lax.ppermute(row_state, "seq", seq_perm(lambda z, x: (z ^ 1, x)))
    pair_state = fold_pair(row_state, other)
    narrow = pair_state.astype(jnp.float16)
    moves = (
        lambda z, x: (z + 2, x) if z + 2 < ZS else None,
        lambda z, x: ((z ^ 1) + 4, x) if z + 4 < ZS else None,
        lambda z, x: (z + 6, x) if z + 6 < ZS else None,
    )
    gathered = [lax.ppermute(narrow, "seq", seq_perm(move)).astype(F32) for move in moves]
    far = fold_far(arrived, other, gathered)
    far = [far[0]] + [along_x(far[k], k) for k in range(1, XS)]
    local_out = local_part(
        table, stretch_kind, inner, running, step, scores, lifted_base, near
    )
    gated, squares = far_part(table, stretch_kind, local_out, gates, lifted_base, far)
    squares = squares + lax.ppermute(squares, "head", head_perm(lambda y, core: (y, 1 - core)))
    sums = [squares] + [
        lax.ppermute(squares, "head", head_perm(lambda y, core, k=k: ((y + k) % YS, core)))
        for k in range(1, YS)
    ]
    total_width = width * lax.axis_size("head")
    return norm(gated, sums, norm_gain[None, :], total_width)


def solution(mesh):
    return jax.shard_map(
        local,
        mesh=mesh,
        in_specs=(
            P("seq", "head"),
            P("seq", None),
            P("seq", "head"),
            P("seq", "head"),
            P("head"),
            P(None, "head"),
            P(),
            P(None, None, "head"),
            P("seq"),
            P("head"),
        ),
        out_specs=P("seq", "head"),
        check_vma=False,
    )
```

```python
import functools
import jax
import jax.numpy as jnp
from jax import lax
from jax.experimental import pallas as pl
from jax.experimental.pallas import tpu as pltpu
from jax.sharding import PartitionSpec as P

F32 = jnp.float32
BF16 = jnp.bfloat16

XS = 4
ZS = 8
YS = 4
CORES = 2
PAIR = 2
DIM = 128
HALO = 16
TILE = 128
WIDE = 256
TOP = 16384.0
MESSAGE = PAIR * DIM + 8


def seq_perm(move):
    pairs = []
    for z in range(ZS):
        for x in range(XS):
            target = move(z, x)
            if target is not None:
                pairs.append((z * XS + x, target[0] * XS + target[1]))
    return pairs


def head_perm(move):
    pairs = []
    for y in range(YS):
        for core in range(CORES):
            target = move(y, core)
            pairs.append((y * CORES + core, target[0] * CORES + target[1]))
    return pairs


def along_x(value, step):
    return lax.ppermute(value, "seq", seq_perm(lambda z, x: (z, (x + step) % XS)))


def sent(message, move):
    return lax.ppermute(message.astype(jnp.float16), "seq", seq_perm(move)).astype(F32)


def silu(value):
    half = 0.5 * value
    return half + half * jnp.tanh(half)


VMEM = pl.BlockSpec(memory_space=pltpu.VMEM)
SMEM = pl.BlockSpec(memory_space=pltpu.SMEM)
HBM = pl.BlockSpec(memory_space=pltpu.HBM)
DMA = pltpu.SemaphoreType.DMA


def params(mebibytes):
    return pltpu.CompilerParams(vmem_limit_bytes=mebibytes * 2**20)


def in_hbm(value):
    return pltpu.with_memory_space_constraint(value, pltpu.HBM)


def block_place():
    index = lax.axis_index("seq")
    return lax.rem(index, XS), lax.div(index, XS)


def conv(block, halo, taps):
    length = block.shape[0]
    width = taps.shape[0]
    joined = jnp.concatenate([halo[HALO - 8 :].astype(F32), block.astype(F32)], axis=0)
    taps = taps.astype(F32)
    total = jnp.zeros((length, block.shape[1]), F32)
    for offset in range(width):
        shift = width - 1 - offset
        moved = joined if shift == 0 else pltpu.roll(joined, shift, axis=0)
        total = total + moved[8:] * taps[offset : offset + 1]
    return silu(total).astype(BF16)


def flag(condition):
    return jnp.where(condition, 1.0, 0.0).astype(F32)


def encode(message, states, decays):
    spot = lax.broadcasted_iota(jnp.int32, (8, DIM), 0)
    tail = jnp.zeros((8, DIM), F32)
    for head in range(PAIR):
        state, decay = states[head], decays[head]
        coarse = jnp.floor(decay)
        middle = jnp.floor((decay - coarse) * 1024.0) / 1024.0
        rest = decay - coarse - middle
        most = jnp.max(jnp.max(jnp.abs(state), axis=0, keepdims=True), axis=1, keepdims=True)
        power = jnp.ceil(jnp.log(jnp.maximum(most, 1e-30)))
        message[head * DIM : (head + 1) * DIM] = state * (jnp.exp(-power) * TOP)
        for index, value in enumerate((coarse, middle, rest, power)):
            tail = jnp.where(spot == PAIR * index + head, value, tail)
    message[PAIR * DIM :] = tail


def decode_decay(message):
    tail = message[PAIR * DIM :]
    return tail[:PAIR] + tail[PAIR : 2 * PAIR] + tail[2 * PAIR : 3 * PAIR]


def decode_size(message):
    return jnp.exp(message[PAIR * DIM :][3 * PAIR :]) / TOP


def tails_kernel(mixer, state, out, sems):
    length, width = mixer.shape
    span = pl.ds(length - HALO, HALO)
    copies = [
        pltpu.make_async_copy(mixer.at[span], out.at[:, :width], sems.at[0]),
        pltpu.make_async_copy(state.at[span], out.at[:, width:], sems.at[1]),
    ]
    for copy in copies:
        copy.start()
    for copy in copies:
        copy.wait()


def last_rows(mixer, state):
    return pl.pallas_call(
        tails_kernel,
        in_specs=[HBM, HBM],
        out_specs=VMEM,
        out_shape=pltpu.VMEM((HALO, mixer.shape[1] + state.shape[1]), BF16),
        scratch_shapes=[DMA((2,))],
        compiler_params=params(2),
        name="last_rows",
    )(in_hbm(mixer), in_hbm(state))


def prepare_kernel(
    mixer,
    state,
    taps,
    state_taps,
    step_raw,
    rate,
    inner,
    rows,
    running_out,
    step_out,
    first_rows,
    first_scale,
    last,
    taps_here,
    part0,
    part1,
    part2,
    part3,
    mixer_here,
    state_here,
    raw_here,
    rate_here,
    keys_t,
    scale,
    mixer_sem,
    small_sem,
):
    x, _ = block_place()
    heads, length = step_raw.shape
    width = mixer.shape[1]
    wide = PAIR * DIM
    small = [
        pltpu.make_async_copy(source, target, small_sem.at[n])
        for n, (source, target) in enumerate(
            (
                (step_raw, raw_here),
                (rate, rate_here),
                (state, state_here),
                (state_taps, taps_here.at[:, width:]),
                (taps, taps_here.at[:, :width]),
            )
        )
    ]
    for copy in small:
        copy.start()
    pairs = [lax.rem(x + turn, XS) for turn in range(XS)]
    columns = [pl.ds(pl.multiple_of(pair * wide, wide), wide) for pair in pairs]
    large = [
        pltpu.make_async_copy(
            mixer.at[:, columns[turn]], mixer_here.at[turn], mixer_sem.at[turn]
        )
        for turn in range(XS)
    ]
    for copy in large:
        copy.start()

    for copy in small:
        copy.wait()
    raw = raw_here[...]
    step = jnp.maximum(raw, 0.0) + jnp.log1p(jnp.exp(-jnp.abs(raw)))
    spot = lax.broadcasted_iota(jnp.int32, (heads, length), 0)
    rates = jnp.zeros((heads, length), F32)
    for head in range(heads):
        rates = jnp.where(spot == head, rate_here[head], rates)
    running = -rates * step
    lane = lax.broadcasted_iota(jnp.int32, (heads, length), 1)
    shift = 1
    while shift < length:
        moved = pltpu.roll(running, shift, axis=1)
        running = running + jnp.where(lane >= shift, moved, 0.0)
        shift *= 2
    final = running[:, length - 1 :]
    running_out[...] = running
    step_out[...] = step
    scaled = jnp.exp(final - running) * step
    first_scale[...] = scaled[:, :DIM]
    scale[...] = jnp.where(lane < HALO, 0.0, scaled)
    last[...] = jnp.broadcast_to(final, last.shape)
    nothing = jnp.zeros((HALO, wide), BF16)
    first_rows[:, width:] = state_here[:HALO]
    state_rows = conv(state_here[...], nothing, taps_here[:, width:])
    rows[...] = state_rows
    keys_t[...] = state_rows[:, :DIM].astype(F32).T

    for turn, part in enumerate((part0, part1, part2, part3)):
        large[turn].wait()
        first_rows[:, columns[turn]] = mixer_here[turn, :HALO]
        values = conv(mixer_here[turn], nothing, taps_here[:, columns[turn]])
        inner[:, columns[turn]] = values
        for head in range(PAIR):
            row = scale[pl.ds(pairs[turn] * PAIR + head, 1), :]
            scaled_t = (keys_t[...] * row).astype(BF16)
            part[head * DIM : (head + 1) * DIM] = jnp.dot(
                scaled_t, values[:, head * DIM : (head + 1) * DIM], preferred_element_type=F32
            )


def prepare(mixer, state, taps, state_taps, step_raw_t, rate):
    length, width = mixer.shape
    heads = step_raw_t.shape[0]
    every = width + 2 * DIM
    return pl.pallas_call(
        prepare_kernel,
        in_specs=[HBM] * 6,
        out_specs=[VMEM] * (8 + XS),
        out_shape=[
            pltpu.VMEM((length, width), BF16),
            pltpu.VMEM((length, 2 * DIM), BF16),
            pltpu.VMEM((heads, length), F32),
            pltpu.VMEM((heads, length), F32),
            pltpu.VMEM((HALO, every), BF16),
            pltpu.VMEM((heads, DIM), F32),
            pltpu.VMEM((heads, DIM), F32),
            pltpu.VMEM((taps.shape[0], every), BF16),
        ]
        + [pltpu.VMEM((PAIR * DIM, DIM), F32)] * XS,
        scratch_shapes=[
            pltpu.VMEM((XS, length, PAIR * DIM), BF16),
            pltpu.VMEM((length, 2 * DIM), BF16),
            pltpu.VMEM((heads, length), F32),
            pltpu.SMEM((heads,), F32),
            pltpu.VMEM((DIM, length), F32),
            pltpu.VMEM((heads, length), F32),
            DMA((XS,)),
            DMA((5,)),
        ],
        compiler_params=params(16),
        cost_estimate=pl.CostEstimate(
            flops=2 * length * width * DIM, bytes_accessed=8 * 2**20, transcendentals=2 * length * width
        ),
        name="prepare",
    )(
        in_hbm(mixer),
        in_hbm(state),
        in_hbm(taps),
        in_hbm(state_taps),
        in_hbm(step_raw_t),
        in_hbm(rate),
    )


def finish_kernel(
    halo,
    first_rows,
    first_scale,
    last,
    taps,
    inner_in,
    rows_in,
    p0,
    p1,
    p2,
    p3,
    inner,
    rows,
    m0,
    m1,
    m2,
    m3,
):
    x, _ = block_place()
    width = inner.shape[1]
    heads = width // DIM
    wide = PAIR * DIM
    made = conv(first_rows[:, width:], halo[:, width:], taps[:, width:])
    rows[:HALO] = made
    keys = made[:, :DIM].astype(F32)
    columns = first_scale[...].T
    scaled = [
        (keys * jnp.broadcast_to(columns[:HALO, head : head + 1], (HALO, DIM))).astype(BF16)
        for head in range(heads)
    ]
    added = []
    for pair in range(XS):
        lanes = slice(pair * wide, (pair + 1) * wide)
        values = conv(first_rows[:, lanes], halo[:, lanes], taps[:, lanes])
        inner[:HALO, lanes] = values
        for head in range(PAIR):
            added.append(
                lax.dot_general(
                    scaled[pair * PAIR + head],
                    values[:, head * DIM : (head + 1) * DIM],
                    (((0,), (0,)), ((), ())),
                    preferred_element_type=F32,
                )
            )
    for turn, (part, message) in enumerate(((p0, m0), (p1, m1), (p2, m2), (p3, m3))):
        pair = lax.rem(x + turn, XS)
        states = []
        decays = []
        for head in range(PAIR):
            extra = sum(
                added[other * PAIR + head] * flag(pair == other) for other in range(XS)
            )
            states.append(part[head * DIM : (head + 1) * DIM] + extra)
            decays.append(last[pl.ds(pair * PAIR + head, 1), :])
        encode(message, states, decays)


def finish(halo, first_rows, first_scale, last, taps, inner, rows, parts):
    return pl.pallas_call(
        finish_kernel,
        in_specs=[VMEM] * (7 + XS),
        out_specs=[VMEM] * (2 + XS),
        out_shape=[pltpu.VMEM(inner.shape, BF16), pltpu.VMEM(rows.shape, BF16)]
        + [pltpu.VMEM((MESSAGE, DIM), F32)] * XS,
        input_output_aliases={5: 0, 6: 1},
        compiler_params=params(4),
        cost_estimate=pl.CostEstimate(flops=2**22, bytes_accessed=2**20, transcendentals=2**14),
        name="finish",
    )(halo, first_rows, first_scale, last, taps, inner, rows, *parts)


def shared_kernel(
    rows, running_in, gate, scores, gates, lifted_base, ahead_out, gate_here, gate_sem
):
    length, width = gate.shape
    heads = width // DIM
    tiles = length // TILE
    gate_copy = pltpu.make_async_copy(gate, gate_here, gate_sem)
    gate_copy.start()
    for i in range(tiles):
        wide = (i + 1) * TILE
        scores[i * TILE : wide, :wide] = lax.dot_general(
            rows[i * TILE : wide, DIM:],
            rows[:wide, :DIM],
            (((1,), (1,)), ((), ())),
            preferred_element_type=F32,
        )
    running = running_in[...]
    columns = jnp.exp(running).T
    ahead = jnp.concatenate(
        [
            jnp.exp(running[:, i * WIDE : (i + 1) * WIDE] - running[:, i * WIDE : i * WIDE + 1])
            for i in range(length // WIDE)
        ],
        axis=1,
    ).T
    for i in range(tiles):
        span = slice(i * TILE, (i + 1) * TILE)
        queries = rows[span, DIM:].astype(F32)
        for head in range(heads):
            lanes = slice(head * DIM, (head + 1) * DIM)
            lifted_base[span, lanes] = queries * jnp.broadcast_to(
                columns[span, head : head + 1], (TILE, DIM)
            )
            ahead_out[span, lanes] = jnp.broadcast_to(ahead[span, head : head + 1], (TILE, DIM))
    gate_copy.wait()

    def one_tile(tile, carry):
        span = pl.ds(pl.multiple_of(tile * TILE, TILE), TILE)
        for piece in range(width // DIM):
            lane = slice(piece * DIM, (piece + 1) * DIM)
            gates[span, lane] = silu(gate_here[span, lane].astype(F32))
        return carry

    lax.fori_loop(0, tiles, one_tile, 0)


def shared_part(rows, running, gate):
    length, width = gate.shape
    return pl.pallas_call(
        shared_kernel,
        in_specs=[VMEM, VMEM, HBM],
        out_specs=[VMEM] * 4,
        out_shape=[pltpu.VMEM((length, length), F32)] + [pltpu.VMEM((length, width), F32)] * 3,
        scratch_shapes=[pltpu.VMEM((length, width), BF16), DMA],
        compiler_params=params(8),
        cost_estimate=pl.CostEstimate(
            flops=length * length * DIM, bytes_accessed=4 * 2**20, transcendentals=2**21
        ),
        name="shared_part",
    )(rows, running, in_hbm(gate))


def local_kernel(
    table,
    kinds,
    inner,
    running_in,
    step_in,
    scores,
    lifted_base,
    ahead_in,
    n0,
    n1,
    n2,
    n3,
    out,
    held,
):
    x, _ = block_place()
    length, width = inner.shape
    heads = width // DIM
    stretch = length // kinds.shape[0]
    each = WIDE // stretch
    for k, near in enumerate((n0, n1, n2, n3)):
        pair = lax.rem(x + XS - k, XS)
        for head in range(PAIR):
            for level in range(2):
                base = (level * PAIR + head) * DIM
                held[pair * PAIR + head, level * DIM : (level + 1) * DIM] = near[
                    base : base + DIM
                ]
    row = lax.broadcasted_iota(jnp.int32, (stretch, TILE), 0)
    column = lax.broadcasted_iota(jnp.int32, (stretch, TILE), 1)
    causal = [row + part * stretch >= column for part in range(TILE // stretch)]
    lane = lax.broadcasted_iota(jnp.int32, (1, TILE), 1)
    empty = jnp.zeros((stretch, TILE), BF16)

    def one_head(head, carry):
        lanes = pl.ds(pl.multiple_of(head * DIM, DIM), DIM)
        running = running_in[pl.ds(head, 1), :]
        step = step_in[pl.ds(head, 1), :]
        starts = [running[:, i * WIDE : i * WIDE + 1] for i in range(length // WIDE)]
        for i in range(length // WIDE):
            wide = (i + 1) * WIDE
            span = slice(i * WIDE, wide)
            behind = jnp.exp(starts[i] - running[:, :wide]) * step[:, :wide]
            bands = []
            lifted = []
            for part in range(each):
                here = i * each + part
                kind = kinds[here]
                weight = [table[kind, head, level] for level in range(7)]
                band = slice(here * stretch, (here + 1) * stretch)
                ahead = ahead_in[band, lanes]
                pieces = []
                for j in range(wide // TILE):
                    first, second = 2 * j, 2 * j + 1
                    if first > here:
                        pieces.append(empty)
                        continue
                    left = weight[(here ^ first).bit_length()]
                    right = weight[(here ^ second).bit_length()]
                    if second > here or (here ^ first).bit_length() == (here ^ second).bit_length():
                        factor = left
                    else:
                        factor = jnp.where(lane < stretch, left, right)
                    tile = slice(j * TILE, (j + 1) * TILE)
                    piece = scores[band, tile] * (behind[:, tile] * factor) * ahead
                    if second >= here:
                        piece = jnp.where(causal[here - first], piece, 0.0)
                    pieces.append(piece.astype(BF16))
                bands.append(jnp.concatenate(pieces, axis=1))
                base = lifted_base[band, lanes]
                lifted.append(
                    jnp.concatenate(
                        [(base * weight[5 + level]).astype(BF16) for level in range(2)], axis=1
                    )
                )
            out[span, lanes] = jnp.dot(
                jnp.concatenate(bands, axis=0), inner[:wide, lanes], preferred_element_type=F32
            ) + jnp.dot(
                jnp.concatenate(lifted, axis=0), held[head], preferred_element_type=F32
            )
        return carry

    lax.fori_loop(0, heads, one_head, 0, unroll=4)


def local_part(table, kinds, inner, running, step, scores, lifted_base, ahead, near):
    length, width = inner.shape
    heads = width // DIM
    return pl.pallas_call(
        local_kernel,
        in_specs=[SMEM, SMEM] + [VMEM] * (6 + XS),
        out_specs=VMEM,
        out_shape=pltpu.VMEM((length, width), F32),
        scratch_shapes=[pltpu.VMEM((heads, 2 * DIM, DIM), BF16)],
        compiler_params=params(8),
        cost_estimate=pl.CostEstimate(
            flops=8 * length * length * DIM, bytes_accessed=8 * 2**20, transcendentals=2**18
        ),
        name="local_part",
    )(table, kinds, inner, running, step, scores, lifted_base, ahead, *near)


def fold_row_kernel(p0, p1, p2, p3, row_out, m0, m1, m2, m3):
    x, _ = block_place()
    parts = (p0, p1, p2, p3)
    owner = [lax.rem(x + XS - k, XS) for k in range(XS)]
    decays = [decode_decay(part) for part in parts]
    sizes = [decode_size(part) for part in parts]

    def pick(values, block):
        return sum(value * flag(owner[k] == block) for k, value in enumerate(values))

    later = [
        jnp.exp(sum(decays[m] * flag(owner[m] > owner[k]) for m in range(XS))) * sizes[k]
        for k in range(XS)
    ]
    decay_one = jnp.exp(pick(decays, 1))
    decay_two = jnp.exp(pick(decays, 2))
    total = sum(decays)
    row_states = []
    for head in range(PAIR):
        span = slice(head * DIM, (head + 1) * DIM)
        row = slice(head, head + 1)
        blocks = [part[span] for part in parts]
        row_states.append(sum(blocks[k] * later[k][row] for k in range(XS)))
        scaled = [blocks[k] * sizes[k][row] for k in range(XS)]
        first = pick(scaled, 0)
        third = pick(scaled, 2)
        joined = first * decay_one[row] + pick(scaled, 1)
        for k, message in enumerate((m0, m1, m2, m3)):
            target = lax.rem(x + k, XS)
            message[span] = (
                first * flag(target == 1) + third * flag(target == 3)
            ).astype(BF16)
            message[PAIR * DIM + head * DIM : PAIR * DIM + (head + 1) * DIM] = (
                joined * (flag(target == 2) + flag(target == 3) * decay_two[row])
            ).astype(BF16)
    encode(row_out, row_states, [total[head : head + 1] for head in range(PAIR)])


def fold_row(parts):
    return pl.pallas_call(
        fold_row_kernel,
        in_specs=[VMEM] * XS,
        out_specs=[VMEM] * (1 + XS),
        out_shape=[pltpu.VMEM((MESSAGE, DIM), F32)] + [pltpu.VMEM((4 * DIM, DIM), BF16)] * XS,
        compiler_params=params(4),
        cost_estimate=pl.CostEstimate(flops=2**20, bytes_accessed=2**20, transcendentals=2**10),
        name="fold_row",
    )(*parts)


def fold_two_kernel(span_rows, own, other, out):
    _, z = block_place()
    upper = flag(lax.rem(lax.div(z, span_rows), 2) == 1)
    own_decay = decode_decay(own)
    other_decay = decode_decay(other)
    own_scale = jnp.exp(other_decay * (1.0 - upper)) * decode_size(own)
    other_scale = jnp.exp(own_decay * upper) * decode_size(other)
    decay = own_decay + other_decay
    states = []
    for head in range(PAIR):
        span = slice(head * DIM, (head + 1) * DIM)
        row = slice(head, head + 1)
        states.append(own[span] * own_scale[row] + other[span] * other_scale[row])
    encode(out, states, [decay[head : head + 1] for head in range(PAIR)])


def fold_two(span_rows, own, other):
    return pl.pallas_call(
        functools.partial(fold_two_kernel, span_rows),
        in_specs=[VMEM] * 2,
        out_specs=VMEM,
        out_shape=pltpu.VMEM((MESSAGE, DIM), F32),
        compiler_params=params(4),
        cost_estimate=pl.CostEstimate(flops=2**18, bytes_accessed=2**19, transcendentals=2**10),
        name="fold_two",
    )(own, other)


def fold_far_kernel(d0, d1, d2, d3, row_before, pair_before, quad_before, m0, m1, m2, m3):
    x, z = block_place()
    odd = flag(lax.rem(z, 2) == 1)
    odd_pair = flag(lax.rem(lax.div(z, 2), 2) == 1)
    upper = flag(z >= ZS // 2)
    decays = [decode_decay(part) for part in (d0, d1, d2, d3)]
    owner = [lax.rem(x + XS - k, XS) for k in range(XS)]
    in_pair = decode_decay(row_before) * odd
    in_quad = in_pair + decode_decay(pair_before) * odd_pair
    levels = (
        (row_before, jnp.zeros_like(in_pair), decode_size(row_before) * odd),
        (pair_before, in_pair, decode_size(pair_before) * odd_pair),
        (quad_before, in_quad, decode_size(quad_before) * upper),
    )
    for k, message in enumerate((m0, m1, m2, m3)):
        target = lax.rem(x + k, XS)
        before = sum(decays[m] * flag(owner[m] < target) for m in range(XS))
        for level, (state, between, size) in enumerate(levels):
            factor = jnp.exp(before + between) * size
            for head in range(PAIR):
                base = (level * PAIR + head) * DIM
                message[base : base + DIM] = (
                    state[head * DIM : (head + 1) * DIM] * factor[head : head + 1]
                ).astype(BF16)


def fold_far(parts, befores):
    return pl.pallas_call(
        fold_far_kernel,
        in_specs=[VMEM] * (XS + 3),
        out_specs=[VMEM] * XS,
        out_shape=[pltpu.VMEM((6 * DIM, DIM), BF16)] * XS,
        compiler_params=params(4),
        cost_estimate=pl.CostEstimate(flops=2**20, bytes_accessed=2**20, transcendentals=2**12),
        name="fold_far",
    )(*parts, *befores)


def far_kernel(
    table, kinds, local, gates, lifted_base, f0, f1, f2, f3, gated, squares, held, total
):
    x, _ = block_place()
    length, width = local.shape
    heads = width // DIM
    for k, far in enumerate((f0, f1, f2, f3)):
        pair = lax.rem(x + XS - k, XS)
        for head in range(PAIR):
            for level in range(3):
                base = (level * PAIR + head) * DIM
                held[pair * PAIR + head, level * DIM : (level + 1) * DIM] = far[base : base + DIM]
    total[...] = jnp.zeros_like(total)

    stretch = length // kinds.shape[0]

    def one_head(head, carry):
        lanes = pl.ds(pl.multiple_of(head * DIM, DIM), DIM)
        for tile in range(length // WIDE):
            span = slice(tile * WIDE, (tile + 1) * WIDE)
            lifted = []
            for here in range(tile * WIDE // stretch, (tile + 1) * WIDE // stretch):
                kind = kinds[here]
                base = lifted_base[here * stretch : (here + 1) * stretch, lanes]
                lifted.append(
                    jnp.concatenate(
                        [
                            (base * table[kind, head, 7 + level]).astype(BF16)
                            for level in range(3)
                        ],
                        axis=1,
                    )
                )
            mixed = local[span, lanes] + jnp.dot(
                jnp.concatenate(lifted, axis=0), held[head], preferred_element_type=F32
            )
            value = mixed * gates[span, lanes]
            gated[span, lanes] = value
            total[span] += value * value
        return carry

    lax.fori_loop(0, heads, one_head, 0, unroll=4)
    for tile in range(length // TILE):
        part = total[tile * TILE : (tile + 1) * TILE].T
        squares[tile : tile + 1] = jnp.sum(part, axis=0, keepdims=True)


def far_part(table, kinds, local, gates, lifted_base, far_states):
    length, width = local.shape
    heads = width // DIM
    return pl.pallas_call(
        far_kernel,
        in_specs=[SMEM, SMEM] + [VMEM] * (3 + XS),
        out_specs=[VMEM] * 2,
        out_shape=[pltpu.VMEM((length, width), F32), pltpu.VMEM((length // TILE, TILE), F32)],
        scratch_shapes=[pltpu.VMEM((heads, 3 * DIM, DIM), BF16), pltpu.VMEM((length, DIM), F32)],
        compiler_params=params(8),
        cost_estimate=pl.CostEstimate(
            flops=6 * length * width * DIM, bytes_accessed=12 * 2**20, transcendentals=0
        ),
        name="far_part",
    )(table, kinds, local, gates, lifted_base, *far_states)


def norm_kernel(total_width, gated, s0, s1, s2, s3, gain, out, made, sems):
    scale = lax.rsqrt((s0[...] + s1[...] + s2[...] + s3[...]) / total_width + 1e-05)
    length, width = gated.shape
    copies = []
    for tile in range(length // TILE):
        span = slice(tile * TILE, (tile + 1) * TILE)
        column = jnp.broadcast_to(scale[tile : tile + 1], (TILE, TILE)).T
        for piece in range(width // TILE):
            lane = slice(piece * TILE, (piece + 1) * TILE)
            made[span, lane] = (gated[span, lane] * column * gain[:, lane]).astype(BF16)
        copies.append(pltpu.make_async_copy(made.at[span], out.at[span], sems.at[tile]))
        copies[-1].start()
    for copy in copies:
        copy.wait()


def norm(gated, squares, gain, total_width):
    length, width = gated.shape
    return pl.pallas_call(
        functools.partial(norm_kernel, total_width),
        in_specs=[VMEM] * (2 + YS),
        out_specs=HBM,
        out_shape=jax.ShapeDtypeStruct((length, width), BF16),
        scratch_shapes=[pltpu.VMEM((length, width), BF16), DMA((length // TILE,))],
        compiler_params=params(8),
        cost_estimate=pl.CostEstimate(
            flops=2 * length * width, bytes_accessed=6 * 2**20, transcendentals=2**10
        ),
        name="norm",
    )(gated, *squares, gain)


def local(
    mixer_input,
    state_input,
    gate_input,
    step_raw,
    decay_rate,
    conv_inner,
    conv_state,
    level_table,
    stretch_kind,
    norm_gain,
):
    length, width = mixer_input.shape
    halo = lax.ppermute(
        last_rows(mixer_input, state_input), "seq", [(i, i + 1) for i in range(XS * ZS - 1)]
    )
    inner, rows, running, step, first_rows, first_scale, last, taps, *parts = prepare(
        mixer_input, state_input, conv_inner, conv_state, step_raw.T, decay_rate
    )
    inner, rows, *parts = finish(halo, first_rows, first_scale, last, taps, inner, rows, parts)
    table = jnp.transpose(level_table, (0, 2, 1))
    arrived = [parts[0]] + [
        sent(parts[k], lambda z, x, k=k: (z, (x + k) % XS)) for k in range(1, XS)
    ]
    shared = shared_part(rows, running, gate_input)
    arrived, shared = lax.optimization_barrier((arrived, shared))
    scores, gates, lifted_base, ahead = shared
    row_state, *near = fold_row(arrived)
    near = [near[0]] + [along_x(near[k], k) for k in range(1, XS)]
    row_before = sent(row_state, lambda z, x: (z ^ 1, x))
    pair_state = fold_two(1, row_state, row_before)
    pair_before = sent(pair_state, lambda z, x: (z ^ 2, x))
    quad_state = fold_two(2, pair_state, pair_before)
    quad_before = sent(quad_state, lambda z, x: (ZS - 1 - z, x) if z < ZS // 2 else None)
    far = fold_far(arrived, (row_before, pair_before, quad_before))
    far = [far[0]] + [along_x(far[k], k) for k in range(1, XS)]
    local_out = local_part(
        table, stretch_kind, inner, running, step, scores, lifted_base, ahead, near
    )
    gated, squares = far_part(table, stretch_kind, local_out, gates, lifted_base, far)
    squares = squares + lax.ppermute(squares, "head", head_perm(lambda y, core: (y, 1 - core)))
    sums = [squares] + [
        lax.ppermute(squares, "head", head_perm(lambda y, core, k=k: ((y + k) % YS, core)))
        for k in range(1, YS)
    ]
    total_width = width * lax.axis_size("head")
    return norm(gated, sums, norm_gain[None, :], total_width)


def solution(mesh):
    return jax.shard_map(
        local,
        mesh=mesh,
        in_specs=(
            P("seq", "head"),
            P("seq", None),
            P("seq", "head"),
            P("seq", "head"),
            P("head"),
            P(None, "head"),
            P(),
            P(None, None, "head"),
            P("seq"),
            P("head"),
        ),
        out_specs=P("seq", "head"),
        check_vma=False,
    )
```

```python
import functools
import jax
import jax.numpy as jnp
from jax import lax
from jax.experimental import pallas as pl
from jax.experimental.pallas import tpu as pltpu
from jax.sharding import PartitionSpec as P

F32 = jnp.float32
BF16 = jnp.bfloat16

XS = 4
ZS = 8
YS = 4
CORES = 2
PAIR = 2
DIM = 128
HALO = 16
TILE = 128
WIDE = 256
NEAR = 3
FAR = 2
TOP = 16384.0
MESSAGE = PAIR * DIM + 8


def seq_perm(move):
    pairs = []
    for z in range(ZS):
        for x in range(XS):
            target = move(z, x)
            if target is not None:
                pairs.append((z * XS + x, target[0] * XS + target[1]))
    return pairs


def head_perm(move):
    pairs = []
    for y in range(YS):
        for core in range(CORES):
            target = move(y, core)
            pairs.append((y * CORES + core, target[0] * CORES + target[1]))
    return pairs


def along_x(value, step):
    return lax.ppermute(value, "seq", seq_perm(lambda z, x: (z, (x + step) % XS)))


def sent(message, move):
    return lax.ppermute(message.astype(jnp.float16), "seq", seq_perm(move)).astype(F32)


def silu(value):
    half = 0.5 * value
    return half + half * jnp.tanh(half)


VMEM = pl.BlockSpec(memory_space=pltpu.VMEM)
SMEM = pl.BlockSpec(memory_space=pltpu.SMEM)
HBM = pl.BlockSpec(memory_space=pltpu.HBM)
DMA = pltpu.SemaphoreType.DMA


def params(mebibytes):
    return pltpu.CompilerParams(vmem_limit_bytes=mebibytes * 2**20)


def cost(microseconds):
    return pl.CostEstimate(
        flops=int(microseconds * 1.15e9),
        bytes_accessed=int(microseconds * 3.6e6),
        transcendentals=0,
    )


def in_hbm(value):
    return pltpu.with_memory_space_constraint(value, pltpu.HBM)


def block_place():
    index = lax.axis_index("seq")
    return lax.rem(index, XS), lax.div(index, XS)


def conv(block, halo, taps, pad):
    length, width = block.shape
    count = taps.shape[0]
    taps = taps.astype(F32)
    columns = []
    for lane in range(width // DIM):
        lanes = slice(lane * DIM, (lane + 1) * DIM)
        pad[lane, :8] = halo[HALO - 8 :, lanes].astype(F32)
        pad[lane, 8 : 8 + length] = block[:, lanes].astype(F32)
        made = []
        for base in range(0, length, TILE):
            size = min(TILE, length)
            total = jnp.zeros((size, DIM), F32)
            for offset in range(count):
                first = base + 9 - count + offset
                total = total + pad[lane, first : first + size] * taps[offset : offset + 1, lanes]
            made.append(silu(total).astype(BF16))
        columns.append(jnp.concatenate(made, axis=0))
    return jnp.concatenate(columns, axis=1)


def flag(condition):
    return jnp.where(condition, 1.0, 0.0).astype(F32)


def encode(message, states, decays):
    spot = lax.broadcasted_iota(jnp.int32, (8, DIM), 0)
    tail = jnp.zeros((8, DIM), F32)
    for head in range(PAIR):
        state, decay = states[head], decays[head]
        coarse = jnp.floor(decay)
        middle = jnp.floor((decay - coarse) * 1024.0) / 1024.0
        rest = decay - coarse - middle
        most = jnp.max(jnp.max(jnp.abs(state), axis=0, keepdims=True), axis=1, keepdims=True)
        power = jnp.ceil(jnp.log(jnp.maximum(most, 1e-30)))
        message[head * DIM : (head + 1) * DIM] = state * (jnp.exp(-power) * TOP)
        for index, value in enumerate((coarse, middle, rest, power)):
            tail = jnp.where(spot == PAIR * index + head, value, tail)
    message[PAIR * DIM :] = tail


def decode_decay(message):
    tail = message[PAIR * DIM :]
    return tail[:PAIR] + tail[PAIR : 2 * PAIR] + tail[2 * PAIR : 3 * PAIR]


def decode_size(message):
    return jnp.exp(message[PAIR * DIM :][3 * PAIR :]) / TOP


def tails_kernel(mixer, state, out, sems):
    length, width = mixer.shape
    span = pl.ds(length - HALO, HALO)
    copies = [
        pltpu.make_async_copy(mixer.at[span], out.at[:, :width], sems.at[0]),
        pltpu.make_async_copy(state.at[span], out.at[:, width:], sems.at[1]),
    ]
    for copy in copies:
        copy.start()
    for copy in copies:
        copy.wait()


def last_rows(mixer, state):
    return pl.pallas_call(
        tails_kernel,
        in_specs=[HBM, HBM],
        out_specs=VMEM,
        out_shape=pltpu.VMEM((HALO, mixer.shape[1] + state.shape[1]), BF16),
        scratch_shapes=[DMA((2,))],
        compiler_params=params(2),
        name="last_rows",
    )(in_hbm(mixer), in_hbm(state))


def prepare_kernel(
    mixer,
    state,
    taps,
    state_taps,
    step_raw,
    rate,
    inner,
    rows,
    running_out,
    step_out,
    first_rows,
    first_scale,
    last,
    taps_here,
    part0,
    part1,
    part2,
    part3,
    mixer_here,
    state_here,
    raw_here,
    rate_here,
    keys_t,
    scale,
    pad,
    mixer_sem,
    small_sem,
):
    x, _ = block_place()
    heads, length = step_raw.shape
    width = mixer.shape[1]
    wide = PAIR * DIM
    small = [
        pltpu.make_async_copy(source, target, small_sem.at[n])
        for n, (source, target) in enumerate(
            (
                (step_raw, raw_here),
                (rate, rate_here),
                (state, state_here),
                (state_taps, taps_here.at[:, width:]),
                (taps, taps_here.at[:, :width]),
            )
        )
    ]
    for copy in small:
        copy.start()
    pairs = [lax.rem(x + turn, XS) for turn in range(XS)]
    columns = [pl.ds(pl.multiple_of(pair * wide, wide), wide) for pair in pairs]
    large = [
        pltpu.make_async_copy(
            mixer.at[:, columns[turn]], mixer_here.at[turn], mixer_sem.at[turn]
        )
        for turn in range(XS)
    ]
    for copy in large:
        copy.start()

    for copy in small:
        copy.wait()
    raw = raw_here[...]
    step = jnp.maximum(raw, 0.0) + jnp.log1p(jnp.exp(-jnp.abs(raw)))
    spot = lax.broadcasted_iota(jnp.int32, (heads, length), 0)
    rates = jnp.zeros((heads, length), F32)
    for head in range(heads):
        rates = jnp.where(spot == head, rate_here[head], rates)
    running = -rates * step
    lane = lax.broadcasted_iota(jnp.int32, (heads, length), 1)
    shift = 1
    while shift < length:
        moved = pltpu.roll(running, shift, axis=1)
        running = running + jnp.where(lane >= shift, moved, 0.0)
        shift *= 2
    final = running[:, length - 1 :]
    running_out[...] = running
    step_out[...] = step
    scaled = jnp.exp(final - running) * step
    first_scale[...] = scaled[:, :DIM]
    scale[...] = jnp.where(lane < HALO, 0.0, scaled)
    last[...] = jnp.broadcast_to(final, last.shape)
    nothing = jnp.zeros((HALO, wide), BF16)
    first_rows[:, width:] = state_here[:HALO]
    state_rows = conv(state_here[...], nothing, taps_here[:, width:], pad)
    rows[...] = state_rows
    keys_t[...] = state_rows[:, :DIM].astype(F32).T

    for turn, part in enumerate((part0, part1, part2, part3)):
        large[turn].wait()
        first_rows[:, columns[turn]] = mixer_here[turn, :HALO]
        values = conv(mixer_here[turn], nothing, taps_here[:, columns[turn]], pad)
        inner[:, columns[turn]] = values
        for head in range(PAIR):
            row = scale[pl.ds(pairs[turn] * PAIR + head, 1), :]
            scaled_t = (keys_t[...] * row).astype(BF16)
            part[head * DIM : (head + 1) * DIM] = jnp.dot(
                scaled_t, values[:, head * DIM : (head + 1) * DIM], preferred_element_type=F32
            )


def prepare(mixer, state, taps, state_taps, step_raw_t, rate):
    length, width = mixer.shape
    heads = step_raw_t.shape[0]
    every = width + 2 * DIM
    return pl.pallas_call(
        prepare_kernel,
        in_specs=[HBM] * 6,
        out_specs=[VMEM] * (8 + XS),
        out_shape=[
            pltpu.VMEM((length, width), BF16),
            pltpu.VMEM((length, 2 * DIM), BF16),
            pltpu.VMEM((heads, length), F32),
            pltpu.VMEM((heads, length), F32),
            pltpu.VMEM((HALO, every), BF16),
            pltpu.VMEM((heads, DIM), F32),
            pltpu.VMEM((heads, DIM), F32),
            pltpu.VMEM((taps.shape[0], every), BF16),
        ]
        + [pltpu.VMEM((PAIR * DIM, DIM), F32)] * XS,
        scratch_shapes=[
            pltpu.VMEM((XS, length, PAIR * DIM), BF16),
            pltpu.VMEM((length, 2 * DIM), BF16),
            pltpu.VMEM((heads, length), F32),
            pltpu.SMEM((heads,), F32),
            pltpu.VMEM((DIM, length), F32),
            pltpu.VMEM((heads, length), F32),
            pltpu.VMEM((PAIR, length + 8, DIM), F32),
            DMA((XS,)),
            DMA((5,)),
        ],
        compiler_params=params(16),
        cost_estimate=cost(5.7),
        name="prepare",
    )(
        in_hbm(mixer),
        in_hbm(state),
        in_hbm(taps),
        in_hbm(state_taps),
        in_hbm(step_raw_t),
        in_hbm(rate),
    )


def finish_kernel(
    halo,
    first_rows,
    first_scale,
    last,
    taps,
    inner_in,
    rows_in,
    p0,
    p1,
    p2,
    p3,
    inner,
    rows,
    m0,
    m1,
    m2,
    m3,
    pad,
):
    x, _ = block_place()
    width = inner.shape[1]
    heads = width // DIM
    wide = PAIR * DIM
    made = conv(first_rows[:, width:], halo[:, width:], taps[:, width:], pad)
    rows[:HALO] = made
    keys = made[:, :DIM].astype(F32)
    columns = first_scale[...].T
    scaled = [
        (keys * jnp.broadcast_to(columns[:HALO, head : head + 1], (HALO, DIM))).astype(BF16)
        for head in range(heads)
    ]
    added = []
    for pair in range(XS):
        lanes = slice(pair * wide, (pair + 1) * wide)
        values = conv(first_rows[:, lanes], halo[:, lanes], taps[:, lanes], pad)
        inner[:HALO, lanes] = values
        for head in range(PAIR):
            added.append(
                lax.dot_general(
                    scaled[pair * PAIR + head],
                    values[:, head * DIM : (head + 1) * DIM],
                    (((0,), (0,)), ((), ())),
                    preferred_element_type=F32,
                )
            )
    for turn, (part, message) in enumerate(((p0, m0), (p1, m1), (p2, m2), (p3, m3))):
        pair = lax.rem(x + turn, XS)
        states = []
        decays = []
        for head in range(PAIR):
            extra = sum(
                added[other * PAIR + head] * flag(pair == other) for other in range(XS)
            )
            states.append(part[head * DIM : (head + 1) * DIM] + extra)
            decays.append(last[pl.ds(pair * PAIR + head, 1), :])
        encode(message, states, decays)


def finish(halo, first_rows, first_scale, last, taps, inner, rows, parts):
    return pl.pallas_call(
        finish_kernel,
        in_specs=[VMEM] * (7 + XS),
        out_specs=[VMEM] * (2 + XS),
        out_shape=[pltpu.VMEM(inner.shape, BF16), pltpu.VMEM(rows.shape, BF16)]
        + [pltpu.VMEM((MESSAGE, DIM), F32)] * XS,
        scratch_shapes=[pltpu.VMEM((PAIR, HALO + 8, DIM), F32)],
        input_output_aliases={5: 0, 6: 1},
        compiler_params=params(4),
        cost_estimate=cost(0.75),
        name="finish",
    )(halo, first_rows, first_scale, last, taps, inner, rows, *parts)


def shared_kernel(
    rows, running_in, gate, scores, gates, lifted_base, ahead_out, gate_here, gate_sem
):
    length, width = gate.shape
    heads = width // DIM
    tiles = length // TILE
    gate_copy = pltpu.make_async_copy(gate, gate_here, gate_sem)
    gate_copy.start()
    for i in range(tiles):
        wide = (i + 1) * TILE
        scores[i * TILE : wide, :wide] = lax.dot_general(
            rows[i * TILE : wide, DIM:],
            rows[:wide, :DIM],
            (((1,), (1,)), ((), ())),
            preferred_element_type=F32,
        )
    running = running_in[...]
    columns = jnp.exp(running).T
    ahead = jnp.concatenate(
        [
            jnp.exp(running[:, i * WIDE : (i + 1) * WIDE] - running[:, i * WIDE : i * WIDE + 1])
            for i in range(length // WIDE)
        ],
        axis=1,
    ).T
    for i in range(tiles):
        span = slice(i * TILE, (i + 1) * TILE)
        queries = rows[span, DIM:].astype(F32)
        for head in range(heads):
            lanes = slice(head * DIM, (head + 1) * DIM)
            lifted_base[span, lanes] = queries * jnp.broadcast_to(
                columns[span, head : head + 1], (TILE, DIM)
            )
            ahead_out[span, lanes] = jnp.broadcast_to(ahead[span, head : head + 1], (TILE, DIM))
    gate_copy.wait()

    def one_tile(tile, carry):
        span = pl.ds(pl.multiple_of(tile * TILE, TILE), TILE)
        for piece in range(width // DIM):
            lane = slice(piece * DIM, (piece + 1) * DIM)
            gates[span, lane] = silu(gate_here[span, lane].astype(F32))
        return carry

    lax.fori_loop(0, tiles, one_tile, 0)


def shared_part(rows, running, gate):
    length, width = gate.shape
    return pl.pallas_call(
        shared_kernel,
        in_specs=[VMEM, VMEM, HBM],
        out_specs=[VMEM] * 4,
        out_shape=[pltpu.VMEM((length, length), F32)] + [pltpu.VMEM((length, width), F32)] * 3,
        scratch_shapes=[pltpu.VMEM((length, width), BF16), DMA],
        compiler_params=params(8),
        cost_estimate=cost(3.4),
        name="shared_part",
    )(rows, running, in_hbm(gate))


def mix_head(head, table, kinds, inner, running_in, step_in, scores, ahead_in, emit):
    length = inner.shape[0]
    stretch = length // kinds.shape[0]
    each = WIDE // stretch
    row = lax.broadcasted_iota(jnp.int32, (stretch, TILE), 0)
    column = lax.broadcasted_iota(jnp.int32, (stretch, TILE), 1)
    causal = [row + part * stretch >= column for part in range(TILE // stretch)]
    lane = lax.broadcasted_iota(jnp.int32, (1, TILE), 1)
    empty = jnp.zeros((stretch, TILE), BF16)
    lanes = pl.ds(pl.multiple_of(head * DIM, DIM), DIM)
    running = running_in[pl.ds(head, 1), :]
    step = step_in[pl.ds(head, 1), :]
    for i in range(length // WIDE):
        wide = (i + 1) * WIDE
        start = running[:, i * WIDE : i * WIDE + 1]
        behind = jnp.exp(start - running[:, :wide]) * step[:, :wide]
        bands = []
        for part in range(each):
            here = i * each + part
            kind = kinds[here]
            weight = [table[kind, head, level] for level in range(5)]
            band = slice(here * stretch, (here + 1) * stretch)
            ahead = ahead_in[band, lanes]
            pieces = []
            for j in range(wide // TILE):
                first, second = 2 * j, 2 * j + 1
                if first > here:
                    pieces.append(empty)
                    continue
                left = weight[(here ^ first).bit_length()]
                right = weight[(here ^ second).bit_length()]
                if second > here or (here ^ first).bit_length() == (here ^ second).bit_length():
                    factor = left
                else:
                    factor = jnp.where(lane < stretch, left, right)
                tile = slice(j * TILE, (j + 1) * TILE)
                piece = scores[band, tile] * (behind[:, tile] * factor) * ahead
                if second >= here:
                    piece = jnp.where(causal[here - first], piece, 0.0)
                pieces.append(piece.astype(BF16))
            bands.append(jnp.concatenate(pieces, axis=1))
        emit(
            i,
            jnp.dot(
                jnp.concatenate(bands, axis=0), inner[:wide, lanes], preferred_element_type=F32
            ),
        )


def lift(table, kinds, lifted_base, head, tile, levels, held):
    length = lifted_base.shape[0]
    stretch = length // kinds.shape[0]
    lanes = pl.ds(pl.multiple_of(head * DIM, DIM), DIM)
    bands = []
    for here in range(tile * WIDE // stretch, (tile + 1) * WIDE // stretch):
        kind = kinds[here]
        base = lifted_base[here * stretch : (here + 1) * stretch, lanes]
        bands.append(
            jnp.concatenate(
                [(base * table[kind, head, level]).astype(BF16) for level in levels], axis=1
            )
        )
    return jnp.dot(jnp.concatenate(bands, axis=0), held[head], preferred_element_type=F32)


def mix_kernel(first, table, kinds, inner, running_in, step_in, scores, ahead_in, out):
    def one_head(offset, carry):
        lanes = pl.ds(pl.multiple_of(offset * DIM, DIM), DIM)

        def emit(i, value):
            out[i * WIDE : (i + 1) * WIDE, lanes] = value

        mix_head(
            first + offset, table, kinds, inner, running_in, step_in, scores, ahead_in, emit
        )
        return carry

    lax.fori_loop(0, PAIR, one_head, 0)


def mix_part(first, table, kinds, inner, running, step, scores, ahead):
    length, width = inner.shape
    return pl.pallas_call(
        functools.partial(mix_kernel, first),
        in_specs=[SMEM, SMEM] + [VMEM] * 5,
        out_specs=VMEM,
        out_shape=pltpu.VMEM((length, PAIR * DIM), F32),
        compiler_params=params(8),
        cost_estimate=cost(2.4),
        name="mix_part",
    )(table, kinds, inner, running, step, scores, ahead)


def local_kernel(
    done,
    table,
    kinds,
    inner,
    running_in,
    step_in,
    scores,
    ahead_in,
    lifted_base,
    *rest,
):
    mixed = rest[:done]
    nears = rest[done : done + XS]
    out, held = rest[done + XS :]
    x, _ = block_place()
    length, width = inner.shape
    heads = width // DIM
    for k, near in enumerate(nears):
        pair = lax.rem(x + XS - k, XS)
        for head in range(PAIR):
            for level in range(NEAR):
                base = (level * PAIR + head) * DIM
                held[pair * PAIR + head, level * DIM : (level + 1) * DIM] = near[
                    base : base + DIM
                ]
    levels = range(5, 5 + NEAR)
    for group, value in enumerate(mixed):
        for offset in range(PAIR):
            head = group * PAIR + offset
            for tile in range(length // WIDE):
                span = slice(tile * WIDE, (tile + 1) * WIDE)
                out[span, head * DIM : (head + 1) * DIM] = value[
                    span, offset * DIM : (offset + 1) * DIM
                ] + lift(table, kinds, lifted_base, head, tile, levels, held)

    def one_head(head, carry):
        lanes = pl.ds(pl.multiple_of(head * DIM, DIM), DIM)

        def emit(i, value):
            out[i * WIDE : (i + 1) * WIDE, lanes] = value + lift(
                table, kinds, lifted_base, head, i, levels, held
            )

        mix_head(head, table, kinds, inner, running_in, step_in, scores, ahead_in, emit)
        return carry

    lax.fori_loop(len(mixed) * PAIR, heads, one_head, 0, unroll=2)


def local_part(table, kinds, inner, running, step, scores, ahead, lifted_base, mixed, near):
    length, width = inner.shape
    heads = width // DIM
    return pl.pallas_call(
        functools.partial(local_kernel, len(mixed)),
        in_specs=[SMEM, SMEM] + [VMEM] * (6 + len(mixed) + XS),
        out_specs=VMEM,
        out_shape=pltpu.VMEM((length, width), F32),
        scratch_shapes=[pltpu.VMEM((heads, NEAR * DIM, DIM), BF16)],
        compiler_params=params(8),
        cost_estimate=cost(3.8),
        name="local_part",
    )(table, kinds, inner, running, step, scores, ahead, lifted_base, *mixed, *near)


def fold_row_kernel(p0, p1, p2, p3, row_out):
    x, _ = block_place()
    parts = (p0, p1, p2, p3)
    owner = [lax.rem(x + XS - k, XS) for k in range(XS)]
    decays = [decode_decay(part) for part in parts]
    later = [
        jnp.exp(sum(decays[m] * flag(owner[m] > owner[k]) for m in range(XS)))
        * decode_size(parts[k])
        for k in range(XS)
    ]
    total = sum(decays)
    states = []
    for head in range(PAIR):
        span = slice(head * DIM, (head + 1) * DIM)
        states.append(sum(parts[k][span] * later[k][head : head + 1] for k in range(XS)))
    encode(row_out, states, [total[head : head + 1] for head in range(PAIR)])


def fold_row(parts):
    return pl.pallas_call(
        fold_row_kernel,
        in_specs=[VMEM] * XS,
        out_specs=VMEM,
        out_shape=pltpu.VMEM((MESSAGE, DIM), F32),
        compiler_params=params(4),
        cost_estimate=cost(0.25),
        name="fold_row",
    )(*parts)


def fold_near_kernel(p0, p1, p2, p3, row_before, m0, m1, m2, m3):
    x, z = block_place()
    parts = (p0, p1, p2, p3)
    owner = [lax.rem(x + XS - k, XS) for k in range(XS)]
    decays = [decode_decay(part) for part in parts]
    sizes = [decode_size(part) for part in parts]
    odd_size = decode_size(row_before) * flag(lax.rem(z, 2) == 1)

    def pick(values, block):
        return sum(value * flag(owner[k] == block) for k, value in enumerate(values))

    decay_one = jnp.exp(pick(decays, 1))
    decay_two = jnp.exp(pick(decays, 2))
    for head in range(PAIR):
        span = slice(head * DIM, (head + 1) * DIM)
        row = slice(head, head + 1)
        scaled = [parts[k][span] * sizes[k][row] for k in range(XS)]
        first = pick(scaled, 0)
        third = pick(scaled, 2)
        joined = first * decay_one[row] + pick(scaled, 1)
        above = row_before[span]
        for k, message in enumerate((m0, m1, m2, m3)):
            target = lax.rem(x + k, XS)
            before = sum(decays[m][row] * flag(owner[m] < target) for m in range(XS))
            levels = (
                first * flag(target == 1) + third * flag(target == 3),
                joined * (flag(target == 2) + flag(target == 3) * decay_two[row]),
                above * (jnp.exp(before) * odd_size[row]),
            )
            for level, value in enumerate(levels):
                base = (level * PAIR + head) * DIM
                message[base : base + DIM] = value.astype(BF16)


def fold_near(parts, row_before):
    return pl.pallas_call(
        fold_near_kernel,
        in_specs=[VMEM] * (XS + 1),
        out_specs=[VMEM] * XS,
        out_shape=[pltpu.VMEM((NEAR * PAIR * DIM, DIM), BF16)] * XS,
        compiler_params=params(4),
        cost_estimate=cost(0.3),
        name="fold_near",
    )(*parts, row_before)


def fold_two_kernel(span_rows, own, other, out):
    _, z = block_place()
    upper = flag(lax.rem(lax.div(z, span_rows), 2) == 1)
    own_decay = decode_decay(own)
    other_decay = decode_decay(other)
    own_scale = jnp.exp(other_decay * (1.0 - upper)) * decode_size(own)
    other_scale = jnp.exp(own_decay * upper) * decode_size(other)
    decay = own_decay + other_decay
    states = []
    for head in range(PAIR):
        span = slice(head * DIM, (head + 1) * DIM)
        row = slice(head, head + 1)
        states.append(own[span] * own_scale[row] + other[span] * other_scale[row])
    encode(out, states, [decay[head : head + 1] for head in range(PAIR)])


def fold_two(span_rows, own, other):
    return pl.pallas_call(
        functools.partial(fold_two_kernel, span_rows),
        in_specs=[VMEM] * 2,
        out_specs=VMEM,
        out_shape=pltpu.VMEM((MESSAGE, DIM), F32),
        compiler_params=params(4),
        cost_estimate=cost(0.2),
        name="fold_two",
    )(own, other)


def fold_far_kernel(d0, d1, d2, d3, row_before, pair_before, quad_before, m0, m1, m2, m3):
    x, z = block_place()
    odd = flag(lax.rem(z, 2) == 1)
    odd_pair = flag(lax.rem(lax.div(z, 2), 2) == 1)
    upper = flag(z >= ZS // 2)
    decays = [decode_decay(part) for part in (d0, d1, d2, d3)]
    owner = [lax.rem(x + XS - k, XS) for k in range(XS)]
    in_pair = decode_decay(row_before) * odd
    in_quad = in_pair + decode_decay(pair_before) * odd_pair
    levels = (
        (pair_before, in_pair, decode_size(pair_before) * odd_pair),
        (quad_before, in_quad, decode_size(quad_before) * upper),
    )
    for k, message in enumerate((m0, m1, m2, m3)):
        target = lax.rem(x + k, XS)
        before = sum(decays[m] * flag(owner[m] < target) for m in range(XS))
        for level, (state, between, size) in enumerate(levels):
            factor = jnp.exp(before + between) * size
            for head in range(PAIR):
                base = (level * PAIR + head) * DIM
                message[base : base + DIM] = (
                    state[head * DIM : (head + 1) * DIM] * factor[head : head + 1]
                ).astype(BF16)


def fold_far(parts, befores):
    return pl.pallas_call(
        fold_far_kernel,
        in_specs=[VMEM] * (XS + 3),
        out_specs=[VMEM] * XS,
        out_shape=[pltpu.VMEM((FAR * PAIR * DIM, DIM), BF16)] * XS,
        compiler_params=params(4),
        cost_estimate=cost(0.25),
        name="fold_far",
    )(*parts, *befores)


def far_kernel(
    table, kinds, local, gates, lifted_base, f0, f1, f2, f3, gated, squares, held, total
):
    x, _ = block_place()
    length, width = local.shape
    heads = width // DIM
    for k, far in enumerate((f0, f1, f2, f3)):
        pair = lax.rem(x + XS - k, XS)
        for head in range(PAIR):
            for level in range(FAR):
                base = (level * PAIR + head) * DIM
                held[pair * PAIR + head, level * DIM : (level + 1) * DIM] = far[base : base + DIM]
    total[...] = jnp.zeros_like(total)

    levels = range(5 + NEAR, 5 + NEAR + FAR)

    def one_head(head, carry):
        lanes = pl.ds(pl.multiple_of(head * DIM, DIM), DIM)
        for tile in range(length // WIDE):
            span = slice(tile * WIDE, (tile + 1) * WIDE)
            mixed = local[span, lanes] + lift(
                table, kinds, lifted_base, head, tile, levels, held
            )
            value = mixed * gates[span, lanes]
            gated[span, lanes] = value
            total[span] += value * value
        return carry

    lax.fori_loop(0, heads, one_head, 0, unroll=4)
    for tile in range(length // TILE):
        part = total[tile * TILE : (tile + 1) * TILE].T
        squares[tile : tile + 1] = jnp.sum(part, axis=0, keepdims=True)


def far_part(table, kinds, local, gates, lifted_base, far_states):
    length, width = local.shape
    heads = width // DIM
    return pl.pallas_call(
        far_kernel,
        in_specs=[SMEM, SMEM] + [VMEM] * (3 + XS),
        out_specs=[VMEM] * 2,
        out_shape=[pltpu.VMEM((length, width), F32), pltpu.VMEM((length // TILE, TILE), F32)],
        scratch_shapes=[pltpu.VMEM((heads, FAR * DIM, DIM), BF16), pltpu.VMEM((length, DIM), F32)],
        compiler_params=params(8),
        cost_estimate=cost(3.5),
        name="far_part",
    )(table, kinds, local, gates, lifted_base, *far_states)


def norm_kernel(total_width, gated, s0, s1, s2, s3, gain, out, made, sems):
    scale = lax.rsqrt((s0[...] + s1[...] + s2[...] + s3[...]) / total_width + 1e-05)
    length, width = gated.shape
    copies = []
    for tile in range(length // TILE):
        span = slice(tile * TILE, (tile + 1) * TILE)
        column = jnp.broadcast_to(scale[tile : tile + 1], (TILE, TILE)).T
        for piece in range(width // TILE):
            lane = slice(piece * TILE, (piece + 1) * TILE)
            made[span, lane] = (gated[span, lane] * column * gain[:, lane]).astype(BF16)
        copies.append(pltpu.make_async_copy(made.at[span], out.at[span], sems.at[tile]))
        copies[-1].start()
    for copy in copies:
        copy.wait()


def norm(gated, squares, gain, total_width):
    length, width = gated.shape
    return pl.pallas_call(
        functools.partial(norm_kernel, total_width),
        in_specs=[VMEM] * (2 + YS),
        out_specs=HBM,
        out_shape=jax.ShapeDtypeStruct((length, width), BF16),
        scratch_shapes=[pltpu.VMEM((length, width), BF16), DMA((length // TILE,))],
        compiler_params=params(8),
        cost_estimate=cost(1.6),
        name="norm",
    )(gated, *squares, gain)


def local(
    mixer_input,
    state_input,
    gate_input,
    step_raw,
    decay_rate,
    conv_inner,
    conv_state,
    level_table,
    stretch_kind,
    norm_gain,
):
    length, width = mixer_input.shape
    halo = lax.ppermute(
        last_rows(mixer_input, state_input), "seq", [(i, i + 1) for i in range(XS * ZS - 1)]
    )
    inner, rows, running, step, first_rows, first_scale, last, taps, *parts = prepare(
        mixer_input, state_input, conv_inner, conv_state, step_raw.T, decay_rate
    )
    inner, rows, *parts = finish(halo, first_rows, first_scale, last, taps, inner, rows, parts)
    table = jnp.transpose(level_table, (0, 2, 1))
    arrived = [parts[0]] + [
        sent(parts[k], lambda z, x, k=k: (z, (x + k) % XS)) for k in range(1, XS)
    ]
    shared = shared_part(rows, running, gate_input)
    arrived, shared = lax.optimization_barrier((arrived, shared))
    scores, gates, lifted_base, ahead = shared
    mix = functools.partial(
        mix_part,
        table=table,
        kinds=stretch_kind,
        inner=inner,
        running=running,
        step=step,
        scores=scores,
        ahead=ahead,
    )
    row_state = fold_row(arrived)
    row_before = sent(row_state, lambda z, x: (z ^ 1, x))
    row_before, mixed_first = lax.optimization_barrier((row_before, mix(0)))
    pair_state = fold_two(1, row_state, row_before)
    near = fold_near(arrived, row_before)
    pair_before = sent(pair_state, lambda z, x: (z ^ 2, x))
    near = [near[0]] + [along_x(near[k], k) for k in range(1, XS)]
    quad_state = fold_two(2, pair_state, pair_before)
    quad_state, step_late = lax.optimization_barrier((quad_state, step))
    quad_before = sent(quad_state, lambda z, x: (ZS - 1 - z, x) if z < ZS // 2 else None)
    quad_before, mixed_second, mixed_third = lax.optimization_barrier(
        (quad_before, mix(PAIR, step=step_late), mix(2 * PAIR, step=step_late))
    )
    far = fold_far(arrived, (row_before, pair_before, quad_before))
    far = [far[0]] + [along_x(far[k], k) for k in range(1, XS)]
    local_out = local_part(
        table,
        stretch_kind,
        inner,
        running,
        step,
        scores,
        ahead,
        lifted_base,
        (mixed_first, mixed_second, mixed_third),
        near,
    )
    gated, squares = far_part(table, stretch_kind, local_out, gates, lifted_base, far)
    squares = squares + lax.ppermute(squares, "head", head_perm(lambda y, core: (y, 1 - core)))
    sums = [squares] + [
        lax.ppermute(squares, "head", head_perm(lambda y, core, k=k: ((y + k) % YS, core)))
        for k in range(1, YS)
    ]
    total_width = width * lax.axis_size("head")
    return norm(gated, sums, norm_gain[None, :], total_width)


def solution(mesh):
    return jax.shard_map(
        local,
        mesh=mesh,
        in_specs=(
            P("seq", "head"),
            P("seq", None),
            P("seq", "head"),
            P("seq", "head"),
            P("head"),
            P(None, "head"),
            P(),
            P(None, None, "head"),
            P("seq"),
            P("head"),
        ),
        out_specs=P("seq", "head"),
        check_vma=False,
    )
```

```python
import functools
import jax
import jax.numpy as jnp
from jax import lax
from jax.experimental import pallas as pl
from jax.experimental.pallas import tpu as pltpu
from jax.sharding import PartitionSpec as P

F32 = jnp.float32
BF16 = jnp.bfloat16

XS = 4
ZS = 8
YS = 4
CORES = 2
PAIR = 2
DIM = 128
HALO = 16
TILE = 128
WIDE = 256
NEAR = 3
FAR = 2
TOP = 16384.0
MESSAGE = PAIR * DIM + 8


def seq_perm(move):
    pairs = []
    for z in range(ZS):
        for x in range(XS):
            target = move(z, x)
            if target is not None:
                pairs.append((z * XS + x, target[0] * XS + target[1]))
    return pairs


def head_perm(move):
    pairs = []
    for y in range(YS):
        for core in range(CORES):
            target = move(y, core)
            pairs.append((y * CORES + core, target[0] * CORES + target[1]))
    return pairs


def along_x(value, step):
    return lax.ppermute(value, "seq", seq_perm(lambda z, x: (z, (x + step) % XS)))


def sent(message, move):
    return lax.ppermute(message.astype(jnp.float16), "seq", seq_perm(move)).astype(F32)


def silu_of_twice(half):
    return half + half * jnp.tanh(half)


def silu(value):
    return silu_of_twice(0.5 * value)


VMEM = pl.BlockSpec(memory_space=pltpu.VMEM)
SMEM = pl.BlockSpec(memory_space=pltpu.SMEM)
HBM = pl.BlockSpec(memory_space=pltpu.HBM)
DMA = pltpu.SemaphoreType.DMA


def params(mebibytes):
    return pltpu.CompilerParams(vmem_limit_bytes=mebibytes * 2**20)


def cost(microseconds):
    return pl.CostEstimate(
        flops=int(microseconds * 1.15e9),
        bytes_accessed=int(microseconds * 3.6e6),
        transcendentals=0,
    )


def in_hbm(value):
    return pltpu.with_memory_space_constraint(value, pltpu.HBM)


def block_place():
    index = lax.axis_index("seq")
    return lax.rem(index, XS), lax.div(index, XS)


def conv(block, halo, taps, pad):
    length, width = block.shape
    count = taps.shape[0]
    taps = 0.5 * taps.astype(F32)
    columns = []
    for lane in range(width // DIM):
        lanes = slice(lane * DIM, (lane + 1) * DIM)
        pad[lane, :8] = halo[HALO - 8 :, lanes].astype(F32)
        pad[lane, 8 : 8 + length] = block[:, lanes].astype(F32)
        made = []
        for base in range(0, length, TILE):
            size = min(TILE, length)
            total = jnp.zeros((size, DIM), F32)
            for offset in range(count):
                first = base + 9 - count + offset
                total = total + pad[lane, first : first + size] * taps[offset : offset + 1, lanes]
            made.append(silu_of_twice(total).astype(BF16))
        columns.append(jnp.concatenate(made, axis=0))
    return jnp.concatenate(columns, axis=1)


def flag(condition):
    return jnp.where(condition, 1.0, 0.0).astype(F32)


def encode(message, states, decays):
    spot = lax.broadcasted_iota(jnp.int32, (8, DIM), 0)
    tail = jnp.zeros((8, DIM), F32)
    for head in range(PAIR):
        state, decay = states[head], decays[head]
        coarse = jnp.floor(decay)
        middle = jnp.floor((decay - coarse) * 1024.0) / 1024.0
        rest = decay - coarse - middle
        most = jnp.max(jnp.max(jnp.abs(state), axis=0, keepdims=True), axis=1, keepdims=True)
        power = jnp.ceil(jnp.log(jnp.maximum(most, 1e-30)))
        message[head * DIM : (head + 1) * DIM] = state * (jnp.exp(-power) * TOP)
        for index, value in enumerate((coarse, middle, rest, power)):
            tail = jnp.where(spot == PAIR * index + head, value, tail)
    message[PAIR * DIM :] = tail


def decode_decay(message):
    tail = message[PAIR * DIM :]
    return tail[:PAIR] + tail[PAIR : 2 * PAIR] + tail[2 * PAIR : 3 * PAIR]


def decode_size(message):
    return jnp.exp(message[PAIR * DIM :][3 * PAIR :]) / TOP


def tails_kernel(mixer, state, out, sems):
    length, width = mixer.shape
    span = pl.ds(length - HALO, HALO)
    copies = [
        pltpu.make_async_copy(mixer.at[span], out.at[:, :width], sems.at[0]),
        pltpu.make_async_copy(state.at[span], out.at[:, width:], sems.at[1]),
    ]
    for copy in copies:
        copy.start()
    for copy in copies:
        copy.wait()


def last_rows(mixer, state):
    return pl.pallas_call(
        tails_kernel,
        in_specs=[HBM, HBM],
        out_specs=VMEM,
        out_shape=pltpu.VMEM((HALO, mixer.shape[1] + state.shape[1]), BF16),
        scratch_shapes=[DMA((2,))],
        compiler_params=params(2),
        name="last_rows",
    )(in_hbm(mixer), in_hbm(state))


def prepare_kernel(
    mixer,
    state,
    taps,
    state_taps,
    step_raw,
    rate,
    inner,
    rows,
    running_out,
    step_out,
    first_rows,
    first_scale,
    last,
    taps_here,
    part0,
    part1,
    part2,
    part3,
    mixer_here,
    state_here,
    raw_here,
    rate_here,
    keys_t,
    scale,
    pad,
    mixer_sem,
    small_sem,
):
    x, _ = block_place()
    heads, length = step_raw.shape
    width = mixer.shape[1]
    wide = PAIR * DIM
    small = [
        pltpu.make_async_copy(source, target, small_sem.at[n])
        for n, (source, target) in enumerate(
            (
                (step_raw, raw_here),
                (rate, rate_here),
                (state, state_here),
                (state_taps, taps_here.at[:, width:]),
                (taps, taps_here.at[:, :width]),
            )
        )
    ]
    for copy in small:
        copy.start()
    pairs = [lax.rem(x + turn, XS) for turn in range(XS)]
    columns = [pl.ds(pl.multiple_of(pair * wide, wide), wide) for pair in pairs]
    large = [
        pltpu.make_async_copy(
            mixer.at[:, columns[turn]], mixer_here.at[turn], mixer_sem.at[turn]
        )
        for turn in range(XS)
    ]
    for copy in large:
        copy.start()

    for copy in small:
        copy.wait()
    raw = raw_here[...]
    step = jnp.maximum(raw, 0.0) + jnp.log1p(jnp.exp(-jnp.abs(raw)))
    spot = lax.broadcasted_iota(jnp.int32, (heads, length), 0)
    rates = jnp.zeros((heads, length), F32)
    for head in range(heads):
        rates = jnp.where(spot == head, rate_here[head], rates)
    running = -rates * step
    lane = lax.broadcasted_iota(jnp.int32, (heads, length), 1)
    shift = 1
    while shift < length:
        moved = pltpu.roll(running, shift, axis=1)
        running = running + jnp.where(lane >= shift, moved, 0.0)
        shift *= 2
    final = running[:, length - 1 :]
    running_out[...] = running
    step_out[...] = step
    scaled = jnp.exp(final - running) * step
    first_scale[...] = scaled[:, :DIM]
    scale[...] = jnp.where(lane < HALO, 0.0, scaled)
    last[...] = jnp.broadcast_to(final, last.shape)
    nothing = jnp.zeros((HALO, wide), BF16)
    first_rows[:, width:] = state_here[:HALO]
    state_rows = conv(state_here[...], nothing, taps_here[:, width:], pad)
    rows[...] = state_rows
    keys_t[...] = state_rows[:, :DIM].astype(F32).T

    for turn, part in enumerate((part0, part1, part2, part3)):
        large[turn].wait()
        first_rows[:, columns[turn]] = mixer_here[turn, :HALO]
        values = conv(mixer_here[turn], nothing, taps_here[:, columns[turn]], pad)
        inner[:, columns[turn]] = values
        for head in range(PAIR):
            row = scale[pl.ds(pairs[turn] * PAIR + head, 1), :]
            scaled_t = (keys_t[...] * row).astype(BF16)
            part[head * DIM : (head + 1) * DIM] = jnp.dot(
                scaled_t, values[:, head * DIM : (head + 1) * DIM], preferred_element_type=F32
            )


def prepare(mixer, state, taps, state_taps, step_raw_t, rate):
    length, width = mixer.shape
    heads = step_raw_t.shape[0]
    every = width + 2 * DIM
    return pl.pallas_call(
        prepare_kernel,
        in_specs=[HBM] * 6,
        out_specs=[VMEM] * (8 + XS),
        out_shape=[
            pltpu.VMEM((length, width), BF16),
            pltpu.VMEM((length, 2 * DIM), BF16),
            pltpu.VMEM((heads, length), F32),
            pltpu.VMEM((heads, length), F32),
            pltpu.VMEM((HALO, every), BF16),
            pltpu.VMEM((heads, DIM), F32),
            pltpu.VMEM((heads, DIM), F32),
            pltpu.VMEM((taps.shape[0], every), BF16),
        ]
        + [pltpu.VMEM((PAIR * DIM, DIM), F32)] * XS,
        scratch_shapes=[
            pltpu.VMEM((XS, length, PAIR * DIM), BF16),
            pltpu.VMEM((length, 2 * DIM), BF16),
            pltpu.VMEM((heads, length), F32),
            pltpu.SMEM((heads,), F32),
            pltpu.VMEM((DIM, length), F32),
            pltpu.VMEM((heads, length), F32),
            pltpu.VMEM((PAIR, length + 8, DIM), F32),
            DMA((XS,)),
            DMA((5,)),
        ],
        compiler_params=params(16),
        cost_estimate=cost(5.7),
        name="prepare",
    )(
        in_hbm(mixer),
        in_hbm(state),
        in_hbm(taps),
        in_hbm(state_taps),
        in_hbm(step_raw_t),
        in_hbm(rate),
    )


def finish_kernel(
    halo,
    first_rows,
    first_scale,
    last,
    taps,
    inner_in,
    rows_in,
    p0,
    p1,
    p2,
    p3,
    inner,
    rows,
    m0,
    m1,
    m2,
    m3,
    pad,
):
    x, _ = block_place()
    width = inner.shape[1]
    heads = width // DIM
    wide = PAIR * DIM
    made = conv(first_rows[:, width:], halo[:, width:], taps[:, width:], pad)
    rows[:HALO] = made
    keys = made[:, :DIM].astype(F32)
    columns = first_scale[...].T
    scaled = [
        (keys * jnp.broadcast_to(columns[:HALO, head : head + 1], (HALO, DIM))).astype(BF16)
        for head in range(heads)
    ]
    added = []
    for pair in range(XS):
        lanes = slice(pair * wide, (pair + 1) * wide)
        values = conv(first_rows[:, lanes], halo[:, lanes], taps[:, lanes], pad)
        inner[:HALO, lanes] = values
        for head in range(PAIR):
            added.append(
                lax.dot_general(
                    scaled[pair * PAIR + head],
                    values[:, head * DIM : (head + 1) * DIM],
                    (((0,), (0,)), ((), ())),
                    preferred_element_type=F32,
                )
            )
    for turn, (part, message) in enumerate(((p0, m0), (p1, m1), (p2, m2), (p3, m3))):
        pair = lax.rem(x + turn, XS)
        states = []
        decays = []
        for head in range(PAIR):
            extra = sum(
                added[other * PAIR + head] * flag(pair == other) for other in range(XS)
            )
            states.append(part[head * DIM : (head + 1) * DIM] + extra)
            decays.append(last[pl.ds(pair * PAIR + head, 1), :])
        encode(message, states, decays)


def finish(halo, first_rows, first_scale, last, taps, inner, rows, parts):
    return pl.pallas_call(
        finish_kernel,
        in_specs=[VMEM] * (7 + XS),
        out_specs=[VMEM] * (2 + XS),
        out_shape=[pltpu.VMEM(inner.shape, BF16), pltpu.VMEM(rows.shape, BF16)]
        + [pltpu.VMEM((MESSAGE, DIM), F32)] * XS,
        scratch_shapes=[pltpu.VMEM((PAIR, HALO + 8, DIM), F32)],
        input_output_aliases={5: 0, 6: 1},
        compiler_params=params(4),
        cost_estimate=cost(0.75),
        name="finish",
    )(halo, first_rows, first_scale, last, taps, inner, rows, *parts)


def shared_kernel(
    rows, running_in, gate, scores, gates, lifted_base, ahead_out, gate_here, gate_sem
):
    length, width = gate.shape
    heads = width // DIM
    tiles = length // TILE
    gate_copy = pltpu.make_async_copy(gate, gate_here, gate_sem)
    gate_copy.start()
    for i in range(tiles):
        wide = (i + 1) * TILE
        scores[i * TILE : wide, :wide] = lax.dot_general(
            rows[i * TILE : wide, DIM:],
            rows[:wide, :DIM],
            (((1,), (1,)), ((), ())),
            preferred_element_type=F32,
        )
    running = running_in[...]
    columns = jnp.exp(running).T
    ahead = jnp.concatenate(
        [
            jnp.exp(running[:, i * WIDE : (i + 1) * WIDE] - running[:, i * WIDE : i * WIDE + 1])
            for i in range(length // WIDE)
        ],
        axis=1,
    ).T
    for i in range(tiles):
        span = slice(i * TILE, (i + 1) * TILE)
        queries = rows[span, DIM:].astype(F32)
        for head in range(heads):
            lanes = slice(head * DIM, (head + 1) * DIM)
            lifted_base[span, lanes] = queries * jnp.broadcast_to(
                columns[span, head : head + 1], (TILE, DIM)
            )
            ahead_out[span, lanes] = jnp.broadcast_to(ahead[span, head : head + 1], (TILE, DIM))
    gate_copy.wait()

    def one_tile(tile, carry):
        span = pl.ds(pl.multiple_of(tile * TILE, TILE), TILE)
        for piece in range(width // DIM):
            lane = slice(piece * DIM, (piece + 1) * DIM)
            gates[span, lane] = silu(gate_here[span, lane].astype(F32))
        return carry

    lax.fori_loop(0, tiles, one_tile, 0)


def shared_part(rows, running, gate):
    length, width = gate.shape
    return pl.pallas_call(
        shared_kernel,
        in_specs=[VMEM, VMEM, HBM],
        out_specs=[VMEM] * 4,
        out_shape=[pltpu.VMEM((length, length), F32)] + [pltpu.VMEM((length, width), F32)] * 3,
        scratch_shapes=[pltpu.VMEM((length, width), BF16), DMA],
        compiler_params=params(8),
        cost_estimate=cost(3.4),
        name="shared_part",
    )(rows, running, in_hbm(gate))


def mix_head(head, table, kinds, inner, running_in, step_in, scores, ahead_in, emit):
    length = inner.shape[0]
    stretch = length // kinds.shape[0]
    each = WIDE // stretch
    row = lax.broadcasted_iota(jnp.int32, (stretch, TILE), 0)
    column = lax.broadcasted_iota(jnp.int32, (stretch, TILE), 1)
    causal = [row + part * stretch >= column for part in range(TILE // stretch)]
    lane = lax.broadcasted_iota(jnp.int32, (1, TILE), 1)
    empty = jnp.zeros((stretch, TILE), BF16)
    lanes = pl.ds(pl.multiple_of(head * DIM, DIM), DIM)
    running = running_in[pl.ds(head, 1), :]
    step = step_in[pl.ds(head, 1), :]
    for i in range(length // WIDE):
        wide = (i + 1) * WIDE
        start = running[:, i * WIDE : i * WIDE + 1]
        behind = jnp.exp(start - running[:, :wide]) * step[:, :wide]
        bands = []
        for part in range(each):
            here = i * each + part
            kind = kinds[here]
            weight = [table[kind, head, level] for level in range(5)]
            band = slice(here * stretch, (here + 1) * stretch)
            ahead = ahead_in[band, lanes]
            pieces = []
            for j in range(wide // TILE):
                first, second = 2 * j, 2 * j + 1
                if first > here:
                    pieces.append(empty)
                    continue
                left = weight[(here ^ first).bit_length()]
                right = weight[(here ^ second).bit_length()]
                if second > here or (here ^ first).bit_length() == (here ^ second).bit_length():
                    factor = left
                else:
                    factor = jnp.where(lane < stretch, left, right)
                tile = slice(j * TILE, (j + 1) * TILE)
                piece = scores[band, tile] * (behind[:, tile] * factor) * ahead
                if second >= here:
                    piece = jnp.where(causal[here - first], piece, 0.0)
                pieces.append(piece.astype(BF16))
            bands.append(jnp.concatenate(pieces, axis=1))
        emit(
            i,
            jnp.dot(
                jnp.concatenate(bands, axis=0), inner[:wide, lanes], preferred_element_type=F32
            ),
        )


def lift(table, kinds, lifted_base, head, tile, levels, held, WIDE=WIDE):
    length = lifted_base.shape[0]
    stretch = length // kinds.shape[0]
    lanes = pl.ds(pl.multiple_of(head * DIM, DIM), DIM)
    bands = []
    for here in range(tile * WIDE // stretch, (tile + 1) * WIDE // stretch):
        kind = kinds[here]
        base = lifted_base[here * stretch : (here + 1) * stretch, lanes]
        bands.append(
            jnp.concatenate(
                [(base * table[kind, head, level]).astype(BF16) for level in levels], axis=1
            )
        )
    return jnp.dot(jnp.concatenate(bands, axis=0), held[head], preferred_element_type=F32)


def mix_kernel(first, count, table, kinds, inner, running_in, step_in, scores, ahead_in, out):
    def one_head(offset, carry):
        lanes = pl.ds(pl.multiple_of(offset * DIM, DIM), DIM)

        def emit(i, value):
            out[i * WIDE : (i + 1) * WIDE, lanes] = value

        mix_head(
            first + offset, table, kinds, inner, running_in, step_in, scores, ahead_in, emit
        )
        return carry

    lax.fori_loop(0, count, one_head, 0, unroll=True)


def mix_part(first, count, table, kinds, inner, running, step, scores, ahead):
    length, width = inner.shape
    return pl.pallas_call(
        functools.partial(mix_kernel, first, count),
        in_specs=[SMEM, SMEM] + [VMEM] * 5,
        out_specs=VMEM,
        out_shape=pltpu.VMEM((length, count * DIM), F32),
        compiler_params=params(8),
        cost_estimate=cost(0.75 * count + 0.5),
        name="mix_part",
    )(table, kinds, inner, running, step, scores, ahead)


def local_kernel(
    done,
    table,
    kinds,
    inner,
    running_in,
    step_in,
    scores,
    ahead_in,
    lifted_base,
    *rest,
):
    mixed = rest[:done]
    nears = rest[done : done + XS]
    out, held = rest[done + XS :]
    x, _ = block_place()
    length, width = inner.shape
    heads = width // DIM
    for k, near in enumerate(nears):
        pair = lax.rem(x + XS - k, XS)
        for head in range(PAIR):
            for level in range(NEAR):
                base = (level * PAIR + head) * DIM
                held[pair * PAIR + head, level * DIM : (level + 1) * DIM] = near[
                    base : base + DIM
                ]
    levels = range(5, 5 + NEAR)
    head = 0
    for value in mixed:
        for offset in range(value.shape[1] // DIM):
            for tile in range(length // WIDE):
                span = slice(tile * WIDE, (tile + 1) * WIDE)
                out[span, head * DIM : (head + 1) * DIM] = value[
                    span, offset * DIM : (offset + 1) * DIM
                ] + lift(table, kinds, lifted_base, head, tile, levels, held)
            head += 1

    def one_head(head, carry):
        lanes = pl.ds(pl.multiple_of(head * DIM, DIM), DIM)

        def emit(i, value):
            out[i * WIDE : (i + 1) * WIDE, lanes] = value + lift(
                table, kinds, lifted_base, head, i, levels, held
            )

        mix_head(head, table, kinds, inner, running_in, step_in, scores, ahead_in, emit)
        return carry

    lax.fori_loop(head, heads, one_head, 0, unroll=2)


def local_part(table, kinds, inner, running, step, scores, ahead, lifted_base, mixed, near):
    length, width = inner.shape
    heads = width // DIM
    return pl.pallas_call(
        functools.partial(local_kernel, len(mixed)),
        in_specs=[SMEM, SMEM] + [VMEM] * (6 + len(mixed) + XS),
        out_specs=VMEM,
        out_shape=pltpu.VMEM((length, width), F32),
        scratch_shapes=[pltpu.VMEM((heads, NEAR * DIM, DIM), BF16)],
        compiler_params=params(8),
        cost_estimate=cost(3.8),
        name="local_part",
    )(table, kinds, inner, running, step, scores, ahead, lifted_base, *mixed, *near)


def fold_row_kernel(p0, p1, p2, p3, row_out):
    x, _ = block_place()
    parts = (p0, p1, p2, p3)
    owner = [lax.rem(x + XS - k, XS) for k in range(XS)]
    decays = [decode_decay(part) for part in parts]
    later = [
        jnp.exp(sum(decays[m] * flag(owner[m] > owner[k]) for m in range(XS)))
        * decode_size(parts[k])
        for k in range(XS)
    ]
    total = sum(decays)
    states = []
    for head in range(PAIR):
        span = slice(head * DIM, (head + 1) * DIM)
        states.append(sum(parts[k][span] * later[k][head : head + 1] for k in range(XS)))
    encode(row_out, states, [total[head : head + 1] for head in range(PAIR)])


def fold_row(parts):
    return pl.pallas_call(
        fold_row_kernel,
        in_specs=[VMEM] * XS,
        out_specs=VMEM,
        out_shape=pltpu.VMEM((MESSAGE, DIM), F32),
        compiler_params=params(4),
        cost_estimate=cost(0.25),
        name="fold_row",
    )(*parts)


def fold_near_kernel(p0, p1, p2, p3, row_before, m0, m1, m2, m3):
    x, z = block_place()
    parts = (p0, p1, p2, p3)
    owner = [lax.rem(x + XS - k, XS) for k in range(XS)]
    decays = [decode_decay(part) for part in parts]
    sizes = [decode_size(part) for part in parts]
    odd_size = decode_size(row_before) * flag(lax.rem(z, 2) == 1)

    def pick(values, block):
        return sum(value * flag(owner[k] == block) for k, value in enumerate(values))

    decay_one = jnp.exp(pick(decays, 1))
    decay_two = jnp.exp(pick(decays, 2))
    for head in range(PAIR):
        span = slice(head * DIM, (head + 1) * DIM)
        row = slice(head, head + 1)
        scaled = [parts[k][span] * sizes[k][row] for k in range(XS)]
        first = pick(scaled, 0)
        third = pick(scaled, 2)
        joined = first * decay_one[row] + pick(scaled, 1)
        above = row_before[span]
        for k, message in enumerate((m0, m1, m2, m3)):
            target = lax.rem(x + k, XS)
            before = sum(decays[m][row] * flag(owner[m] < target) for m in range(XS))
            levels = (
                first * flag(target == 1) + third * flag(target == 3),
                joined * (flag(target == 2) + flag(target == 3) * decay_two[row]),
                above * (jnp.exp(before) * odd_size[row]),
            )
            for level, value in enumerate(levels):
                base = (level * PAIR + head) * DIM
                message[base : base + DIM] = value.astype(BF16)


def fold_near(parts, row_before):
    return pl.pallas_call(
        fold_near_kernel,
        in_specs=[VMEM] * (XS + 1),
        out_specs=[VMEM] * XS,
        out_shape=[pltpu.VMEM((NEAR * PAIR * DIM, DIM), BF16)] * XS,
        compiler_params=params(4),
        cost_estimate=cost(0.3),
        name="fold_near",
    )(*parts, row_before)


def fold_two_kernel(span_rows, own, other, out):
    _, z = block_place()
    upper = flag(lax.rem(lax.div(z, span_rows), 2) == 1)
    own_decay = decode_decay(own)
    other_decay = decode_decay(other)
    own_scale = jnp.exp(other_decay * (1.0 - upper)) * decode_size(own)
    other_scale = jnp.exp(own_decay * upper) * decode_size(other)
    decay = own_decay + other_decay
    states = []
    for head in range(PAIR):
        span = slice(head * DIM, (head + 1) * DIM)
        row = slice(head, head + 1)
        states.append(own[span] * own_scale[row] + other[span] * other_scale[row])
    encode(out, states, [decay[head : head + 1] for head in range(PAIR)])


def fold_two(span_rows, own, other):
    return pl.pallas_call(
        functools.partial(fold_two_kernel, span_rows),
        in_specs=[VMEM] * 2,
        out_specs=VMEM,
        out_shape=pltpu.VMEM((MESSAGE, DIM), F32),
        compiler_params=params(4),
        cost_estimate=cost(0.2),
        name="fold_two",
    )(own, other)


def fold_far_kernel(d0, d1, d2, d3, row_before, pair_before, quad_before, m0, m1, m2, m3):
    x, z = block_place()
    odd = flag(lax.rem(z, 2) == 1)
    odd_pair = flag(lax.rem(lax.div(z, 2), 2) == 1)
    upper = flag(z >= ZS // 2)
    decays = [decode_decay(part) for part in (d0, d1, d2, d3)]
    owner = [lax.rem(x + XS - k, XS) for k in range(XS)]
    in_pair = decode_decay(row_before) * odd
    in_quad = in_pair + decode_decay(pair_before) * odd_pair
    levels = (
        (pair_before, in_pair, decode_size(pair_before) * odd_pair),
        (quad_before, in_quad, decode_size(quad_before) * upper),
    )
    for k, message in enumerate((m0, m1, m2, m3)):
        target = lax.rem(x + k, XS)
        before = sum(decays[m] * flag(owner[m] < target) for m in range(XS))
        for level, (state, between, size) in enumerate(levels):
            factor = jnp.exp(before + between) * size
            for head in range(PAIR):
                base = (level * PAIR + head) * DIM
                message[base : base + DIM] = (
                    state[head * DIM : (head + 1) * DIM] * factor[head : head + 1]
                ).astype(BF16)


def fold_far(parts, befores):
    return pl.pallas_call(
        fold_far_kernel,
        in_specs=[VMEM] * (XS + 3),
        out_specs=[VMEM] * XS,
        out_shape=[pltpu.VMEM((FAR * PAIR * DIM, DIM), BF16)] * XS,
        compiler_params=params(4),
        cost_estimate=cost(0.25),
        name="fold_far",
    )(*parts, *befores)


def far_kernel(
    table, kinds, local, gates, lifted_base, f0, f1, f2, f3, gated, squares, held, total
):
    x, _ = block_place()
    length, width = local.shape
    heads = width // DIM
    for k, far in enumerate((f0, f1, f2, f3)):
        pair = lax.rem(x + XS - k, XS)
        for head in range(PAIR):
            for level in range(FAR):
                base = (level * PAIR + head) * DIM
                held[pair * PAIR + head, level * DIM : (level + 1) * DIM] = far[base : base + DIM]
    levels = range(5 + NEAR, 5 + NEAR + FAR)
    for pair in range(heads // 2):
        values = []
        for head in (2 * pair, 2 * pair + 1):
            lanes = slice(head * DIM, (head + 1) * DIM)
            mixed = local[:, lanes] + lift(
                table, kinds, lifted_base, head, 0, levels, held, length
            )
            value = mixed * gates[:, lanes]
            gated[:, lanes] = value
            values.append(value * value)
        if pair == 0:
            total[...] = values[0] + values[1]
        else:
            total[...] += values[0] + values[1]
    for tile in range(length // TILE):
        part = total[tile * TILE : (tile + 1) * TILE].T
        squares[tile : tile + 1] = jnp.sum(part, axis=0, keepdims=True)


def far_part(table, kinds, local, gates, lifted_base, far_states):
    length, width = local.shape
    heads = width // DIM
    return pl.pallas_call(
        far_kernel,
        in_specs=[SMEM, SMEM] + [VMEM] * (3 + XS),
        out_specs=[VMEM] * 2,
        out_shape=[pltpu.VMEM((length, width), F32), pltpu.VMEM((length // TILE, TILE), F32)],
        scratch_shapes=[pltpu.VMEM((heads, FAR * DIM, DIM), BF16), pltpu.VMEM((length, DIM), F32)],
        compiler_params=params(8),
        cost_estimate=cost(3.5),
        name="far_part",
    )(table, kinds, local, gates, lifted_base, *far_states)


def norm_kernel(total_width, gated, s0, s1, s2, s3, gain, out, made, sems):
    scale = lax.rsqrt((s0[...] + s1[...] + s2[...] + s3[...]) / total_width + 1e-05)
    length, width = gated.shape
    copies = []
    for tile in range(length // TILE):
        span = slice(tile * TILE, (tile + 1) * TILE)
        column = jnp.broadcast_to(scale[tile : tile + 1], (TILE, TILE)).T
        for piece in range(width // TILE):
            lane = slice(piece * TILE, (piece + 1) * TILE)
            made[span, lane] = (gated[span, lane] * column * gain[:, lane]).astype(BF16)
        copies.append(pltpu.make_async_copy(made.at[span], out.at[span], sems.at[tile]))
        copies[-1].start()
    for copy in copies:
        copy.wait()


def norm(gated, squares, gain, total_width):
    length, width = gated.shape
    return pl.pallas_call(
        functools.partial(norm_kernel, total_width),
        in_specs=[VMEM] * (2 + YS),
        out_specs=HBM,
        out_shape=jax.ShapeDtypeStruct((length, width), BF16),
        scratch_shapes=[pltpu.VMEM((length, width), BF16), DMA((length // TILE,))],
        compiler_params=params(8),
        cost_estimate=cost(1.6),
        name="norm",
    )(gated, *squares, gain)


def local(
    mixer_input,
    state_input,
    gate_input,
    step_raw,
    decay_rate,
    conv_inner,
    conv_state,
    level_table,
    stretch_kind,
    norm_gain,
):
    length, width = mixer_input.shape
    halo = lax.ppermute(
        last_rows(mixer_input, state_input), "seq", [(i, i + 1) for i in range(XS * ZS - 1)]
    )
    inner, rows, running, step, first_rows, first_scale, last, taps, *parts = prepare(
        mixer_input, state_input, conv_inner, conv_state, step_raw.T, decay_rate
    )
    inner, rows, *parts = finish(halo, first_rows, first_scale, last, taps, inner, rows, parts)
    table = jnp.transpose(level_table, (0, 2, 1))
    arrived = [parts[0]] + [
        sent(parts[k], lambda z, x, k=k: (z, (x + k) % XS)) for k in range(1, XS)
    ]
    shared = shared_part(rows, running, gate_input)
    arrived, shared = lax.optimization_barrier((arrived, shared))
    scores, gates, lifted_base, ahead = shared
    mix = functools.partial(
        mix_part,
        table=table,
        kinds=stretch_kind,
        inner=inner,
        running=running,
        step=step,
        scores=scores,
        ahead=ahead,
    )
    row_state = fold_row(arrived)
    row_before = sent(row_state, lambda z, x: (z ^ 1, x))
    row_before, mixed_first = lax.optimization_barrier((row_before, mix(0, PAIR)))
    pair_state = fold_two(1, row_state, row_before)
    near = fold_near(arrived, row_before)
    pair_before = sent(pair_state, lambda z, x: (z ^ 2, x))
    near = [near[0]] + [along_x(near[k], k) for k in range(1, XS)]
    quad_state = fold_two(2, pair_state, pair_before)
    quad_state, step_late = lax.optimization_barrier((quad_state, step))
    quad_before = sent(quad_state, lambda z, x: (ZS - 1 - z, x) if z < ZS // 2 else None)
    quad_before, mixed_second = lax.optimization_barrier(
        (quad_before, mix(PAIR, 2 * PAIR, step=step_late))
    )
    far = fold_far(arrived, (row_before, pair_before, quad_before))
    far = [far[0]] + [along_x(far[k], k) for k in range(1, XS)]
    local_out = local_part(
        table,
        stretch_kind,
        inner,
        running,
        step,
        scores,
        ahead,
        lifted_base,
        (mixed_first, mixed_second),
        near,
    )
    gated, squares = far_part(table, stretch_kind, local_out, gates, lifted_base, far)
    squares = squares + lax.ppermute(squares, "head", head_perm(lambda y, core: (y, 1 - core)))
    sums = [squares] + [
        lax.ppermute(squares, "head", head_perm(lambda y, core, k=k: ((y + k) % YS, core)))
        for k in range(1, YS)
    ]
    total_width = width * lax.axis_size("head")
    return norm(gated, sums, norm_gain[None, :], total_width)


def solution(mesh):
    return jax.shard_map(
        local,
        mesh=mesh,
        in_specs=(
            P("seq", "head"),
            P("seq", None),
            P("seq", "head"),
            P("seq", "head"),
            P("head"),
            P(None, "head"),
            P(),
            P(None, None, "head"),
            P("seq"),
            P("head"),
        ),
        out_specs=P("seq", "head"),
        check_vma=False,
    )
```

```python
import functools
import jax
import jax.numpy as jnp
from jax import lax
from jax.experimental import pallas as pl
from jax.experimental.pallas import tpu as pltpu
from jax.sharding import PartitionSpec as P

F32 = jnp.float32
BF16 = jnp.bfloat16

XS = 4
ZS = 8
YS = 4
CORES = 2
PAIR = 2
DIM = 128
HALO = 16
TILE = 128
WIDE = 256
NEAR = 3
FAR = 2
TOP = 16384.0
MESSAGE = PAIR * DIM + 8


def seq_perm(move):
    pairs = []
    for z in range(ZS):
        for x in range(XS):
            target = move(z, x)
            if target is not None:
                pairs.append((z * XS + x, target[0] * XS + target[1]))
    return pairs


def head_perm(move):
    pairs = []
    for y in range(YS):
        for core in range(CORES):
            target = move(y, core)
            pairs.append((y * CORES + core, target[0] * CORES + target[1]))
    return pairs


def along_x(value, step):
    return lax.ppermute(value, "seq", seq_perm(lambda z, x: (z, (x + step) % XS)))


def sent(message, move):
    return lax.ppermute(message.astype(jnp.float16), "seq", seq_perm(move)).astype(F32)


def silu_of_twice(half):
    return half + half * jnp.tanh(half)


def silu(value):
    return silu_of_twice(0.5 * value)


VMEM = pl.BlockSpec(memory_space=pltpu.VMEM)
SMEM = pl.BlockSpec(memory_space=pltpu.SMEM)
HBM = pl.BlockSpec(memory_space=pltpu.HBM)
DMA = pltpu.SemaphoreType.DMA


def params(mebibytes):
    return pltpu.CompilerParams(vmem_limit_bytes=mebibytes * 2**20)


def cost(microseconds):
    return pl.CostEstimate(
        flops=int(microseconds * 1.15e9),
        bytes_accessed=int(microseconds * 3.6e6),
        transcendentals=0,
    )


def in_hbm(value):
    return pltpu.with_memory_space_constraint(value, pltpu.HBM)


def block_place():
    index = lax.axis_index("seq")
    return lax.rem(index, XS), lax.div(index, XS)


def conv(block, halo, taps, pad):
    length, width = block.shape
    count = taps.shape[0]
    taps = 0.5 * taps.astype(F32)
    columns = []
    for lane in range(width // DIM):
        lanes = slice(lane * DIM, (lane + 1) * DIM)
        pad[lane, :8] = halo[HALO - 8 :, lanes].astype(F32)
        pad[lane, 8 : 8 + length] = block[:, lanes].astype(F32)
        made = []
        for base in range(0, length, TILE):
            size = min(TILE, length)
            total = jnp.zeros((size, DIM), F32)
            for offset in range(count):
                first = base + 9 - count + offset
                total = total + pad[lane, first : first + size] * taps[offset : offset + 1, lanes]
            made.append(silu_of_twice(total).astype(BF16))
        columns.append(jnp.concatenate(made, axis=0))
    return jnp.concatenate(columns, axis=1)


def flag(condition):
    return jnp.where(condition, 1.0, 0.0).astype(F32)


def encode(message, states, decays):
    spot = lax.broadcasted_iota(jnp.int32, (8, DIM), 0)
    tail = jnp.zeros((8, DIM), F32)
    for head in range(PAIR):
        state, decay = states[head], decays[head]
        coarse = jnp.floor(decay)
        middle = jnp.floor((decay - coarse) * 1024.0) / 1024.0
        rest = decay - coarse - middle
        most = jnp.max(jnp.max(jnp.abs(state), axis=0, keepdims=True), axis=1, keepdims=True)
        power = jnp.ceil(jnp.log(jnp.maximum(most, 1e-30)))
        message[head * DIM : (head + 1) * DIM] = state * (jnp.exp(-power) * TOP)
        for index, value in enumerate((coarse, middle, rest, power)):
            tail = jnp.where(spot == PAIR * index + head, value, tail)
    message[PAIR * DIM :] = tail


def decode_decay(message):
    tail = message[PAIR * DIM :]
    return tail[:PAIR] + tail[PAIR : 2 * PAIR] + tail[2 * PAIR : 3 * PAIR]


def decode_size(message):
    return jnp.exp(message[PAIR * DIM :][3 * PAIR :]) / TOP


def tails_kernel(mixer, state, out, sems):
    length, width = mixer.shape
    span = pl.ds(length - HALO, HALO)
    copies = [
        pltpu.make_async_copy(mixer.at[span], out.at[:, :width], sems.at[0]),
        pltpu.make_async_copy(state.at[span], out.at[:, width:], sems.at[1]),
    ]
    for copy in copies:
        copy.start()
    for copy in copies:
        copy.wait()


def last_rows(mixer, state):
    return pl.pallas_call(
        tails_kernel,
        in_specs=[HBM, HBM],
        out_specs=VMEM,
        out_shape=pltpu.VMEM((HALO, mixer.shape[1] + state.shape[1]), BF16),
        scratch_shapes=[DMA((2,))],
        compiler_params=params(2),
        name="last_rows",
    )(in_hbm(mixer), in_hbm(state))


def prepare_kernel(
    mixer,
    state,
    taps,
    state_taps,
    step_raw,
    rate,
    inner,
    keys,
    running_out,
    step_out,
    scale,
    first_rows,
    last,
    taps_here,
    part1,
    part2,
    part3,
    mixer_here,
    keys_here,
    raw_here,
    rate_here,
    keys_t,
    late_scale,
    pad,
    mixer_sem,
    small_sem,
):
    x, _ = block_place()
    heads, length = step_raw.shape
    width = mixer.shape[1]
    wide = PAIR * DIM
    head_span = pl.ds(0, HALO)
    small = [
        pltpu.make_async_copy(source, target, small_sem.at[n])
        for n, (source, target) in enumerate(
            (
                (step_raw, raw_here),
                (rate, rate_here),
                (state.at[:, :DIM], keys_here),
                (state_taps, taps_here.at[:, width:]),
                (taps, taps_here.at[:, :width]),
                (state.at[head_span], first_rows.at[:, width:]),
                (mixer.at[head_span], first_rows.at[:, :width]),
            )
        )
    ]
    for copy in small[:5]:
        copy.start()
    pairs = [lax.rem(x + turn, XS) for turn in range(1, XS)]
    columns = [pl.ds(pl.multiple_of(pair * wide, wide), wide) for pair in pairs]
    large = [
        pltpu.make_async_copy(mixer.at[:, columns[turn]], mixer_here.at[turn], mixer_sem.at[turn])
        for turn in range(XS - 1)
    ]
    for copy in large + small[5:]:
        copy.start()

    for copy in small[:5]:
        copy.wait()
    raw = raw_here[...]
    step = jnp.maximum(raw, 0.0) + jnp.log1p(jnp.exp(-jnp.abs(raw)))
    spot = lax.broadcasted_iota(jnp.int32, (heads, length), 0)
    rates = jnp.zeros((heads, length), F32)
    for head in range(heads):
        rates = jnp.where(spot == head, rate_here[head], rates)
    running = -rates * step
    lane = lax.broadcasted_iota(jnp.int32, (heads, length), 1)
    shift = 1
    while shift < length:
        moved = pltpu.roll(running, shift, axis=1)
        running = running + jnp.where(lane >= shift, moved, 0.0)
        shift *= 2
    final = running[:, length - 1 :]
    running_out[...] = running
    step_out[...] = step
    scaled = jnp.exp(final - running) * step
    scale[...] = scaled
    late_scale[...] = jnp.where(lane < HALO, 0.0, scaled)
    last[...] = jnp.broadcast_to(final, last.shape)
    nothing = jnp.zeros((HALO, wide), BF16)
    made = conv(keys_here, nothing, taps_here[:, width : width + DIM], pad)
    keys[...] = made
    keys_t[...] = made.astype(F32).T

    for turn, part in enumerate((part1, part2, part3)):
        large[turn].wait()
        values = conv(mixer_here.at[turn], nothing, taps_here[:, columns[turn]], pad)
        inner[:, columns[turn]] = values
        for head in range(PAIR):
            row = late_scale[pl.ds(pairs[turn] * PAIR + head, 1), :]
            scaled_t = (keys_t[...] * row).astype(BF16)
            part[head * DIM : (head + 1) * DIM] = jnp.dot(
                scaled_t, values[:, head * DIM : (head + 1) * DIM], preferred_element_type=F32
            )
    for copy in small[5:]:
        copy.wait()


def prepare(mixer, state, taps, state_taps, step_raw_t, rate):
    length, width = mixer.shape
    heads = step_raw_t.shape[0]
    every = width + 2 * DIM
    by_token = pltpu.VMEM((heads, length), F32)
    return pl.pallas_call(
        prepare_kernel,
        in_specs=[HBM] * 6,
        out_specs=[VMEM] * (7 + XS),
        out_shape=[
            pltpu.VMEM((length, width), BF16),
            pltpu.VMEM((length, DIM), BF16),
            by_token,
            by_token,
            by_token,
            pltpu.VMEM((HALO, every), BF16),
            pltpu.VMEM((heads, DIM), F32),
            pltpu.VMEM((taps.shape[0], every), BF16),
        ]
        + [pltpu.VMEM((PAIR * DIM, DIM), F32)] * (XS - 1),
        scratch_shapes=[
            pltpu.VMEM((XS - 1, length, PAIR * DIM), BF16),
            pltpu.VMEM((length, DIM), BF16),
            by_token,
            pltpu.SMEM((heads,), F32),
            pltpu.VMEM((DIM, length), F32),
            by_token,
            pltpu.VMEM((PAIR, length + 8, DIM), F32),
            DMA((XS - 1,)),
            DMA((7,)),
        ],
        compiler_params=params(16),
        cost_estimate=cost(4.5),
        name="prepare",
    )(
        in_hbm(mixer),
        in_hbm(state),
        in_hbm(taps),
        in_hbm(state_taps),
        in_hbm(step_raw_t),
        in_hbm(rate),
    )


def finish_kernel(
    halo,
    first_rows,
    scale,
    last,
    taps,
    inner_in,
    keys_in,
    p1,
    p2,
    p3,
    inner,
    keys,
    m1,
    m2,
    m3,
    pad,
):
    x, _ = block_place()
    width = inner.shape[1]
    heads = width // DIM
    wide = PAIR * DIM
    states = slice(width, width + DIM)
    made = conv(first_rows.at[:, states], halo[:, states], taps[:, states], pad)
    keys[:HALO] = made
    early = made.astype(F32)
    columns = scale[:, :DIM].T
    scaled = [
        (early * jnp.broadcast_to(columns[:HALO, head : head + 1], (HALO, DIM))).astype(BF16)
        for head in range(heads)
    ]
    added = []
    for pair in range(XS):
        lanes = slice(pair * wide, (pair + 1) * wide)
        values = conv(first_rows.at[:, lanes], halo[:, lanes], taps[:, lanes], pad)
        inner[:HALO, lanes] = values
        for head in range(PAIR):
            added.append(
                lax.dot_general(
                    scaled[pair * PAIR + head],
                    values[:, head * DIM : (head + 1) * DIM],
                    (((0,), (0,)), ((), ())),
                    preferred_element_type=F32,
                )
            )
    for turn, (part, message) in enumerate(((p1, m1), (p2, m2), (p3, m3)), start=1):
        pair = lax.rem(x + turn, XS)
        totals = []
        decays = []
        for head in range(PAIR):
            extra = sum(
                added[other * PAIR + head] * flag(pair == other) for other in range(XS)
            )
            totals.append(part[head * DIM : (head + 1) * DIM] + extra)
            decays.append(last[pl.ds(pair * PAIR + head, 1), :])
        encode(message, totals, decays)


def finish(halo, first_rows, scale, last, taps, inner, keys, parts):
    return pl.pallas_call(
        finish_kernel,
        in_specs=[VMEM] * (6 + XS),
        out_specs=[VMEM] * (1 + XS),
        out_shape=[pltpu.VMEM(inner.shape, BF16), pltpu.VMEM(keys.shape, BF16)]
        + [pltpu.VMEM((MESSAGE, DIM), F32)] * (XS - 1),
        scratch_shapes=[pltpu.VMEM((PAIR, HALO + 8, DIM), F32)],
        input_output_aliases={5: 0, 6: 1},
        compiler_params=params(4),
        cost_estimate=cost(0.75),
        name="finish",
    )(halo, first_rows, scale, last, taps, inner, keys, *parts)


def shared_kernel(
    mixer,
    state,
    halo,
    taps,
    scale,
    last,
    running_in,
    keys,
    inner_in,
    inner,
    scores,
    lifted_base,
    ahead_out,
    message,
    mixer_here,
    state_here,
    queries,
    keys_t,
    pad,
    sems,
):
    x, _ = block_place()
    length, width = inner.shape
    heads = width // DIM
    tiles = length // TILE
    wide = PAIR * DIM
    own = pl.ds(pl.multiple_of(x * wide, wide), wide)
    copies = [
        pltpu.make_async_copy(state.at[:, DIM:], state_here, sems.at[0]),
        pltpu.make_async_copy(mixer.at[:, own], mixer_here, sems.at[1]),
    ]
    for copy in copies:
        copy.start()
    running = running_in[...]
    columns = jnp.exp(running).T
    ahead = jnp.concatenate(
        [
            jnp.exp(running[:, i * WIDE : (i + 1) * WIDE] - running[:, i * WIDE : i * WIDE + 1])
            for i in range(length // WIDE)
        ],
        axis=1,
    ).T
    keys_t[...] = keys[...].astype(F32).T
    for i in range(tiles):
        span = slice(i * TILE, (i + 1) * TILE)
        for head in range(heads):
            ahead_out[span, head * DIM : (head + 1) * DIM] = jnp.broadcast_to(
                ahead[span, head : head + 1], (TILE, DIM)
            )
    for copy in copies:
        copy.wait()
    states = slice(width + DIM, width + 2 * DIM)
    queries[...] = conv(state_here, halo[:, states], taps[:, states], pad)
    values = conv(mixer_here, halo[:, own], taps[:, own], pad)
    inner[:, own] = values
    totals = []
    decays = []
    for offset in range(PAIR):
        head = pl.ds(x * PAIR + offset, 1)
        totals.append(
            jnp.dot(
                (keys_t[...] * scale[head, :]).astype(BF16),
                values[:, offset * DIM : (offset + 1) * DIM],
                preferred_element_type=F32,
            )
        )
        decays.append(last[head, :])
    encode(message, totals, decays)
    for i in range(tiles):
        span = slice(i * TILE, (i + 1) * TILE)
        end = (i + 1) * TILE
        scores[span, :end] = lax.dot_general(
            queries[span],
            keys[:end],
            (((1,), (1,)), ((), ())),
            preferred_element_type=F32,
        )
        here = queries[span].astype(F32)
        for head in range(heads):
            lifted_base[span, head * DIM : (head + 1) * DIM] = here * jnp.broadcast_to(
                columns[span, head : head + 1], (TILE, DIM)
            )


def shared_part(mixer, state, halo, taps, scale, last, running, keys, inner):
    length, width = inner.shape
    return pl.pallas_call(
        shared_kernel,
        in_specs=[HBM, HBM] + [VMEM] * 7,
        out_specs=[VMEM] * 5,
        out_shape=[
            pltpu.VMEM((length, width), BF16),
            pltpu.VMEM((length, length), F32),
            pltpu.VMEM((length, width), F32),
            pltpu.VMEM((length, width), F32),
            pltpu.VMEM((MESSAGE, DIM), F32),
        ],
        scratch_shapes=[
            pltpu.VMEM((length, PAIR * DIM), BF16),
            pltpu.VMEM((length, DIM), BF16),
            pltpu.VMEM((length, DIM), BF16),
            pltpu.VMEM((DIM, length), F32),
            pltpu.VMEM((PAIR, length + 8, DIM), F32),
            DMA((2,)),
        ],
        input_output_aliases={8: 0},
        compiler_params=params(8),
        cost_estimate=cost(3.4),
        name="shared_part",
    )(in_hbm(mixer), in_hbm(state), halo, taps, scale, last, running, keys, inner)


def gates_kernel(gate, gates):
    length, width = gate.shape

    def one_tile(tile, carry):
        span = pl.ds(pl.multiple_of(tile * TILE, TILE), TILE)
        for piece in range(width // DIM):
            lane = slice(piece * DIM, (piece + 1) * DIM)
            gates[span, lane] = silu(gate[span, lane].astype(F32))
        return carry

    lax.fori_loop(0, length // TILE, one_tile, 0)


def mix_head(head, table, kinds, inner, running_in, step_in, scores, ahead_in, emit):
    length = inner.shape[0]
    stretch = length // kinds.shape[0]
    each = WIDE // stretch
    row = lax.broadcasted_iota(jnp.int32, (stretch, TILE), 0)
    column = lax.broadcasted_iota(jnp.int32, (stretch, TILE), 1)
    causal = [row + part * stretch >= column for part in range(TILE // stretch)]
    lane = lax.broadcasted_iota(jnp.int32, (1, TILE), 1)
    empty = jnp.zeros((stretch, TILE), BF16)
    lanes = pl.ds(pl.multiple_of(head * DIM, DIM), DIM)
    running = running_in[pl.ds(head, 1), :]
    step = step_in[pl.ds(head, 1), :]
    for i in range(length // WIDE):
        wide = (i + 1) * WIDE
        start = running[:, i * WIDE : i * WIDE + 1]
        behind = jnp.exp(start - running[:, :wide]) * step[:, :wide]
        bands = []
        for part in range(each):
            here = i * each + part
            kind = kinds[here]
            weight = [table[kind, head, level] for level in range(5)]
            band = slice(here * stretch, (here + 1) * stretch)
            ahead = ahead_in[band, lanes]
            pieces = []
            for j in range(wide // TILE):
                first, second = 2 * j, 2 * j + 1
                if first > here:
                    pieces.append(empty)
                    continue
                left = weight[(here ^ first).bit_length()]
                right = weight[(here ^ second).bit_length()]
                if second > here or (here ^ first).bit_length() == (here ^ second).bit_length():
                    factor = left
                else:
                    factor = jnp.where(lane < stretch, left, right)
                tile = slice(j * TILE, (j + 1) * TILE)
                piece = scores[band, tile] * (behind[:, tile] * factor) * ahead
                if second >= here:
                    piece = jnp.where(causal[here - first], piece, 0.0)
                pieces.append(piece.astype(BF16))
            bands.append(jnp.concatenate(pieces, axis=1))
        emit(
            i,
            jnp.dot(
                jnp.concatenate(bands, axis=0), inner[:wide, lanes], preferred_element_type=F32
            ),
        )


def lift(table, kinds, lifted_base, head, tile, levels, held, WIDE=WIDE):
    length = lifted_base.shape[0]
    stretch = length // kinds.shape[0]
    lanes = pl.ds(pl.multiple_of(head * DIM, DIM), DIM)
    bands = []
    for here in range(tile * WIDE // stretch, (tile + 1) * WIDE // stretch):
        kind = kinds[here]
        base = lifted_base[here * stretch : (here + 1) * stretch, lanes]
        bands.append(
            jnp.concatenate(
                [(base * table[kind, head, level]).astype(BF16) for level in levels], axis=1
            )
        )
    return jnp.dot(jnp.concatenate(bands, axis=0), held[head], preferred_element_type=F32)


def mix_kernel(first, count, table, kinds, inner, running_in, step_in, scores, ahead_in, out):
    def one_head(offset, carry):
        lanes = pl.ds(pl.multiple_of(offset * DIM, DIM), DIM)

        def emit(i, value):
            out[i * WIDE : (i + 1) * WIDE, lanes] = value

        mix_head(
            first + offset, table, kinds, inner, running_in, step_in, scores, ahead_in, emit
        )
        return carry

    lax.fori_loop(0, count, one_head, 0, unroll=True)


def mix_part(first, count, table, kinds, inner, running, step, scores, ahead):
    length, width = inner.shape
    return pl.pallas_call(
        functools.partial(mix_kernel, first, count),
        in_specs=[SMEM, SMEM] + [VMEM] * 5,
        out_specs=VMEM,
        out_shape=pltpu.VMEM((length, count * DIM), F32),
        compiler_params=params(8),
        cost_estimate=cost(0.75 * count + 0.5),
        name="mix_part",
    )(table, kinds, inner, running, step, scores, ahead)


def turn_kernel(first, count, upper, *refs):
    table, kinds, inner, running_in, step_in, scores, ahead_in, gate = refs[:8]
    out, gates = refs[-2:]
    _, z = block_place()

    @pl.when((z >= ZS // 2) == upper)
    def _():
        mix_kernel(
            first, count, table, kinds, inner, running_in, step_in, scores, ahead_in, out
        )
        gates_kernel(gate, gates)


def turn_part(first, count, upper, earlier, table, kinds, inner, running, step, scores, ahead, gate):
    length, width = inner.shape
    return pl.pallas_call(
        functools.partial(turn_kernel, first, count, upper),
        in_specs=[SMEM, SMEM] + [VMEM] * (6 + len(earlier)),
        out_specs=[VMEM] * 2,
        out_shape=[pltpu.VMEM((length, count * DIM), F32), pltpu.VMEM(gate.shape, F32)],
        input_output_aliases={8: 0, 9: 1} if earlier else {},
        compiler_params=params(8),
        cost_estimate=cost(0.6 * count + 1.2 if upper else 0.2),
        name="turn_part",
    )(table, kinds, inner, running, step, scores, ahead, gate, *earlier)


def local_kernel(
    done,
    table,
    kinds,
    inner,
    running_in,
    step_in,
    scores,
    ahead_in,
    lifted_base,
    *rest,
):
    mixed = rest[:done]
    nears = rest[done : done + XS]
    out, held = rest[done + XS :]
    x, _ = block_place()
    length, width = inner.shape
    heads = width // DIM
    for k, near in enumerate(nears):
        pair = lax.rem(x + XS - k, XS)
        for head in range(PAIR):
            for level in range(NEAR):
                base = (level * PAIR + head) * DIM
                held[pair * PAIR + head, level * DIM : (level + 1) * DIM] = near[
                    base : base + DIM
                ]
    levels = range(5, 5 + NEAR)
    head = 0
    for value in mixed:
        for offset in range(value.shape[1] // DIM):
            for tile in range(length // WIDE):
                span = slice(tile * WIDE, (tile + 1) * WIDE)
                out[span, head * DIM : (head + 1) * DIM] = value[
                    span, offset * DIM : (offset + 1) * DIM
                ] + lift(table, kinds, lifted_base, head, tile, levels, held)
            head += 1

    def one_head(head, carry):
        lanes = pl.ds(pl.multiple_of(head * DIM, DIM), DIM)

        def emit(i, value):
            out[i * WIDE : (i + 1) * WIDE, lanes] = value + lift(
                table, kinds, lifted_base, head, i, levels, held
            )

        mix_head(head, table, kinds, inner, running_in, step_in, scores, ahead_in, emit)
        return carry

    lax.fori_loop(head, heads, one_head, 0, unroll=2)


def local_part(table, kinds, inner, running, step, scores, ahead, lifted_base, mixed, near):
    length, width = inner.shape
    heads = width // DIM
    return pl.pallas_call(
        functools.partial(local_kernel, len(mixed)),
        in_specs=[SMEM, SMEM] + [VMEM] * (6 + len(mixed) + XS),
        out_specs=VMEM,
        out_shape=pltpu.VMEM((length, width), F32),
        scratch_shapes=[pltpu.VMEM((heads, NEAR * DIM, DIM), BF16)],
        compiler_params=params(8),
        cost_estimate=cost(3.8),
        name="local_part",
    )(table, kinds, inner, running, step, scores, ahead, lifted_base, *mixed, *near)


def fold_row_kernel(p0, p1, p2, p3, row_out):
    x, _ = block_place()
    parts = (p0, p1, p2, p3)
    owner = [lax.rem(x + XS - k, XS) for k in range(XS)]
    decays = [decode_decay(part) for part in parts]
    later = [
        jnp.exp(sum(decays[m] * flag(owner[m] > owner[k]) for m in range(XS)))
        * decode_size(parts[k])
        for k in range(XS)
    ]
    total = sum(decays)
    states = []
    for head in range(PAIR):
        span = slice(head * DIM, (head + 1) * DIM)
        states.append(sum(parts[k][span] * later[k][head : head + 1] for k in range(XS)))
    encode(row_out, states, [total[head : head + 1] for head in range(PAIR)])


def fold_row(parts):
    return pl.pallas_call(
        fold_row_kernel,
        in_specs=[VMEM] * XS,
        out_specs=VMEM,
        out_shape=pltpu.VMEM((MESSAGE, DIM), F32),
        compiler_params=params(4),
        cost_estimate=cost(0.25),
        name="fold_row",
    )(*parts)


def fold_near_kernel(p0, p1, p2, p3, row_before, m0, m1, m2, m3):
    x, z = block_place()
    parts = (p0, p1, p2, p3)
    owner = [lax.rem(x + XS - k, XS) for k in range(XS)]
    decays = [decode_decay(part) for part in parts]
    sizes = [decode_size(part) for part in parts]
    odd_size = decode_size(row_before) * flag(lax.rem(z, 2) == 1)

    def pick(values, block):
        return sum(value * flag(owner[k] == block) for k, value in enumerate(values))

    decay_one = jnp.exp(pick(decays, 1))
    decay_two = jnp.exp(pick(decays, 2))
    for head in range(PAIR):
        span = slice(head * DIM, (head + 1) * DIM)
        row = slice(head, head + 1)
        scaled = [parts[k][span] * sizes[k][row] for k in range(XS)]
        first = pick(scaled, 0)
        third = pick(scaled, 2)
        joined = first * decay_one[row] + pick(scaled, 1)
        above = row_before[span]
        for k, message in enumerate((m0, m1, m2, m3)):
            target = lax.rem(x + k, XS)
            before = sum(decays[m][row] * flag(owner[m] < target) for m in range(XS))
            levels = (
                first * flag(target == 1) + third * flag(target == 3),
                joined * (flag(target == 2) + flag(target == 3) * decay_two[row]),
                above * (jnp.exp(before) * odd_size[row]),
            )
            for level, value in enumerate(levels):
                base = (level * PAIR + head) * DIM
                message[base : base + DIM] = value.astype(BF16)


def fold_near(parts, row_before):
    return pl.pallas_call(
        fold_near_kernel,
        in_specs=[VMEM] * (XS + 1),
        out_specs=[VMEM] * XS,
        out_shape=[pltpu.VMEM((NEAR * PAIR * DIM, DIM), BF16)] * XS,
        compiler_params=params(4),
        cost_estimate=cost(0.3),
        name="fold_near",
    )(*parts, row_before)


def fold_two_kernel(span_rows, own, other, out):
    _, z = block_place()
    upper = flag(lax.rem(lax.div(z, span_rows), 2) == 1)
    own_decay = decode_decay(own)
    other_decay = decode_decay(other)
    own_scale = jnp.exp(other_decay * (1.0 - upper)) * decode_size(own)
    other_scale = jnp.exp(own_decay * upper) * decode_size(other)
    decay = own_decay + other_decay
    states = []
    for head in range(PAIR):
        span = slice(head * DIM, (head + 1) * DIM)
        row = slice(head, head + 1)
        states.append(own[span] * own_scale[row] + other[span] * other_scale[row])
    encode(out, states, [decay[head : head + 1] for head in range(PAIR)])


def fold_two(span_rows, own, other):
    return pl.pallas_call(
        functools.partial(fold_two_kernel, span_rows),
        in_specs=[VMEM] * 2,
        out_specs=VMEM,
        out_shape=pltpu.VMEM((MESSAGE, DIM), F32),
        compiler_params=params(4),
        cost_estimate=cost(0.2),
        name="fold_two",
    )(own, other)


def fold_far_kernel(d0, d1, d2, d3, row_before, pair_before, quad_before, m0, m1, m2, m3):
    x, z = block_place()
    odd = flag(lax.rem(z, 2) == 1)
    odd_pair = flag(lax.rem(lax.div(z, 2), 2) == 1)
    upper = flag(z >= ZS // 2)
    decays = [decode_decay(part) for part in (d0, d1, d2, d3)]
    owner = [lax.rem(x + XS - k, XS) for k in range(XS)]
    in_pair = decode_decay(row_before) * odd
    in_quad = in_pair + decode_decay(pair_before) * odd_pair
    levels = (
        (pair_before, in_pair, decode_size(pair_before) * odd_pair),
        (quad_before, in_quad, decode_size(quad_before) * upper),
    )
    for k, message in enumerate((m0, m1, m2, m3)):
        target = lax.rem(x + k, XS)
        before = sum(decays[m] * flag(owner[m] < target) for m in range(XS))
        for level, (state, between, size) in enumerate(levels):
            factor = jnp.exp(before + between) * size
            for head in range(PAIR):
                base = (level * PAIR + head) * DIM
                message[base : base + DIM] = (
                    state[head * DIM : (head + 1) * DIM] * factor[head : head + 1]
                ).astype(BF16)


def fold_far(parts, befores):
    return pl.pallas_call(
        fold_far_kernel,
        in_specs=[VMEM] * (XS + 3),
        out_specs=[VMEM] * XS,
        out_shape=[pltpu.VMEM((FAR * PAIR * DIM, DIM), BF16)] * XS,
        compiler_params=params(4),
        cost_estimate=cost(0.25),
        name="fold_far",
    )(*parts, *befores)


def far_kernel(
    table, kinds, local, gates, lifted_base, f0, f1, f2, f3, gated, squares, held, total
):
    x, _ = block_place()
    length, width = local.shape
    heads = width // DIM
    for k, far in enumerate((f0, f1, f2, f3)):
        pair = lax.rem(x + XS - k, XS)
        for head in range(PAIR):
            for level in range(FAR):
                base = (level * PAIR + head) * DIM
                held[pair * PAIR + head, level * DIM : (level + 1) * DIM] = far[base : base + DIM]
    levels = range(5 + NEAR, 5 + NEAR + FAR)
    for pair in range(heads // 2):
        values = []
        for head in (2 * pair, 2 * pair + 1):
            lanes = slice(head * DIM, (head + 1) * DIM)
            mixed = local[:, lanes] + lift(
                table, kinds, lifted_base, head, 0, levels, held, length
            )
            value = mixed * gates[:, lanes]
            gated[:, lanes] = value
            values.append(value * value)
        if pair == 0:
            total[...] = values[0] + values[1]
        else:
            total[...] += values[0] + values[1]
    for tile in range(length // TILE):
        part = total[tile * TILE : (tile + 1) * TILE].T
        squares[tile : tile + 1] = jnp.sum(part, axis=0, keepdims=True)


def far_part(table, kinds, local, gates, lifted_base, far_states):
    length, width = local.shape
    heads = width // DIM
    return pl.pallas_call(
        far_kernel,
        in_specs=[SMEM, SMEM] + [VMEM] * (3 + XS),
        out_specs=[VMEM] * 2,
        out_shape=[pltpu.VMEM((length, width), F32), pltpu.VMEM((length // TILE, TILE), F32)],
        scratch_shapes=[pltpu.VMEM((heads, FAR * DIM, DIM), BF16), pltpu.VMEM((length, DIM), F32)],
        compiler_params=params(8),
        cost_estimate=cost(3.5),
        name="far_part",
    )(table, kinds, local, gates, lifted_base, *far_states)


def norm_kernel(total_width, gated, s0, s1, s2, s3, gain, out, made, sems):
    scale = lax.rsqrt((s0[...] + s1[...] + s2[...] + s3[...]) / total_width + 1e-05)
    length, width = gated.shape
    copies = []
    for tile in range(length // TILE):
        span = slice(tile * TILE, (tile + 1) * TILE)
        column = jnp.broadcast_to(scale[tile : tile + 1], (TILE, TILE)).T
        for piece in range(width // TILE):
            lane = slice(piece * TILE, (piece + 1) * TILE)
            made[span, lane] = (gated[span, lane] * column * gain[:, lane]).astype(BF16)
        copies.append(pltpu.make_async_copy(made.at[span], out.at[span], sems.at[tile]))
        copies[-1].start()
    for copy in copies:
        copy.wait()


def norm(gated, squares, gain, total_width):
    length, width = gated.shape
    return pl.pallas_call(
        functools.partial(norm_kernel, total_width),
        in_specs=[VMEM] * (2 + YS),
        out_specs=HBM,
        out_shape=jax.ShapeDtypeStruct((length, width), BF16),
        scratch_shapes=[pltpu.VMEM((length, width), BF16), DMA((length // TILE,))],
        compiler_params=params(8),
        cost_estimate=cost(1.6),
        name="norm",
    )(gated, *squares, gain)


def local(
    mixer_input,
    state_input,
    gate_input,
    step_raw,
    decay_rate,
    conv_inner,
    conv_state,
    level_table,
    stretch_kind,
    norm_gain,
):
    length, width = mixer_input.shape
    halo = lax.ppermute(
        last_rows(mixer_input, state_input), "seq", [(i, i + 1) for i in range(XS * ZS - 1)]
    )
    inner, keys, running, step, scale, first_rows, last, taps, *parts = prepare(
        mixer_input, state_input, conv_inner, conv_state, step_raw.T, decay_rate
    )
    inner, keys, *parts = finish(halo, first_rows, scale, last, taps, inner, keys, parts)
    table = jnp.transpose(level_table, (0, 2, 1))
    moved = {
        k: sent(parts[k - 1], lambda z, x, k=k: (z, (x + k) % XS)) for k in (2, 1, 3)
    }
    arrived = [moved[k] for k in range(1, XS)]
    inner, scores, lifted_base, ahead, own_part = shared_part(
        mixer_input, state_input, halo, taps, scale, last, running, keys, inner
    )
    arrived = [own_part] + arrived
    mix = functools.partial(
        mix_part,
        table=table,
        kinds=stretch_kind,
        inner=inner,
        running=running,
        step=step,
        scores=scores,
        ahead=ahead,
    )
    row_state = fold_row(arrived)
    row_before = sent(row_state, lambda z, x: (z ^ 1, x))
    row_before, mixed_first = lax.optimization_barrier((row_before, mix(0, PAIR)))
    pair_state = fold_two(1, row_state, row_before)
    near = fold_near(arrived, row_before)
    pair_before = sent(pair_state, lambda z, x: (z ^ 2, x))
    near = [near[0]] + [along_x(near[k], k) for k in range(1, XS)]
    quad_state = fold_two(2, pair_state, pair_before)
    turn = functools.partial(
        turn_part,
        PAIR,
        2 * PAIR,
        table=table,
        kinds=stretch_kind,
        inner=inner,
        running=running,
        scores=scores,
        ahead=ahead,
        gate=gate_input,
    )
    quad_state, step_late = lax.optimization_barrier((quad_state, step))
    quad_state, *turned = lax.optimization_barrier(
        (quad_state, *turn(False, (), step=step_late))
    )
    quad_before = sent(quad_state, lambda z, x: (ZS - 1 - z, x) if z < ZS // 2 else None)
    quad_before, mixed_second, gates = lax.optimization_barrier(
        (quad_before, *turn(True, turned, step=step_late))
    )
    far = fold_far(arrived, (row_before, pair_before, quad_before))
    far = [far[0]] + [along_x(far[k], k) for k in range(1, XS)]
    local_out = local_part(
        table,
        stretch_kind,
        inner,
        running,
        step,
        scores,
        ahead,
        lifted_base,
        (mixed_first, mixed_second),
        near,
    )
    gated, squares = far_part(table, stretch_kind, local_out, gates, lifted_base, far)
    squares = squares + lax.ppermute(squares, "head", head_perm(lambda y, core: (y, 1 - core)))
    sums = [squares] + [
        lax.ppermute(squares, "head", head_perm(lambda y, core, k=k: ((y + k) % YS, core)))
        for k in (2, 1, 3)
    ]
    total_width = width * lax.axis_size("head")
    return norm(gated, sums, norm_gain[None, :], total_width)


def solution(mesh):
    return jax.shard_map(
        local,
        mesh=mesh,
        in_specs=(
            P("seq", "head"),
            P("seq", None),
            P("seq", "head"),
            P("seq", "head"),
            P("head"),
            P(None, "head"),
            P(),
            P(None, None, "head"),
            P("seq"),
            P("head"),
        ),
        out_specs=P("seq", "head"),
        check_vma=False,
    )
```

```python
import functools
import jax
import jax.numpy as jnp
from jax import lax
from jax.experimental import pallas as pl
from jax.experimental.pallas import tpu as pltpu
from jax.sharding import PartitionSpec as P

F32 = jnp.float32
BF16 = jnp.bfloat16

XS = 4
ZS = 8
YS = 4
CORES = 2
PAIR = 2
DIM = 128
HALO = 16
TILE = 128
WIDE = 256
NEAR = 3
FAR = 2
LEVELS = 5 + NEAR + FAR
TOP = 16384.0
MESSAGE = PAIR * DIM + 8


def seq_perm(move):
    pairs = []
    for z in range(ZS):
        for x in range(XS):
            target = move(z, x)
            if target is not None:
                pairs.append((z * XS + x, target[0] * XS + target[1]))
    return pairs


def head_perm(move):
    pairs = []
    for y in range(YS):
        for core in range(CORES):
            target = move(y, core)
            pairs.append((y * CORES + core, target[0] * CORES + target[1]))
    return pairs


def along_x(value, step):
    return lax.ppermute(value, "seq", seq_perm(lambda z, x: (z, (x + step) % XS)))


def sent(message, move):
    return lax.ppermute(message.astype(jnp.float16), "seq", seq_perm(move)).astype(F32)


def silu_of_twice(half):
    return half + half * jnp.tanh(half)


def silu(value):
    return silu_of_twice(0.5 * value)


VMEM = pl.BlockSpec(memory_space=pltpu.VMEM)
SMEM = pl.BlockSpec(memory_space=pltpu.SMEM)
HBM = pl.BlockSpec(memory_space=pltpu.HBM)
DMA = pltpu.SemaphoreType.DMA


def params(mebibytes):
    return pltpu.CompilerParams(vmem_limit_bytes=mebibytes * 2**20)


def cost(microseconds):
    return pl.CostEstimate(
        flops=int(microseconds * 1.15e9),
        bytes_accessed=int(microseconds * 3.6e6),
        transcendentals=0,
    )


def in_hbm(value):
    return pltpu.with_memory_space_constraint(value, pltpu.HBM)


def block_place():
    index = lax.axis_index("seq")
    return lax.rem(index, XS), lax.div(index, XS)


def conv(block, halo, taps, pad):
    length, width = block.shape
    count = taps.shape[0]
    taps = 0.5 * taps.astype(F32)
    columns = []
    for lane in range(width // DIM):
        lanes = slice(lane * DIM, (lane + 1) * DIM)
        pad[lane, :8] = halo[HALO - 8 :, lanes].astype(F32)
        pad[lane, 8 : 8 + length] = block[:, lanes].astype(F32)
        made = []
        for base in range(0, length, TILE):
            size = min(TILE, length)
            total = jnp.zeros((size, DIM), F32)
            for offset in range(count):
                first = base + 9 - count + offset
                total = total + pad[lane, first : first + size] * taps[offset : offset + 1, lanes]
            made.append(silu_of_twice(total).astype(BF16))
        columns.append(jnp.concatenate(made, axis=0))
    return jnp.concatenate(columns, axis=1)


def flag(condition):
    return jnp.where(condition, 1.0, 0.0).astype(F32)


def encode(message, states, decays):
    spot = lax.broadcasted_iota(jnp.int32, (8, DIM), 0)
    tail = jnp.zeros((8, DIM), F32)
    for head in range(PAIR):
        state, decay = states[head], decays[head]
        coarse = jnp.floor(decay)
        middle = jnp.floor((decay - coarse) * 1024.0) / 1024.0
        rest = decay - coarse - middle
        most = jnp.max(jnp.max(jnp.abs(state), axis=0, keepdims=True), axis=1, keepdims=True)
        power = jnp.ceil(jnp.log(jnp.maximum(most, 1e-30)))
        message[head * DIM : (head + 1) * DIM] = state * (jnp.exp(-power) * TOP)
        for index, value in enumerate((coarse, middle, rest, power)):
            tail = jnp.where(spot == PAIR * index + head, value, tail)
    message[PAIR * DIM :] = tail


def decode_decay(message):
    tail = message[PAIR * DIM :]
    return tail[:PAIR] + tail[PAIR : 2 * PAIR] + tail[2 * PAIR : 3 * PAIR]


def decode_size(message):
    return jnp.exp(message[PAIR * DIM :][3 * PAIR :]) / TOP


def tails_kernel(mixer, state, out, sems):
    length, width = mixer.shape
    span = pl.ds(length - HALO, HALO)
    copies = [
        pltpu.make_async_copy(mixer.at[span], out.at[:, :width], sems.at[0]),
        pltpu.make_async_copy(state.at[span], out.at[:, width:], sems.at[1]),
    ]
    for copy in copies:
        copy.start()
    for copy in copies:
        copy.wait()


def last_rows(mixer, state):
    return pl.pallas_call(
        tails_kernel,
        in_specs=[HBM, HBM],
        out_specs=VMEM,
        out_shape=pltpu.VMEM((HALO, mixer.shape[1] + state.shape[1]), BF16),
        scratch_shapes=[DMA((2,))],
        compiler_params=params(2),
        name="last_rows",
    )(in_hbm(mixer), in_hbm(state))


def prepare_kernel(
    mixer,
    state,
    taps,
    state_taps,
    step_raw,
    rate,
    inner,
    keys,
    running_out,
    step_out,
    scale,
    first_rows,
    last,
    taps_here,
    part1,
    part2,
    part3,
    mixer_here,
    keys_here,
    raw_here,
    rate_here,
    keys_t,
    late_scale,
    pad,
    mixer_sem,
    small_sem,
):
    x, _ = block_place()
    heads, length = step_raw.shape
    width = mixer.shape[1]
    wide = PAIR * DIM
    head_span = pl.ds(0, HALO)
    small = [
        pltpu.make_async_copy(source, target, small_sem.at[n])
        for n, (source, target) in enumerate(
            (
                (step_raw, raw_here),
                (rate, rate_here),
                (state.at[:, :DIM], keys_here),
                (state_taps, taps_here.at[:, width:]),
                (taps, taps_here.at[:, :width]),
                (state.at[head_span], first_rows.at[:, width:]),
                (mixer.at[head_span], first_rows.at[:, :width]),
            )
        )
    ]
    for copy in small[:5]:
        copy.start()
    pairs = [lax.rem(x + turn, XS) for turn in range(1, XS)]
    columns = [pl.ds(pl.multiple_of(pair * wide, wide), wide) for pair in pairs]
    large = [
        pltpu.make_async_copy(mixer.at[:, columns[turn]], mixer_here.at[turn], mixer_sem.at[turn])
        for turn in range(XS - 1)
    ]
    for copy in large + small[5:]:
        copy.start()

    for copy in small[:5]:
        copy.wait()
    raw = raw_here[...]
    step = jnp.maximum(raw, 0.0) + jnp.log1p(jnp.exp(-jnp.abs(raw)))
    spot = lax.broadcasted_iota(jnp.int32, (heads, length), 0)
    rates = jnp.zeros((heads, length), F32)
    for head in range(heads):
        rates = jnp.where(spot == head, rate_here[head], rates)
    running = -rates * step
    lane = lax.broadcasted_iota(jnp.int32, (heads, length), 1)
    shift = 1
    while shift < length:
        moved = pltpu.roll(running, shift, axis=1)
        running = running + jnp.where(lane >= shift, moved, 0.0)
        shift *= 2
    final = running[:, length - 1 :]
    running_out[...] = running
    step_out[...] = step
    scaled = jnp.exp(final - running) * step
    scale[...] = scaled
    late_scale[...] = jnp.where(lane < HALO, 0.0, scaled)
    last[...] = jnp.broadcast_to(final, last.shape)
    nothing = jnp.zeros((HALO, wide), BF16)
    made = conv(keys_here, nothing, taps_here[:, width : width + DIM], pad)
    keys[...] = made
    keys_t[...] = made.astype(F32).T

    for turn, part in enumerate((part1, part2, part3)):
        large[turn].wait()
        values = conv(mixer_here.at[turn], nothing, taps_here[:, columns[turn]], pad)
        inner[:, columns[turn]] = values
        for head in range(PAIR):
            row = late_scale[pl.ds(pairs[turn] * PAIR + head, 1), :]
            scaled_t = (keys_t[...] * row).astype(BF16)
            part[head * DIM : (head + 1) * DIM] = jnp.dot(
                scaled_t, values[:, head * DIM : (head + 1) * DIM], preferred_element_type=F32
            )
    for copy in small[5:]:
        copy.wait()


def prepare(mixer, state, taps, state_taps, step_raw_t, rate):
    length, width = mixer.shape
    heads = step_raw_t.shape[0]
    every = width + 2 * DIM
    by_token = pltpu.VMEM((heads, length), F32)
    return pl.pallas_call(
        prepare_kernel,
        in_specs=[HBM] * 6,
        out_specs=[VMEM] * (7 + XS),
        out_shape=[
            pltpu.VMEM((length, width), BF16),
            pltpu.VMEM((length, DIM), BF16),
            by_token,
            by_token,
            by_token,
            pltpu.VMEM((HALO, every), BF16),
            pltpu.VMEM((heads, DIM), F32),
            pltpu.VMEM((taps.shape[0], every), BF16),
        ]
        + [pltpu.VMEM((PAIR * DIM, DIM), F32)] * (XS - 1),
        scratch_shapes=[
            pltpu.VMEM((XS - 1, length, PAIR * DIM), BF16),
            pltpu.VMEM((length, DIM), BF16),
            by_token,
            pltpu.SMEM((heads,), F32),
            pltpu.VMEM((DIM, length), F32),
            by_token,
            pltpu.VMEM((PAIR, length + 8, DIM), F32),
            DMA((XS - 1,)),
            DMA((7,)),
        ],
        compiler_params=params(16),
        cost_estimate=cost(4.5),
        name="prepare",
    )(
        in_hbm(mixer),
        in_hbm(state),
        in_hbm(taps),
        in_hbm(state_taps),
        in_hbm(step_raw_t),
        in_hbm(rate),
    )


def finish_kernel(
    halo,
    first_rows,
    scale,
    last,
    taps,
    inner_in,
    keys_in,
    p1,
    p2,
    p3,
    inner,
    keys,
    m1,
    m2,
    m3,
    pad,
):
    x, _ = block_place()
    width = inner.shape[1]
    heads = width // DIM
    wide = PAIR * DIM
    states = slice(width, width + DIM)
    made = conv(first_rows.at[:, states], halo[:, states], taps[:, states], pad)
    keys[:HALO] = made
    early = made.astype(F32)
    columns = scale[:, :DIM].T
    scaled = [
        (early * jnp.broadcast_to(columns[:HALO, head : head + 1], (HALO, DIM))).astype(BF16)
        for head in range(heads)
    ]
    added = []
    for pair in range(XS):
        lanes = slice(pair * wide, (pair + 1) * wide)
        values = conv(first_rows.at[:, lanes], halo[:, lanes], taps[:, lanes], pad)
        inner[:HALO, lanes] = values
        for head in range(PAIR):
            added.append(
                lax.dot_general(
                    scaled[pair * PAIR + head],
                    values[:, head * DIM : (head + 1) * DIM],
                    (((0,), (0,)), ((), ())),
                    preferred_element_type=F32,
                )
            )
    for turn, (part, message) in enumerate(((p1, m1), (p2, m2), (p3, m3)), start=1):
        pair = lax.rem(x + turn, XS)
        totals = []
        decays = []
        for head in range(PAIR):
            extra = sum(
                added[other * PAIR + head] * flag(pair == other) for other in range(XS)
            )
            totals.append(part[head * DIM : (head + 1) * DIM] + extra)
            decays.append(last[pl.ds(pair * PAIR + head, 1), :])
        encode(message, totals, decays)


def finish(halo, first_rows, scale, last, taps, inner, keys, parts):
    return pl.pallas_call(
        finish_kernel,
        in_specs=[VMEM] * (6 + XS),
        out_specs=[VMEM] * (1 + XS),
        out_shape=[pltpu.VMEM(inner.shape, BF16), pltpu.VMEM(keys.shape, BF16)]
        + [pltpu.VMEM((MESSAGE, DIM), F32)] * (XS - 1),
        scratch_shapes=[pltpu.VMEM((PAIR, HALO + 8, DIM), F32)],
        input_output_aliases={5: 0, 6: 1},
        compiler_params=params(4),
        cost_estimate=cost(0.75),
        name="finish",
    )(halo, first_rows, scale, last, taps, inner, keys, *parts)


def shared_kernel(
    mixer,
    state,
    halo,
    taps,
    scale,
    last,
    running_in,
    keys,
    inner_in,
    inner,
    scores,
    lifted_base,
    ahead_out,
    message,
    mixer_here,
    state_here,
    queries,
    keys_t,
    pad,
    sems,
):
    x, _ = block_place()
    length, width = inner.shape
    heads = width // DIM
    tiles = length // TILE
    wide = PAIR * DIM
    own = pl.ds(pl.multiple_of(x * wide, wide), wide)
    copies = [
        pltpu.make_async_copy(state.at[:, DIM:], state_here, sems.at[0]),
        pltpu.make_async_copy(mixer.at[:, own], mixer_here, sems.at[1]),
    ]
    for copy in copies:
        copy.start()
    running = running_in[...]
    columns = jnp.exp(running).T
    ahead = jnp.concatenate(
        [
            jnp.exp(running[:, i * WIDE : (i + 1) * WIDE] - running[:, i * WIDE : i * WIDE + 1])
            for i in range(length // WIDE)
        ],
        axis=1,
    ).T
    keys_t[...] = keys[...].astype(F32).T
    for i in range(tiles):
        span = slice(i * TILE, (i + 1) * TILE)
        for head in range(heads):
            ahead_out[span, head * DIM : (head + 1) * DIM] = jnp.broadcast_to(
                ahead[span, head : head + 1], (TILE, DIM)
            )
    for copy in copies:
        copy.wait()
    states = slice(width + DIM, width + 2 * DIM)
    queries[...] = conv(state_here, halo[:, states], taps[:, states], pad)
    values = conv(mixer_here, halo[:, own], taps[:, own], pad)
    inner[:, own] = values
    totals = []
    decays = []
    for offset in range(PAIR):
        head = pl.ds(x * PAIR + offset, 1)
        totals.append(
            jnp.dot(
                (keys_t[...] * scale[head, :]).astype(BF16),
                values[:, offset * DIM : (offset + 1) * DIM],
                preferred_element_type=F32,
            )
        )
        decays.append(last[head, :])
    encode(message, totals, decays)
    for i in range(tiles):
        span = slice(i * TILE, (i + 1) * TILE)
        end = (i + 1) * TILE
        scores[span, :end] = lax.dot_general(
            queries[span],
            keys[:end],
            (((1,), (1,)), ((), ())),
            preferred_element_type=F32,
        )
        here = queries[span].astype(F32)
        for head in range(heads):
            lifted_base[span, head * DIM : (head + 1) * DIM] = here * jnp.broadcast_to(
                columns[span, head : head + 1], (TILE, DIM)
            )


def shared_part(mixer, state, halo, taps, scale, last, running, keys, inner):
    length, width = inner.shape
    return pl.pallas_call(
        shared_kernel,
        in_specs=[HBM, HBM] + [VMEM] * 7,
        out_specs=[VMEM] * 5,
        out_shape=[
            pltpu.VMEM((length, width), BF16),
            pltpu.VMEM((length, length), F32),
            pltpu.VMEM((length, width), F32),
            pltpu.VMEM((length, width), F32),
            pltpu.VMEM((MESSAGE, DIM), F32),
        ],
        scratch_shapes=[
            pltpu.VMEM((length, PAIR * DIM), BF16),
            pltpu.VMEM((length, DIM), BF16),
            pltpu.VMEM((length, DIM), BF16),
            pltpu.VMEM((DIM, length), F32),
            pltpu.VMEM((PAIR, length + 8, DIM), F32),
            DMA((2,)),
        ],
        input_output_aliases={8: 0},
        compiler_params=params(8),
        cost_estimate=cost(3.4),
        name="shared_part",
    )(in_hbm(mixer), in_hbm(state), halo, taps, scale, last, running, keys, inner)


def gates_kernel(gate, gates):
    length, width = gate.shape

    def one_tile(tile, carry):
        span = pl.ds(pl.multiple_of(tile * TILE, TILE), TILE)
        for piece in range(width // DIM):
            lane = slice(piece * DIM, (piece + 1) * DIM)
            gates[span, lane] = silu(gate[span, lane].astype(F32))
        return carry

    lax.fori_loop(0, length // TILE, one_tile, 0)


def level_weight(table, kind, head, level, heads):
    return table[(kind * heads + head) * LEVELS + level]


def mix_head(head, table, kinds, inner, running_in, step_in, scores, ahead_in, emit):
    length = inner.shape[0]
    heads = inner.shape[1] // DIM
    stretch = length // kinds.shape[0]
    each = WIDE // stretch
    row = lax.broadcasted_iota(jnp.int32, (stretch, TILE), 0)
    column = lax.broadcasted_iota(jnp.int32, (stretch, TILE), 1)
    causal = [row + part * stretch >= column for part in range(TILE // stretch)]
    lane = lax.broadcasted_iota(jnp.int32, (1, TILE), 1)
    empty = jnp.zeros((stretch, TILE), BF16)
    lanes = pl.ds(pl.multiple_of(head * DIM, DIM), DIM)
    running = running_in[pl.ds(head, 1), :]
    step = step_in[pl.ds(head, 1), :]
    for i in range(length // WIDE):
        wide = (i + 1) * WIDE
        start = running[:, i * WIDE : i * WIDE + 1]
        behind = jnp.exp(start - running[:, :wide]) * step[:, :wide]
        bands = []
        for part in range(each):
            here = i * each + part
            kind = kinds[here]
            weight = [level_weight(table, kind, head, level, heads) for level in range(5)]
            band = slice(here * stretch, (here + 1) * stretch)
            ahead = ahead_in[band, lanes]
            pieces = []
            for j in range(wide // TILE):
                first, second = 2 * j, 2 * j + 1
                if first > here:
                    pieces.append(empty)
                    continue
                left = weight[(here ^ first).bit_length()]
                right = weight[(here ^ second).bit_length()]
                if second > here or (here ^ first).bit_length() == (here ^ second).bit_length():
                    factor = left
                else:
                    factor = jnp.where(lane < stretch, left, right)
                tile = slice(j * TILE, (j + 1) * TILE)
                piece = scores[band, tile] * (behind[:, tile] * factor) * ahead
                if second >= here:
                    piece = jnp.where(causal[here - first], piece, 0.0)
                pieces.append(piece.astype(BF16))
            bands.append(jnp.concatenate(pieces, axis=1))
        emit(
            i,
            jnp.dot(
                jnp.concatenate(bands, axis=0), inner[:wide, lanes], preferred_element_type=F32
            ),
        )


def lift(table, kinds, lifted_base, head, tile, levels, held, WIDE=WIDE):
    length = lifted_base.shape[0]
    stretch = length // kinds.shape[0]
    lanes = pl.ds(pl.multiple_of(head * DIM, DIM), DIM)
    heads = lifted_base.shape[1] // DIM
    bands = []
    for here in range(tile * WIDE // stretch, (tile + 1) * WIDE // stretch):
        kind = kinds[here]
        base = lifted_base[here * stretch : (here + 1) * stretch, lanes]
        bands.append(
            jnp.concatenate(
                [(base * level_weight(table, kind, head, level, heads)).astype(BF16) for level in levels], axis=1
            )
        )
    return jnp.dot(jnp.concatenate(bands, axis=0), held[head], preferred_element_type=F32)


def mix_kernel(first, count, table, kinds, inner, running_in, step_in, scores, ahead_in, out):
    def one_head(offset, carry):
        lanes = pl.ds(pl.multiple_of(offset * DIM, DIM), DIM)

        def emit(i, value):
            out[i * WIDE : (i + 1) * WIDE, lanes] = value

        mix_head(
            first + offset, table, kinds, inner, running_in, step_in, scores, ahead_in, emit
        )
        return carry

    lax.fori_loop(0, count, one_head, 0, unroll=True)


def mix_part(first, count, table, kinds, inner, running, step, scores, ahead):
    length, width = inner.shape
    return pl.pallas_call(
        functools.partial(mix_kernel, first, count),
        in_specs=[SMEM, SMEM] + [VMEM] * 5,
        out_specs=VMEM,
        out_shape=pltpu.VMEM((length, count * DIM), F32),
        compiler_params=params(8),
        cost_estimate=cost(0.75 * count + 0.5),
        name="mix_part",
    )(table, kinds, inner, running, step, scores, ahead)


def turn_kernel(first, count, upper, *refs):
    table, kinds, inner, running_in, step_in, scores, ahead_in, gate = refs[:8]
    out, gates, table_here, kinds_here, sems = refs[-5:]
    _, z = block_place()

    @pl.when((z >= ZS // 2) == upper)
    def _():
        copies = [
            pltpu.make_async_copy(table, table_here, sems.at[0]),
            pltpu.make_async_copy(kinds, kinds_here, sems.at[1]),
        ]
        for copy in copies:
            copy.start()
        gates_kernel(gate, gates)
        for copy in copies:
            copy.wait()
        mix_kernel(
            first,
            count,
            table_here,
            kinds_here,
            inner,
            running_in,
            step_in,
            scores,
            ahead_in,
            out,
        )


def turn_part(first, count, upper, earlier, table, kinds, inner, running, step, scores, ahead, gate):
    length, width = inner.shape
    return pl.pallas_call(
        functools.partial(turn_kernel, first, count, upper),
        in_specs=[HBM, HBM] + [VMEM] * (6 + len(earlier)),
        out_specs=[VMEM] * 2,
        out_shape=[pltpu.VMEM((length, count * DIM), F32), pltpu.VMEM(gate.shape, F32)],
        scratch_shapes=[
            pltpu.SMEM(table.shape, F32),
            pltpu.SMEM(kinds.shape, jnp.int32),
            DMA((2,)),
        ],
        input_output_aliases={8: 0, 9: 1} if earlier else {},
        compiler_params=params(8),
        cost_estimate=cost(0.6 * count + 1.2 if upper else 0.2),
        name="turn_part",
    )(in_hbm(table), in_hbm(kinds), inner, running, step, scores, ahead, gate, *earlier)


def local_kernel(
    done,
    table,
    kinds,
    inner,
    running_in,
    step_in,
    scores,
    ahead_in,
    lifted_base,
    *rest,
):
    mixed = rest[:done]
    nears = rest[done : done + XS]
    out, held = rest[done + XS :]
    x, _ = block_place()
    length, width = inner.shape
    heads = width // DIM
    for k, near in enumerate(nears):
        pair = lax.rem(x + XS - k, XS)
        for head in range(PAIR):
            for level in range(NEAR):
                base = (level * PAIR + head) * DIM
                held[pair * PAIR + head, level * DIM : (level + 1) * DIM] = near[
                    base : base + DIM
                ]
    levels = range(5, 5 + NEAR)
    head = 0
    for value in mixed:
        for offset in range(value.shape[1] // DIM):
            for tile in range(length // WIDE):
                span = slice(tile * WIDE, (tile + 1) * WIDE)
                out[span, head * DIM : (head + 1) * DIM] = value[
                    span, offset * DIM : (offset + 1) * DIM
                ] + lift(table, kinds, lifted_base, head, tile, levels, held)
            head += 1

    def one_head(head, carry):
        lanes = pl.ds(pl.multiple_of(head * DIM, DIM), DIM)

        def emit(i, value):
            out[i * WIDE : (i + 1) * WIDE, lanes] = value + lift(
                table, kinds, lifted_base, head, i, levels, held
            )

        mix_head(head, table, kinds, inner, running_in, step_in, scores, ahead_in, emit)
        return carry

    lax.fori_loop(head, heads, one_head, 0, unroll=2)


def local_part(table, kinds, inner, running, step, scores, ahead, lifted_base, mixed, near):
    length, width = inner.shape
    heads = width // DIM
    return pl.pallas_call(
        functools.partial(local_kernel, len(mixed)),
        in_specs=[SMEM, SMEM] + [VMEM] * (6 + len(mixed) + XS),
        out_specs=VMEM,
        out_shape=pltpu.VMEM((length, width), F32),
        scratch_shapes=[pltpu.VMEM((heads, NEAR * DIM, DIM), BF16)],
        compiler_params=params(8),
        cost_estimate=cost(3.8),
        name="local_part",
    )(table, kinds, inner, running, step, scores, ahead, lifted_base, *mixed, *near)


def fold_row_kernel(p0, p1, p2, p3, row_out):
    x, _ = block_place()
    parts = (p0, p1, p2, p3)
    owner = [lax.rem(x + XS - k, XS) for k in range(XS)]
    decays = [decode_decay(part) for part in parts]
    later = [
        jnp.exp(sum(decays[m] * flag(owner[m] > owner[k]) for m in range(XS)))
        * decode_size(parts[k])
        for k in range(XS)
    ]
    total = sum(decays)
    states = []
    for head in range(PAIR):
        span = slice(head * DIM, (head + 1) * DIM)
        states.append(sum(parts[k][span] * later[k][head : head + 1] for k in range(XS)))
    encode(row_out, states, [total[head : head + 1] for head in range(PAIR)])


def fold_row(parts):
    return pl.pallas_call(
        fold_row_kernel,
        in_specs=[VMEM] * XS,
        out_specs=VMEM,
        out_shape=pltpu.VMEM((MESSAGE, DIM), F32),
        compiler_params=params(4),
        cost_estimate=cost(0.25),
        name="fold_row",
    )(*parts)


def fold_near_kernel(p0, p1, p2, p3, row_before, m0, m1, m2, m3):
    x, z = block_place()
    parts = (p0, p1, p2, p3)
    owner = [lax.rem(x + XS - k, XS) for k in range(XS)]
    decays = [decode_decay(part) for part in parts]
    sizes = [decode_size(part) for part in parts]
    odd_size = decode_size(row_before) * flag(lax.rem(z, 2) == 1)

    def pick(values, block):
        return sum(value * flag(owner[k] == block) for k, value in enumerate(values))

    decay_one = jnp.exp(pick(decays, 1))
    decay_two = jnp.exp(pick(decays, 2))
    for head in range(PAIR):
        span = slice(head * DIM, (head + 1) * DIM)
        row = slice(head, head + 1)
        scaled = [parts[k][span] * sizes[k][row] for k in range(XS)]
        first = pick(scaled, 0)
        third = pick(scaled, 2)
        joined = first * decay_one[row] + pick(scaled, 1)
        above = row_before[span]
        for k, message in enumerate((m0, m1, m2, m3)):
            target = lax.rem(x + k, XS)
            before = sum(decays[m][row] * flag(owner[m] < target) for m in range(XS))
            levels = (
                first * flag(target == 1) + third * flag(target == 3),
                joined * (flag(target == 2) + flag(target == 3) * decay_two[row]),
                above * (jnp.exp(before) * odd_size[row]),
            )
            for level, value in enumerate(levels):
                base = (level * PAIR + head) * DIM
                message[base : base + DIM] = value.astype(BF16)


def fold_near(parts, row_before):
    return pl.pallas_call(
        fold_near_kernel,
        in_specs=[VMEM] * (XS + 1),
        out_specs=[VMEM] * XS,
        out_shape=[pltpu.VMEM((NEAR * PAIR * DIM, DIM), BF16)] * XS,
        compiler_params=params(4),
        cost_estimate=cost(0.3),
        name="fold_near",
    )(*parts, row_before)


def fold_two_kernel(span_rows, own, other, out):
    _, z = block_place()
    upper = flag(lax.rem(lax.div(z, span_rows), 2) == 1)
    own_decay = decode_decay(own)
    other_decay = decode_decay(other)
    own_scale = jnp.exp(other_decay * (1.0 - upper)) * decode_size(own)
    other_scale = jnp.exp(own_decay * upper) * decode_size(other)
    decay = own_decay + other_decay
    states = []
    for head in range(PAIR):
        span = slice(head * DIM, (head + 1) * DIM)
        row = slice(head, head + 1)
        states.append(own[span] * own_scale[row] + other[span] * other_scale[row])
    encode(out, states, [decay[head : head + 1] for head in range(PAIR)])


def fold_two(span_rows, own, other):
    return pl.pallas_call(
        functools.partial(fold_two_kernel, span_rows),
        in_specs=[VMEM] * 2,
        out_specs=VMEM,
        out_shape=pltpu.VMEM((MESSAGE, DIM), F32),
        compiler_params=params(4),
        cost_estimate=cost(0.2),
        name="fold_two",
    )(own, other)


def fold_far_kernel(d0, d1, d2, d3, row_before, pair_before, quad_before, m0, m1, m2, m3):
    x, z = block_place()
    odd = flag(lax.rem(z, 2) == 1)
    odd_pair = flag(lax.rem(lax.div(z, 2), 2) == 1)
    upper = flag(z >= ZS // 2)
    decays = [decode_decay(part) for part in (d0, d1, d2, d3)]
    owner = [lax.rem(x + XS - k, XS) for k in range(XS)]
    in_pair = decode_decay(row_before) * odd
    in_quad = in_pair + decode_decay(pair_before) * odd_pair
    levels = (
        (pair_before, in_pair, decode_size(pair_before) * odd_pair),
        (quad_before, in_quad, decode_size(quad_before) * upper),
    )
    for k, message in enumerate((m0, m1, m2, m3)):
        target = lax.rem(x + k, XS)
        before = sum(decays[m] * flag(owner[m] < target) for m in range(XS))
        for level, (state, between, size) in enumerate(levels):
            factor = jnp.exp(before + between) * size
            for head in range(PAIR):
                base = (level * PAIR + head) * DIM
                message[base : base + DIM] = (
                    state[head * DIM : (head + 1) * DIM] * factor[head : head + 1]
                ).astype(BF16)


def fold_far(parts, befores):
    return pl.pallas_call(
        fold_far_kernel,
        in_specs=[VMEM] * (XS + 3),
        out_specs=[VMEM] * XS,
        out_shape=[pltpu.VMEM((FAR * PAIR * DIM, DIM), BF16)] * XS,
        compiler_params=params(4),
        cost_estimate=cost(0.25),
        name="fold_far",
    )(*parts, *befores)


def far_kernel(
    table, kinds, local, gates, lifted_base, f0, f1, f2, f3, gated, squares, held, total
):
    x, _ = block_place()
    length, width = local.shape
    heads = width // DIM
    for k, far in enumerate((f0, f1, f2, f3)):
        pair = lax.rem(x + XS - k, XS)
        for head in range(PAIR):
            for level in range(FAR):
                base = (level * PAIR + head) * DIM
                held[pair * PAIR + head, level * DIM : (level + 1) * DIM] = far[base : base + DIM]
    levels = range(5 + NEAR, 5 + NEAR + FAR)
    for pair in range(heads // 2):
        values = []
        for head in (2 * pair, 2 * pair + 1):
            lanes = slice(head * DIM, (head + 1) * DIM)
            mixed = local[:, lanes] + lift(
                table, kinds, lifted_base, head, 0, levels, held, length
            )
            value = mixed * gates[:, lanes]
            gated[:, lanes] = value
            values.append(value * value)
        if pair == 0:
            total[...] = values[0] + values[1]
        else:
            total[...] += values[0] + values[1]
    for tile in range(length // TILE):
        part = total[tile * TILE : (tile + 1) * TILE].T
        squares[tile : tile + 1] = jnp.sum(part, axis=0, keepdims=True)


def far_part(table, kinds, local, gates, lifted_base, far_states):
    length, width = local.shape
    heads = width // DIM
    return pl.pallas_call(
        far_kernel,
        in_specs=[SMEM, SMEM] + [VMEM] * (3 + XS),
        out_specs=[VMEM] * 2,
        out_shape=[pltpu.VMEM((length, width), F32), pltpu.VMEM((length // TILE, TILE), F32)],
        scratch_shapes=[pltpu.VMEM((heads, FAR * DIM, DIM), BF16), pltpu.VMEM((length, DIM), F32)],
        compiler_params=params(8),
        cost_estimate=cost(3.5),
        name="far_part",
    )(table, kinds, local, gates, lifted_base, *far_states)


def norm_kernel(total_width, gated, s0, s1, s2, s3, gain, out, made, sems):
    scale = lax.rsqrt((s0[...] + s1[...] + s2[...] + s3[...]) / total_width + 1e-05)
    length, width = gated.shape
    copies = []
    for tile in range(length // TILE):
        span = slice(tile * TILE, (tile + 1) * TILE)
        column = jnp.broadcast_to(scale[tile : tile + 1], (TILE, TILE)).T
        for piece in range(width // TILE):
            lane = slice(piece * TILE, (piece + 1) * TILE)
            made[span, lane] = (gated[span, lane] * column * gain[:, lane]).astype(BF16)
        copies.append(pltpu.make_async_copy(made.at[span], out.at[span], sems.at[tile]))
        copies[-1].start()
    for copy in copies:
        copy.wait()


def norm(gated, squares, gain, total_width):
    length, width = gated.shape
    return pl.pallas_call(
        functools.partial(norm_kernel, total_width),
        in_specs=[VMEM] * (2 + YS),
        out_specs=HBM,
        out_shape=jax.ShapeDtypeStruct((length, width), BF16),
        scratch_shapes=[pltpu.VMEM((length, width), BF16), DMA((length // TILE,))],
        compiler_params=params(8),
        cost_estimate=cost(1.6),
        name="norm",
    )(gated, *squares, gain)


def local(
    mixer_input,
    state_input,
    gate_input,
    step_raw,
    decay_rate,
    conv_inner,
    conv_state,
    level_table,
    stretch_kind,
    norm_gain,
):
    length, width = mixer_input.shape
    halo = lax.ppermute(
        last_rows(mixer_input, state_input), "seq", [(i, i + 1) for i in range(XS * ZS - 1)]
    )
    inner, keys, running, step, scale, first_rows, last, taps, *parts = prepare(
        mixer_input, state_input, conv_inner, conv_state, step_raw.T, decay_rate
    )
    inner, keys, *parts = finish(halo, first_rows, scale, last, taps, inner, keys, parts)
    table = jnp.transpose(level_table, (0, 2, 1))[:, :, :LEVELS].reshape(-1)
    moved = {
        k: sent(parts[k - 1], lambda z, x, k=k: (z, (x + k) % XS)) for k in (2, 1, 3)
    }
    arrived = [moved[k] for k in range(1, XS)]
    inner, scores, lifted_base, ahead, own_part = shared_part(
        mixer_input, state_input, halo, taps, scale, last, running, keys, inner
    )
    arrived = [own_part] + arrived
    mix = functools.partial(
        mix_part,
        table=table,
        kinds=stretch_kind,
        inner=inner,
        running=running,
        step=step,
        scores=scores,
        ahead=ahead,
    )
    row_state = fold_row(arrived)
    row_before = sent(row_state, lambda z, x: (z ^ 1, x))
    row_before, mixed_first = lax.optimization_barrier((row_before, mix(0, PAIR)))
    pair_state = fold_two(1, row_state, row_before)
    near = fold_near(arrived, row_before)
    pair_before = sent(pair_state, lambda z, x: (z ^ 2, x))
    near = [near[0]] + [along_x(near[k], k) for k in range(1, XS)]
    quad_state = fold_two(2, pair_state, pair_before)
    turn = functools.partial(
        turn_part,
        PAIR,
        2 * PAIR,
        table=table,
        kinds=stretch_kind,
        inner=inner,
        running=running,
        scores=scores,
        ahead=ahead,
        gate=gate_input,
    )
    quad_state, step_late = lax.optimization_barrier((quad_state, step))
    quad_state, *turned = lax.optimization_barrier(
        (quad_state, *turn(False, (), step=step_late))
    )
    quad_before = sent(quad_state, lambda z, x: (ZS - 1 - z, x) if z < ZS // 2 else None)
    quad_before, mixed_second, gates = lax.optimization_barrier(
        (quad_before, *turn(True, turned, step=step_late))
    )
    far = fold_far(arrived, (row_before, pair_before, quad_before))
    far = [far[0]] + [along_x(far[k], k) for k in range(1, XS)]
    local_out = local_part(
        table,
        stretch_kind,
        inner,
        running,
        step,
        scores,
        ahead,
        lifted_base,
        (mixed_first, mixed_second),
        near,
    )
    gated, squares = far_part(table, stretch_kind, local_out, gates, lifted_base, far)
    squares = squares + lax.ppermute(squares, "head", head_perm(lambda y, core: (y, 1 - core)))
    sums = [squares] + [
        lax.ppermute(squares, "head", head_perm(lambda y, core, k=k: ((y + k) % YS, core)))
        for k in (2, 1, 3)
    ]
    total_width = width * lax.axis_size("head")
    return norm(gated, sums, norm_gain[None, :], total_width)


def solution(mesh):
    return jax.shard_map(
        local,
        mesh=mesh,
        in_specs=(
            P("seq", "head"),
            P("seq", None),
            P("seq", "head"),
            P("seq", "head"),
            P("head"),
            P(None, "head"),
            P(),
            P(None, None, "head"),
            P("seq"),
            P("head"),
        ),
        out_specs=P("seq", "head"),
        check_vma=False,
    )
```

```python
import functools
import jax
import jax.numpy as jnp
from jax import lax
from jax.experimental import pallas as pl
from jax.experimental.pallas import tpu as pltpu
from jax.sharding import PartitionSpec as P

F32 = jnp.float32
BF16 = jnp.bfloat16

XS = 4
ZS = 8
YS = 4
CORES = 2
PAIR = 2
DIM = 128
HALO = 16
TILE = 128
WIDE = 256
NEAR = 3
FAR = 2
LEVELS = 5 + NEAR + FAR
TOP = 16384.0
MESSAGE = PAIR * DIM + 8


def seq_perm(move):
    pairs = []
    for z in range(ZS):
        for x in range(XS):
            target = move(z, x)
            if target is not None:
                pairs.append((z * XS + x, target[0] * XS + target[1]))
    return pairs


def head_perm(move):
    pairs = []
    for y in range(YS):
        for core in range(CORES):
            target = move(y, core)
            pairs.append((y * CORES + core, target[0] * CORES + target[1]))
    return pairs


def along_x(value, step):
    return lax.ppermute(value, "seq", seq_perm(lambda z, x: (z, (x + step) % XS)))


def sent(message, move):
    return lax.ppermute(message.astype(jnp.float16), "seq", seq_perm(move)).astype(F32)


def silu_of_twice(half):
    return half + half * jnp.tanh(half)


def silu(value):
    return silu_of_twice(0.5 * value)


VMEM = pl.BlockSpec(memory_space=pltpu.VMEM)
SMEM = pl.BlockSpec(memory_space=pltpu.SMEM)
HBM = pl.BlockSpec(memory_space=pltpu.HBM)
DMA = pltpu.SemaphoreType.DMA


def params(mebibytes):
    return pltpu.CompilerParams(vmem_limit_bytes=mebibytes * 2**20)


def cost(microseconds):
    return pl.CostEstimate(
        flops=int(microseconds * 1.15e9),
        bytes_accessed=int(microseconds * 3.6e6),
        transcendentals=0,
    )


def in_hbm(value):
    return pltpu.with_memory_space_constraint(value, pltpu.HBM)


def block_place():
    index = lax.axis_index("seq")
    return lax.rem(index, XS), lax.div(index, XS)


def conv(block, halo, taps, pad):
    length, width = block.shape
    count = taps.shape[0]
    taps = 0.5 * taps.astype(F32)
    columns = []
    for lane in range(width // DIM):
        lanes = slice(lane * DIM, (lane + 1) * DIM)
        pad[lane, :8] = halo[HALO - 8 :, lanes].astype(F32)
        pad[lane, 8 : 8 + length] = block[:, lanes].astype(F32)
        made = []
        for base in range(0, length, TILE):
            size = min(TILE, length)
            total = jnp.zeros((size, DIM), F32)
            for offset in range(count):
                first = base + 9 - count + offset
                total = total + pad[lane, first : first + size] * taps[offset : offset + 1, lanes]
            made.append(silu_of_twice(total).astype(BF16))
        columns.append(jnp.concatenate(made, axis=0))
    return jnp.concatenate(columns, axis=1)


def flag(condition):
    return jnp.where(condition, 1.0, 0.0).astype(F32)


def encode(message, states, decays):
    spot = lax.broadcasted_iota(jnp.int32, (8, DIM), 0)
    tail = jnp.zeros((8, DIM), F32)
    for head in range(PAIR):
        state, decay = states[head], decays[head]
        coarse = jnp.floor(decay)
        middle = jnp.floor((decay - coarse) * 1024.0) / 1024.0
        rest = decay - coarse - middle
        most = jnp.max(jnp.max(jnp.abs(state), axis=0, keepdims=True), axis=1, keepdims=True)
        power = jnp.ceil(jnp.log(jnp.maximum(most, 1e-30)))
        message[head * DIM : (head + 1) * DIM] = state * (jnp.exp(-power) * TOP)
        for index, value in enumerate((coarse, middle, rest, power)):
            tail = jnp.where(spot == PAIR * index + head, value, tail)
    message[PAIR * DIM :] = tail


def decode_decay(message):
    tail = message[PAIR * DIM :]
    return tail[:PAIR] + tail[PAIR : 2 * PAIR] + tail[2 * PAIR : 3 * PAIR]


def decode_size(message):
    return jnp.exp(message[PAIR * DIM :][3 * PAIR :]) / TOP


def tails_kernel(mixer, state, out, sems):
    length, width = mixer.shape
    span = pl.ds(length - HALO, HALO)
    copies = [
        pltpu.make_async_copy(mixer.at[span], out.at[:, :width], sems.at[0]),
        pltpu.make_async_copy(state.at[span], out.at[:, width:], sems.at[1]),
    ]
    for copy in copies:
        copy.start()
    for copy in copies:
        copy.wait()


def last_rows(mixer, state):
    return pl.pallas_call(
        tails_kernel,
        in_specs=[HBM, HBM],
        out_specs=VMEM,
        out_shape=pltpu.VMEM((HALO, mixer.shape[1] + state.shape[1]), BF16),
        scratch_shapes=[DMA((2,))],
        compiler_params=params(2),
        name="last_rows",
    )(in_hbm(mixer), in_hbm(state))


def prepare_kernel(
    mixer,
    state,
    taps,
    state_taps,
    step_raw,
    rate,
    inner,
    keys,
    running_out,
    step_out,
    scale,
    first_rows,
    last,
    taps_here,
    part1,
    part2,
    part3,
    mixer_here,
    keys_here,
    raw_here,
    rate_here,
    keys_t,
    late_scale,
    pad,
    mixer_sem,
    small_sem,
):
    x, _ = block_place()
    heads, length = step_raw.shape
    width = mixer.shape[1]
    wide = PAIR * DIM
    head_span = pl.ds(0, HALO)
    small = [
        pltpu.make_async_copy(source, target, small_sem.at[n])
        for n, (source, target) in enumerate(
            (
                (step_raw, raw_here),
                (rate, rate_here),
                (state.at[:, :DIM], keys_here),
                (state_taps, taps_here.at[:, width:]),
                (taps, taps_here.at[:, :width]),
                (state.at[head_span], first_rows.at[:, width:]),
                (mixer.at[head_span], first_rows.at[:, :width]),
            )
        )
    ]
    for copy in small[:5]:
        copy.start()
    pairs = [lax.rem(x + turn, XS) for turn in range(1, XS)]
    columns = [pl.ds(pl.multiple_of(pair * wide, wide), wide) for pair in pairs]
    large = [
        pltpu.make_async_copy(mixer.at[:, columns[turn]], mixer_here.at[turn], mixer_sem.at[turn])
        for turn in range(XS - 1)
    ]
    for copy in large + small[5:]:
        copy.start()

    for copy in small[:5]:
        copy.wait()
    raw = raw_here[...]
    step = jnp.maximum(raw, 0.0) + jnp.log1p(jnp.exp(-jnp.abs(raw)))
    spot = lax.broadcasted_iota(jnp.int32, (heads, length), 0)
    rates = jnp.zeros((heads, length), F32)
    for head in range(heads):
        rates = jnp.where(spot == head, rate_here[head], rates)
    running = -rates * step
    lane = lax.broadcasted_iota(jnp.int32, (heads, length), 1)
    shift = 1
    while shift < length:
        moved = pltpu.roll(running, shift, axis=1)
        running = running + jnp.where(lane >= shift, moved, 0.0)
        shift *= 2
    final = running[:, length - 1 :]
    running_out[...] = running
    step_out[...] = step
    scaled = jnp.exp(final - running) * step
    scale[...] = scaled
    late_scale[...] = jnp.where(lane < HALO, 0.0, scaled)
    last[...] = jnp.broadcast_to(final, last.shape)
    nothing = jnp.zeros((HALO, wide), BF16)
    made = conv(keys_here, nothing, taps_here[:, width : width + DIM], pad)
    keys[...] = made
    keys_t[...] = made.astype(F32).T

    for turn, part in enumerate((part1, part2, part3)):
        large[turn].wait()
        values = conv(mixer_here.at[turn], nothing, taps_here[:, columns[turn]], pad)
        inner[:, columns[turn]] = values
        for head in range(PAIR):
            row = late_scale[pl.ds(pairs[turn] * PAIR + head, 1), :]
            scaled_t = (keys_t[...] * row).astype(BF16)
            part[head * DIM : (head + 1) * DIM] = jnp.dot(
                scaled_t, values[:, head * DIM : (head + 1) * DIM], preferred_element_type=F32
            )
    for copy in small[5:]:
        copy.wait()


def prepare(mixer, state, taps, state_taps, step_raw_t, rate):
    length, width = mixer.shape
    heads = step_raw_t.shape[0]
    every = width + 2 * DIM
    by_token = pltpu.VMEM((heads, length), F32)
    return pl.pallas_call(
        prepare_kernel,
        in_specs=[HBM] * 6,
        out_specs=[VMEM] * (7 + XS),
        out_shape=[
            pltpu.VMEM((length, width), BF16),
            pltpu.VMEM((length, DIM), BF16),
            by_token,
            by_token,
            by_token,
            pltpu.VMEM((HALO, every), BF16),
            pltpu.VMEM((heads, DIM), F32),
            pltpu.VMEM((taps.shape[0], every), BF16),
        ]
        + [pltpu.VMEM((PAIR * DIM, DIM), F32)] * (XS - 1),
        scratch_shapes=[
            pltpu.VMEM((XS - 1, length, PAIR * DIM), BF16),
            pltpu.VMEM((length, DIM), BF16),
            by_token,
            pltpu.SMEM((heads,), F32),
            pltpu.VMEM((DIM, length), F32),
            by_token,
            pltpu.VMEM((PAIR, length + 8, DIM), F32),
            DMA((XS - 1,)),
            DMA((7,)),
        ],
        compiler_params=params(16),
        cost_estimate=cost(4.5),
        name="prepare",
    )(
        in_hbm(mixer),
        in_hbm(state),
        in_hbm(taps),
        in_hbm(state_taps),
        in_hbm(step_raw_t),
        in_hbm(rate),
    )


def finish_kernel(
    halo,
    first_rows,
    scale,
    last,
    taps,
    inner_in,
    keys_in,
    p1,
    p2,
    p3,
    inner,
    keys,
    m1,
    m2,
    m3,
    pad,
):
    x, _ = block_place()
    width = inner.shape[1]
    heads = width // DIM
    wide = PAIR * DIM
    states = slice(width, width + DIM)
    made = conv(first_rows.at[:, states], halo[:, states], taps[:, states], pad)
    keys[:HALO] = made
    early = made.astype(F32)
    columns = scale[:, :DIM].T
    scaled = [
        (early * jnp.broadcast_to(columns[:HALO, head : head + 1], (HALO, DIM))).astype(BF16)
        for head in range(heads)
    ]
    added = []
    for pair in range(XS):
        lanes = slice(pair * wide, (pair + 1) * wide)
        values = conv(first_rows.at[:, lanes], halo[:, lanes], taps[:, lanes], pad)
        inner[:HALO, lanes] = values
        for head in range(PAIR):
            added.append(
                lax.dot_general(
                    scaled[pair * PAIR + head],
                    values[:, head * DIM : (head + 1) * DIM],
                    (((0,), (0,)), ((), ())),
                    preferred_element_type=F32,
                )
            )
    for turn, (part, message) in enumerate(((p1, m1), (p2, m2), (p3, m3)), start=1):
        pair = lax.rem(x + turn, XS)
        totals = []
        decays = []
        for head in range(PAIR):
            extra = sum(
                added[other * PAIR + head] * flag(pair == other) for other in range(XS)
            )
            totals.append(part[head * DIM : (head + 1) * DIM] + extra)
            decays.append(last[pl.ds(pair * PAIR + head, 1), :])
        encode(message, totals, decays)


def finish(halo, first_rows, scale, last, taps, inner, keys, parts):
    return pl.pallas_call(
        finish_kernel,
        in_specs=[VMEM] * (6 + XS),
        out_specs=[VMEM] * (1 + XS),
        out_shape=[pltpu.VMEM(inner.shape, BF16), pltpu.VMEM(keys.shape, BF16)]
        + [pltpu.VMEM((MESSAGE, DIM), F32)] * (XS - 1),
        scratch_shapes=[pltpu.VMEM((PAIR, HALO + 8, DIM), F32)],
        input_output_aliases={5: 0, 6: 1},
        compiler_params=params(4),
        cost_estimate=cost(0.75),
        name="finish",
    )(halo, first_rows, scale, last, taps, inner, keys, *parts)


def shared_kernel(
    mixer,
    state,
    halo,
    taps,
    scale,
    last,
    running_in,
    keys,
    inner_in,
    inner,
    scores,
    lifted_base,
    ahead_out,
    message,
    mixer_here,
    state_here,
    queries,
    keys_t,
    pad,
    sems,
):
    x, _ = block_place()
    length, width = inner.shape
    heads = width // DIM
    tiles = length // TILE
    wide = PAIR * DIM
    own = pl.ds(pl.multiple_of(x * wide, wide), wide)
    copies = [
        pltpu.make_async_copy(state.at[:, DIM:], state_here, sems.at[0]),
        pltpu.make_async_copy(mixer.at[:, own], mixer_here, sems.at[1]),
    ]
    for copy in copies:
        copy.start()
    running = running_in[...]
    columns = jnp.exp(running).T
    ahead = jnp.concatenate(
        [
            jnp.exp(running[:, i * WIDE : (i + 1) * WIDE] - running[:, i * WIDE : i * WIDE + 1])
            for i in range(length // WIDE)
        ],
        axis=1,
    ).T
    keys_t[...] = keys[...].astype(F32).T
    for i in range(tiles):
        span = slice(i * TILE, (i + 1) * TILE)
        for head in range(heads):
            ahead_out[span, head * DIM : (head + 1) * DIM] = jnp.broadcast_to(
                ahead[span, head : head + 1], (TILE, DIM)
            )
    for copy in copies:
        copy.wait()
    states = slice(width + DIM, width + 2 * DIM)
    queries[...] = conv(state_here, halo[:, states], taps[:, states], pad)
    values = conv(mixer_here, halo[:, own], taps[:, own], pad)
    inner[:, own] = values
    totals = []
    decays = []
    for offset in range(PAIR):
        head = pl.ds(x * PAIR + offset, 1)
        totals.append(
            jnp.dot(
                (keys_t[...] * scale[head, :]).astype(BF16),
                values[:, offset * DIM : (offset + 1) * DIM],
                preferred_element_type=F32,
            )
        )
        decays.append(last[head, :])
    encode(message, totals, decays)
    for i in range(tiles):
        span = slice(i * TILE, (i + 1) * TILE)
        end = (i + 1) * TILE
        scores[span, :end] = lax.dot_general(
            queries[span],
            keys[:end],
            (((1,), (1,)), ((), ())),
            preferred_element_type=F32,
        )
        here = queries[span].astype(F32)
        for head in range(heads):
            lifted_base[span, head * DIM : (head + 1) * DIM] = here * jnp.broadcast_to(
                columns[span, head : head + 1], (TILE, DIM)
            )


def shared_part(mixer, state, halo, taps, scale, last, running, keys, inner):
    length, width = inner.shape
    return pl.pallas_call(
        shared_kernel,
        in_specs=[HBM, HBM] + [VMEM] * 7,
        out_specs=[VMEM] * 5,
        out_shape=[
            pltpu.VMEM((length, width), BF16),
            pltpu.VMEM((length, length), F32),
            pltpu.VMEM((length, width), F32),
            pltpu.VMEM((length, width), F32),
            pltpu.VMEM((MESSAGE, DIM), F32),
        ],
        scratch_shapes=[
            pltpu.VMEM((length, PAIR * DIM), BF16),
            pltpu.VMEM((length, DIM), BF16),
            pltpu.VMEM((length, DIM), BF16),
            pltpu.VMEM((DIM, length), F32),
            pltpu.VMEM((PAIR, length + 8, DIM), F32),
            DMA((2,)),
        ],
        input_output_aliases={8: 0},
        compiler_params=params(8),
        cost_estimate=cost(3.4),
        name="shared_part",
    )(in_hbm(mixer), in_hbm(state), halo, taps, scale, last, running, keys, inner)


def gates_kernel(gate, gates):
    length, width = gate.shape

    def one_tile(tile, carry):
        span = pl.ds(pl.multiple_of(tile * TILE, TILE), TILE)
        for piece in range(width // DIM):
            lane = slice(piece * DIM, (piece + 1) * DIM)
            gates[span, lane] = silu(gate[span, lane].astype(F32))
        return carry

    lax.fori_loop(0, length // TILE, one_tile, 0)


def level_weight(table, kind, head, level, heads):
    return table[(kind * heads + head) * LEVELS + level]


def mix_head(head, table, kinds, inner, running_in, step_in, scores, ahead_in, emit):
    length = inner.shape[0]
    heads = inner.shape[1] // DIM
    stretch = length // kinds.shape[0]
    each = WIDE // stretch
    row = lax.broadcasted_iota(jnp.int32, (stretch, TILE), 0)
    column = lax.broadcasted_iota(jnp.int32, (stretch, TILE), 1)
    causal = [row + part * stretch >= column for part in range(TILE // stretch)]
    lane = lax.broadcasted_iota(jnp.int32, (1, TILE), 1)
    empty = jnp.zeros((stretch, TILE), BF16)
    lanes = pl.ds(pl.multiple_of(head * DIM, DIM), DIM)
    running = running_in[pl.ds(head, 1), :]
    step = step_in[pl.ds(head, 1), :]
    for i in range(length // WIDE):
        wide = (i + 1) * WIDE
        start = running[:, i * WIDE : i * WIDE + 1]
        behind = jnp.exp(start - running[:, :wide]) * step[:, :wide]
        bands = []
        for part in range(each):
            here = i * each + part
            kind = kinds[here]
            weight = [level_weight(table, kind, head, level, heads) for level in range(5)]
            band = slice(here * stretch, (here + 1) * stretch)
            ahead = ahead_in[band, lanes]
            pieces = []
            for j in range(wide // TILE):
                first, second = 2 * j, 2 * j + 1
                if first > here:
                    pieces.append(empty)
                    continue
                left = weight[(here ^ first).bit_length()]
                right = weight[(here ^ second).bit_length()]
                if second > here or (here ^ first).bit_length() == (here ^ second).bit_length():
                    factor = left
                else:
                    factor = jnp.where(lane < stretch, left, right)
                tile = slice(j * TILE, (j + 1) * TILE)
                piece = scores[band, tile] * (behind[:, tile] * factor) * ahead
                if second >= here:
                    piece = jnp.where(causal[here - first], piece, 0.0)
                pieces.append(piece.astype(BF16))
            bands.append(jnp.concatenate(pieces, axis=1))
        emit(
            i,
            jnp.dot(
                jnp.concatenate(bands, axis=0), inner[:wide, lanes], preferred_element_type=F32
            ),
        )


def lift_operand(table, kinds, lifted_base, head, tile, levels, size):
    length = lifted_base.shape[0]
    stretch = length // kinds.shape[0]
    lanes = pl.ds(pl.multiple_of(head * DIM, DIM), DIM)
    heads = lifted_base.shape[1] // DIM
    bands = []
    for here in range(tile * size // stretch, (tile + 1) * size // stretch):
        kind = kinds[here]
        base = lifted_base[here * stretch : (here + 1) * stretch, lanes]
        bands.append(
            jnp.concatenate(
                [
                    (base * level_weight(table, kind, head, level, heads)).astype(BF16)
                    for level in levels
                ],
                axis=1,
            )
        )
    return jnp.concatenate(bands, axis=0)


def lift(table, kinds, lifted_base, head, tile, levels, held):
    operand = lift_operand(table, kinds, lifted_base, head, tile, levels, WIDE)
    return jnp.dot(operand, held[head], preferred_element_type=F32)


def mix_kernel(first, count, table, kinds, inner, running_in, step_in, scores, ahead_in, out):
    def one_head(offset, carry):
        lanes = pl.ds(pl.multiple_of(offset * DIM, DIM), DIM)

        def emit(i, value):
            out[i * WIDE : (i + 1) * WIDE, lanes] = value

        mix_head(
            first + offset, table, kinds, inner, running_in, step_in, scores, ahead_in, emit
        )
        return carry

    lax.fori_loop(0, count, one_head, 0, unroll=True)


def mix_part(first, count, table, kinds, inner, running, step, scores, ahead):
    length, width = inner.shape
    return pl.pallas_call(
        functools.partial(mix_kernel, first, count),
        in_specs=[SMEM, SMEM] + [VMEM] * 5,
        out_specs=VMEM,
        out_shape=pltpu.VMEM((length, count * DIM), F32),
        compiler_params=params(8),
        cost_estimate=cost(0.75 * count + 0.5),
        name="mix_part",
    )(table, kinds, inner, running, step, scores, ahead)


def turn_kernel(first, count, upper, *refs):
    table, kinds, inner, running_in, step_in, scores, ahead_in, gate = refs[:8]
    out, gates, table_here, kinds_here, sems = refs[-5:]
    _, z = block_place()

    @pl.when((z >= ZS // 2) == upper)
    def _():
        copies = [
            pltpu.make_async_copy(table, table_here, sems.at[0]),
            pltpu.make_async_copy(kinds, kinds_here, sems.at[1]),
        ]
        for copy in copies:
            copy.start()
        gates_kernel(gate, gates)
        for copy in copies:
            copy.wait()
        mix_kernel(
            first,
            count,
            table_here,
            kinds_here,
            inner,
            running_in,
            step_in,
            scores,
            ahead_in,
            out,
        )


def turn_part(first, count, upper, earlier, table, kinds, inner, running, step, scores, ahead, gate):
    length, width = inner.shape
    return pl.pallas_call(
        functools.partial(turn_kernel, first, count, upper),
        in_specs=[HBM, HBM] + [VMEM] * (6 + len(earlier)),
        out_specs=[VMEM] * 2,
        out_shape=[pltpu.VMEM((length, count * DIM), F32), pltpu.VMEM(gate.shape, F32)],
        scratch_shapes=[
            pltpu.SMEM(table.shape, F32),
            pltpu.SMEM(kinds.shape, jnp.int32),
            DMA((2,)),
        ],
        input_output_aliases={8: 0, 9: 1} if earlier else {},
        compiler_params=params(8),
        cost_estimate=cost(0.6 * count + 1.2 if upper else 0.2),
        name="turn_part",
    )(in_hbm(table), in_hbm(kinds), inner, running, step, scores, ahead, gate, *earlier)


def local_kernel(
    done,
    table,
    kinds,
    inner,
    running_in,
    step_in,
    scores,
    ahead_in,
    lifted_base,
    *rest,
):
    mixed = rest[:done]
    nears = rest[done : done + XS]
    out, lifted_far, held = rest[done + XS :]
    x, _ = block_place()
    length, width = inner.shape
    heads = width // DIM
    for k, near in enumerate(nears):
        pair = lax.rem(x + XS - k, XS)
        for head in range(PAIR):
            for level in range(NEAR):
                base = (level * PAIR + head) * DIM
                held[pair * PAIR + head, level * DIM : (level + 1) * DIM] = near[
                    base : base + DIM
                ]
    levels = range(5, 5 + NEAR)
    head = 0
    for value in mixed:
        for offset in range(value.shape[1] // DIM):
            for tile in range(length // WIDE):
                span = slice(tile * WIDE, (tile + 1) * WIDE)
                out[span, head * DIM : (head + 1) * DIM] = value[
                    span, offset * DIM : (offset + 1) * DIM
                ] + lift(table, kinds, lifted_base, head, tile, levels, held)
            head += 1

    def one_head(head, carry):
        lanes = pl.ds(pl.multiple_of(head * DIM, DIM), DIM)

        def emit(i, value):
            out[i * WIDE : (i + 1) * WIDE, lanes] = value + lift(
                table, kinds, lifted_base, head, i, levels, held
            )

        mix_head(head, table, kinds, inner, running_in, step_in, scores, ahead_in, emit)
        return carry

    lax.fori_loop(head, heads, one_head, 0, unroll=2)
    far_levels = range(5 + NEAR, 5 + NEAR + FAR)
    for head in range(heads):
        lifted_far[:, head * FAR * DIM : (head + 1) * FAR * DIM] = lift_operand(
            table, kinds, lifted_base, head, 0, far_levels, length
        )


def local_part(table, kinds, inner, running, step, scores, ahead, lifted_base, mixed, near):
    length, width = inner.shape
    heads = width // DIM
    return pl.pallas_call(
        functools.partial(local_kernel, len(mixed)),
        in_specs=[SMEM, SMEM] + [VMEM] * (6 + len(mixed) + XS),
        out_specs=[VMEM] * 2,
        out_shape=[pltpu.VMEM((length, width), F32), pltpu.VMEM((length, FAR * width), BF16)],
        scratch_shapes=[pltpu.VMEM((heads, NEAR * DIM, DIM), BF16)],
        compiler_params=params(8),
        cost_estimate=cost(3.8),
        name="local_part",
    )(table, kinds, inner, running, step, scores, ahead, lifted_base, *mixed, *near)


def fold_row_kernel(p0, p1, p2, p3, row_out):
    x, _ = block_place()
    parts = (p0, p1, p2, p3)
    owner = [lax.rem(x + XS - k, XS) for k in range(XS)]
    decays = [decode_decay(part) for part in parts]
    later = [
        jnp.exp(sum(decays[m] * flag(owner[m] > owner[k]) for m in range(XS)))
        * decode_size(parts[k])
        for k in range(XS)
    ]
    total = sum(decays)
    states = []
    for head in range(PAIR):
        span = slice(head * DIM, (head + 1) * DIM)
        states.append(sum(parts[k][span] * later[k][head : head + 1] for k in range(XS)))
    encode(row_out, states, [total[head : head + 1] for head in range(PAIR)])


def fold_row(parts):
    return pl.pallas_call(
        fold_row_kernel,
        in_specs=[VMEM] * XS,
        out_specs=VMEM,
        out_shape=pltpu.VMEM((MESSAGE, DIM), F32),
        compiler_params=params(4),
        cost_estimate=cost(0.25),
        name="fold_row",
    )(*parts)


def fold_near_kernel(p0, p1, p2, p3, row_before, m0, m1, m2, m3):
    x, z = block_place()
    parts = (p0, p1, p2, p3)
    owner = [lax.rem(x + XS - k, XS) for k in range(XS)]
    decays = [decode_decay(part) for part in parts]
    sizes = [decode_size(part) for part in parts]
    odd_size = decode_size(row_before) * flag(lax.rem(z, 2) == 1)

    def pick(values, block):
        return sum(value * flag(owner[k] == block) for k, value in enumerate(values))

    decay_one = jnp.exp(pick(decays, 1))
    decay_two = jnp.exp(pick(decays, 2))
    for head in range(PAIR):
        span = slice(head * DIM, (head + 1) * DIM)
        row = slice(head, head + 1)
        scaled = [parts[k][span] * sizes[k][row] for k in range(XS)]
        first = pick(scaled, 0)
        third = pick(scaled, 2)
        joined = first * decay_one[row] + pick(scaled, 1)
        above = row_before[span]
        for k, message in enumerate((m0, m1, m2, m3)):
            target = lax.rem(x + k, XS)
            before = sum(decays[m][row] * flag(owner[m] < target) for m in range(XS))
            levels = (
                first * flag(target == 1) + third * flag(target == 3),
                joined * (flag(target == 2) + flag(target == 3) * decay_two[row]),
                above * (jnp.exp(before) * odd_size[row]),
            )
            for level, value in enumerate(levels):
                base = (level * PAIR + head) * DIM
                message[base : base + DIM] = value.astype(BF16)


def fold_near(parts, row_before):
    return pl.pallas_call(
        fold_near_kernel,
        in_specs=[VMEM] * (XS + 1),
        out_specs=[VMEM] * XS,
        out_shape=[pltpu.VMEM((NEAR * PAIR * DIM, DIM), BF16)] * XS,
        compiler_params=params(4),
        cost_estimate=cost(0.3),
        name="fold_near",
    )(*parts, row_before)


def fold_two_kernel(span_rows, own, other, out):
    _, z = block_place()
    upper = flag(lax.rem(lax.div(z, span_rows), 2) == 1)
    own_decay = decode_decay(own)
    other_decay = decode_decay(other)
    own_scale = jnp.exp(other_decay * (1.0 - upper)) * decode_size(own)
    other_scale = jnp.exp(own_decay * upper) * decode_size(other)
    decay = own_decay + other_decay
    states = []
    for head in range(PAIR):
        span = slice(head * DIM, (head + 1) * DIM)
        row = slice(head, head + 1)
        states.append(own[span] * own_scale[row] + other[span] * other_scale[row])
    encode(out, states, [decay[head : head + 1] for head in range(PAIR)])


def fold_two(span_rows, own, other):
    return pl.pallas_call(
        functools.partial(fold_two_kernel, span_rows),
        in_specs=[VMEM] * 2,
        out_specs=VMEM,
        out_shape=pltpu.VMEM((MESSAGE, DIM), F32),
        compiler_params=params(4),
        cost_estimate=cost(0.2),
        name="fold_two",
    )(own, other)


def fold_far_kernel(d0, d1, d2, d3, row_before, pair_before, quad_before, m0, m1, m2, m3):
    x, z = block_place()
    odd = flag(lax.rem(z, 2) == 1)
    odd_pair = flag(lax.rem(lax.div(z, 2), 2) == 1)
    upper = flag(z >= ZS // 2)
    decays = [decode_decay(part) for part in (d0, d1, d2, d3)]
    owner = [lax.rem(x + XS - k, XS) for k in range(XS)]
    in_pair = decode_decay(row_before) * odd
    in_quad = in_pair + decode_decay(pair_before) * odd_pair
    levels = (
        (pair_before, in_pair, decode_size(pair_before) * odd_pair),
        (quad_before, in_quad, decode_size(quad_before) * upper),
    )
    for k, message in enumerate((m0, m1, m2, m3)):
        target = lax.rem(x + k, XS)
        before = sum(decays[m] * flag(owner[m] < target) for m in range(XS))
        for level, (state, between, size) in enumerate(levels):
            factor = jnp.exp(before + between) * size
            for head in range(PAIR):
                base = (level * PAIR + head) * DIM
                message[base : base + DIM] = (
                    state[head * DIM : (head + 1) * DIM] * factor[head : head + 1]
                ).astype(BF16)


def fold_far(parts, befores):
    return pl.pallas_call(
        fold_far_kernel,
        in_specs=[VMEM] * (XS + 3),
        out_specs=[VMEM] * XS,
        out_shape=[pltpu.VMEM((FAR * PAIR * DIM, DIM), BF16)] * XS,
        compiler_params=params(4),
        cost_estimate=cost(0.25),
        name="fold_far",
    )(*parts, *befores)


def far_kernel(local, gates, lifted, f0, f1, f2, f3, gated, squares, held, total):
    x, _ = block_place()
    length, width = local.shape
    heads = width // DIM
    for k, far in enumerate((f0, f1, f2, f3)):
        pair = lax.rem(x + XS - k, XS)
        for head in range(PAIR):
            for level in range(FAR):
                base = (level * PAIR + head) * DIM
                held[pair * PAIR + head, level * DIM : (level + 1) * DIM] = far[base : base + DIM]
    for pair in range(heads // 2):
        values = []
        for head in (2 * pair, 2 * pair + 1):
            lanes = slice(head * DIM, (head + 1) * DIM)
            mixed = local[:, lanes] + jnp.dot(
                lifted[:, head * FAR * DIM : (head + 1) * FAR * DIM],
                held[head],
                preferred_element_type=F32,
            )
            value = mixed * gates[:, lanes]
            gated[:, lanes] = value
            values.append(value * value)
        if pair == 0:
            total[...] = values[0] + values[1]
        else:
            total[...] += values[0] + values[1]
    for tile in range(length // TILE):
        part = total[tile * TILE : (tile + 1) * TILE].T
        squares[tile : tile + 1] = jnp.sum(part, axis=0, keepdims=True)


def far_part(local, gates, lifted, far_states):
    length, width = local.shape
    heads = width // DIM
    return pl.pallas_call(
        far_kernel,
        in_specs=[VMEM] * (3 + XS),
        out_specs=[VMEM] * 2,
        out_shape=[pltpu.VMEM((length, width), F32), pltpu.VMEM((length // TILE, TILE), F32)],
        scratch_shapes=[pltpu.VMEM((heads, FAR * DIM, DIM), BF16), pltpu.VMEM((length, DIM), F32)],
        compiler_params=params(8),
        cost_estimate=cost(3.5),
        name="far_part",
    )(local, gates, lifted, *far_states)


def norm_kernel(total_width, gated, s0, s1, s2, s3, gain, out, made, sems):
    scale = lax.rsqrt((s0[...] + s1[...] + s2[...] + s3[...]) / total_width + 1e-05)
    length, width = gated.shape
    copies = []
    for tile in range(length // TILE):
        span = slice(tile * TILE, (tile + 1) * TILE)
        column = jnp.broadcast_to(scale[tile : tile + 1], (TILE, TILE)).T
        for piece in range(width // TILE):
            lane = slice(piece * TILE, (piece + 1) * TILE)
            made[span, lane] = (gated[span, lane] * column * gain[:, lane]).astype(BF16)
        copies.append(pltpu.make_async_copy(made.at[span], out.at[span], sems.at[tile]))
        copies[-1].start()
    for copy in copies:
        copy.wait()


def norm(gated, squares, gain, total_width):
    length, width = gated.shape
    return pl.pallas_call(
        functools.partial(norm_kernel, total_width),
        in_specs=[VMEM] * (2 + YS),
        out_specs=HBM,
        out_shape=jax.ShapeDtypeStruct((length, width), BF16),
        scratch_shapes=[pltpu.VMEM((length, width), BF16), DMA((length // TILE,))],
        compiler_params=params(8),
        cost_estimate=cost(1.6),
        name="norm",
    )(gated, *squares, gain)


def local(
    mixer_input,
    state_input,
    gate_input,
    step_raw,
    decay_rate,
    conv_inner,
    conv_state,
    level_table,
    stretch_kind,
    norm_gain,
):
    length, width = mixer_input.shape
    halo = lax.ppermute(
        last_rows(mixer_input, state_input), "seq", [(i, i + 1) for i in range(XS * ZS - 1)]
    )
    inner, keys, running, step, scale, first_rows, last, taps, *parts = prepare(
        mixer_input, state_input, conv_inner, conv_state, step_raw.T, decay_rate
    )
    inner, keys, *parts = finish(halo, first_rows, scale, last, taps, inner, keys, parts)
    table = jnp.transpose(level_table, (0, 2, 1))[:, :, :LEVELS].reshape(-1)
    moved = {
        k: sent(parts[k - 1], lambda z, x, k=k: (z, (x + k) % XS)) for k in (2, 1, 3)
    }
    arrived = [moved[k] for k in range(1, XS)]
    inner, scores, lifted_base, ahead, own_part = shared_part(
        mixer_input, state_input, halo, taps, scale, last, running, keys, inner
    )
    arrived = [own_part] + arrived
    mix = functools.partial(
        mix_part,
        table=table,
        kinds=stretch_kind,
        inner=inner,
        running=running,
        step=step,
        scores=scores,
        ahead=ahead,
    )
    row_state = fold_row(arrived)
    row_before = sent(row_state, lambda z, x: (z ^ 1, x))
    row_before, mixed_first = lax.optimization_barrier((row_before, mix(0, PAIR)))
    pair_state = fold_two(1, row_state, row_before)
    near = fold_near(arrived, row_before)
    pair_before = sent(pair_state, lambda z, x: (z ^ 2, x))
    near = [near[0]] + [along_x(near[k], k) for k in range(1, XS)]
    quad_state = fold_two(2, pair_state, pair_before)
    turn = functools.partial(
        turn_part,
        PAIR,
        2 * PAIR,
        table=table,
        kinds=stretch_kind,
        inner=inner,
        running=running,
        scores=scores,
        ahead=ahead,
        gate=gate_input,
    )
    quad_state, step_late = lax.optimization_barrier((quad_state, step))
    quad_state, *turned = lax.optimization_barrier(
        (quad_state, *turn(False, (), step=step_late))
    )
    quad_before = sent(quad_state, lambda z, x: (ZS - 1 - z, x) if z < ZS // 2 else None)
    quad_before, mixed_second, gates = lax.optimization_barrier(
        (quad_before, *turn(True, turned, step=step_late))
    )
    far = fold_far(arrived, (row_before, pair_before, quad_before))
    far = [far[0]] + [along_x(far[k], k) for k in range(1, XS)]
    local_out, lifted = local_part(
        table,
        stretch_kind,
        inner,
        running,
        step,
        scores,
        ahead,
        lifted_base,
        (mixed_first, mixed_second),
        near,
    )
    gated, squares = far_part(local_out, gates, lifted, far)
    squares = squares + lax.ppermute(squares, "head", head_perm(lambda y, core: (y, 1 - core)))
    sums = [squares] + [
        lax.ppermute(squares, "head", head_perm(lambda y, core, k=k: ((y + k) % YS, core)))
        for k in (2, 1, 3)
    ]
    total_width = width * lax.axis_size("head")
    return norm(gated, sums, norm_gain[None, :], total_width)


def solution(mesh):
    return jax.shard_map(
        local,
        mesh=mesh,
        in_specs=(
            P("seq", "head"),
            P("seq", None),
            P("seq", "head"),
            P("seq", "head"),
            P("head"),
            P(None, "head"),
            P(),
            P(None, None, "head"),
            P("seq"),
            P("head"),
        ),
        out_specs=P("seq", "head"),
        check_vma=False,
    )
```
